32 devices in a mesh: ctx: 16 (over z, y, x), tp: 2 (over core).
Axes of the slice: x: 2, y: 2, z: 4, core: 2. Of those that a mesh axis runs over, the one named last changes fastest.
Arguments:
- queries: bfloat16 [4096, 4096], P('ctx', 'tp'), may hold values from -6 to 6
- keys: bfloat16 [4096, 2048], P('ctx', 'tp'), may hold values from -6 to 6
- values: bfloat16 [4096, 2048], P('ctx', 'tp'), may hold values from -6 to 6
- out_weight: bfloat16 [4096, 2688], P('tp'), may hold values from -0.09375 to 0.09375
- out_grad: bfloat16 [4096, 2688], P('ctx'), may hold values from -6 to 6
- block_doc: int32 [16], replicated, may hold values from 0 to 3, never falling along the last dimension, each value on 1 to 8 neighbouring positions
Outputs:
- attn_output: bfloat16 [4096, 2688], P('ctx', 'tp')
- query_grad: bfloat16 [4096, 4096], P('ctx', 'tp')
- key_grad: bfloat16 [4096, 2048], P('ctx', 'tp')
- value_grad: bfloat16 [4096, 2048], P('ctx', 'tp')
- out_weight_grad: float32 [4096, 2688], P('tp', 'ctx')
The draws below stay inside these ranges and needn't reach their ends.
Inputs may be any that keep to these rules, and one draw needn't show every extreme that they name: block_doc never falls; each document covers 1 to 8 whole blocks, one exactly 8.
All inputs are finite; a program needn't handle non-finite values.
Results may differ from the reference program's by a relative error of at most 0.017.
Values may be sent and summed in bfloat16 or wider, within the bound.
No kernel may reach another device: no remote copies, remote signals or barrier semaphores. Data moves between devices by JAX's collectives and lax.ppermute only.
A program may use at most 128 MiB of HBM per device.

```python
import math
import jax
import jax.numpy as jnp
import numpy as np
from jax import lax

Q_HEADS = 32
KV_HEADS = 16
HEAD = 128
WINDOW = 1024
D_OUT = 2688
TOK_DEV = 256
TOKENS = 4096
DOCS = 4
DOC_MOST = 8
N_CTX = 16


def base_field(key, width):
    field = jnp.clip(jax.random.normal(jax.random.fold_in(key, 5), (TOKENS, width)), -6.0, 6.0)
    return field.astype(jnp.float32)


def draw_queries(key, part):
    field = base_field(jax.random.fold_in(key, 21), Q_HEADS * HEAD)
    return field.astype(jnp.bfloat16)


def draw_keys(key, part):
    field = base_field(jax.random.fold_in(key, 22), KV_HEADS * HEAD)
    return field.astype(jnp.bfloat16)


def with_spikes(drawn, own_key, source, target, blocks, factor):
    owner, partner = [(jnp.arange(drawn.shape[axis_at]) // (drawn.shape[axis_at] // blocks)).reshape([-1 if axis == axis_at else 1 for axis in range(drawn.ndim)]) for axis_at in (source, target)]
    chosen = jax.random.permutation(own_key, blocks)[partner]
    strong = (owner == chosen) | (owner == (partner + blocks // 2) % blocks)
    return jnp.where(strong, factor * drawn, drawn)


def levels(stream_key, dims, split, low, high):
    factor_of, own = 1.0, jax.random.fold_in(stream_key, 6)
    for dim, shards_of in split:
        draws = jnp.exp(jax.random.uniform(jax.random.fold_in(own, dim), (shards_of,), jnp.float32, low / len(split), high / len(split)))
        factor_of = factor_of * jnp.repeat(draws, dims[dim] // shards_of).reshape([-1 if axis == dim else 1 for axis in range(len(dims))])
    return factor_of


def length_profile(count, total, most, slope):
    weights = [(1 << 20) // math.isqrt(standing ** slope) + 1 for standing in range(2, count + 1)]
    spare, counts = total - most - (count - 1), [1] * (count - 1)
    while spare > 0:
        movable = [i for i in range(count - 1) if counts[i] < most]
        mass, remaining = sum([weights[i] for i in movable]), spare
        for i in movable:
            addition = min(most - counts[i], max(1, remaining * weights[i] // mass), spare)
            counts[i] = counts[i] + addition
            spare = spare - addition
    return np.array([most] + counts)


def ragged(key, number_of, total, most, slope):
    if number_of == 2:
        one = jax.random.randint(key, (), max(1, total - most), min(most, total - 1) + 1)
        return jnp.stack([one, total - one])
    sizes = jnp.asarray(length_profile(number_of, total, most, slope), jnp.int32)
    pairs = (number_of - 1) // 2
    source_of, taker = sizes[1:1 + 2 * pairs:2], sizes[2:2 + 2 * pairs:2]
    slack = jnp.minimum(source_of - 1, most - taker)
    passed = jax.random.randint(jax.random.fold_in(key, 1), (pairs,), 0, 1 << 20) % (slack + 1)
    sizes = sizes.at[1:1 + 2 * pairs:2].set(source_of - passed).at[2:2 + 2 * pairs:2].set(taker + passed)
    return sizes[jax.random.permutation(jax.random.fold_in(key, 2), number_of)]


def normal_values(own_key, extent, scale, bound, split=(), held_as=jnp.bfloat16):
    array = jax.random.normal(own_key, extent, jnp.float32) * scale
    if len(split) > 0:
        array = levels(own_key, extent, split, -0.22, 0.18) * array
    return jnp.clip(array, min=-bound, max=bound).astype(held_as)


def heavy_noise(rng, dims, scale, limit, pieces, heavy, held_as=jnp.bfloat16):
    result = scale * jax.random.normal(rng, dims, jnp.float32)
    if pieces:
        result = result * levels(rng, dims, pieces, -0.22, 0.18)
    return jnp.clip(with_spikes(result, jax.random.fold_in(rng, 3), *heavy), -limit, limit).astype(held_as)


def setup_inputs(seed: int = 0) -> dict:
    arg_keys = jax.random.split(jax.random.key(seed), 7)
    return {
        "queries": draw_queries(jax.random.fold_in(arg_keys[6], 71), 0),
        "keys": draw_keys(jax.random.fold_in(arg_keys[6], 71), 0),
        "values": normal_values(arg_keys[2], (TOKENS, KV_HEADS * HEAD), 1.0, 6.0, ((0, 16), (1, 2))),
        "out_weight": normal_values(arg_keys[3], (Q_HEADS * HEAD, D_OUT), (Q_HEADS * HEAD) ** -0.5, 0.09375, ((0, 2),)),
        "out_grad": heavy_noise(arg_keys[4], (TOKENS, D_OUT), 1.0, 6.0, ((0, 16),), (0, 1, 16, 2.0)),
        "block_doc": jnp.searchsorted(jnp.cumsum(ragged(arg_keys[5], DOCS, N_CTX, DOC_MOST, 2)), jnp.arange(N_CTX), side="right").astype(jnp.int32),
    }


query_scale = 168.0 ** -0.5


def reference(queries, keys, values, out_weight, out_grad, block_doc):
    span_blocks = WINDOW // TOK_DEV
    group_size = Q_HEADS // KV_HEADS
    window_rows = (span_blocks + 1) * TOK_DEV
    lead_rows = span_blocks * TOK_DEV
    key_width = KV_HEADS * HEAD
    key_padded = jnp.concatenate([jnp.zeros((lead_rows, key_width), jnp.bfloat16), keys], axis=0)
    value_padded = jnp.concatenate([jnp.zeros((lead_rows, key_width), jnp.bfloat16), values], axis=0)
    doc_padded = jnp.concatenate([jnp.full((span_blocks,), -1, jnp.int32), block_doc.astype(jnp.int32)])
    rel_key = jnp.arange(window_rows, dtype=jnp.int32)
    rel_query = jnp.arange(TOK_DEV, dtype=jnp.int32) + lead_rows
    near = (rel_key[None, :] <= rel_query[:, None]) & (rel_key[None, :] > rel_query[:, None] - WINDOW)

    def per_block(carry, block):
        key_acc, value_acc = carry
        start = (block * TOK_DEV).astype(jnp.int32)
        zero_index = jnp.zeros((), jnp.int32)
        query_block = lax.dynamic_slice_in_dim(queries, start, TOK_DEV, 0).astype(jnp.float32)
        query_block = query_block.reshape(TOK_DEV, KV_HEADS, group_size, HEAD)
        key_block = lax.dynamic_slice_in_dim(key_padded, start, window_rows, 0).astype(jnp.float32)
        key_block = key_block.reshape(window_rows, KV_HEADS, HEAD)
        value_block = lax.dynamic_slice_in_dim(value_padded, start, window_rows, 0).astype(jnp.float32)
        value_block = value_block.reshape(window_rows, KV_HEADS, HEAD)
        window_docs = lax.dynamic_slice_in_dim(doc_padded, block.astype(jnp.int32), span_blocks + 1, 0)
        key_docs = jnp.repeat(window_docs, TOK_DEV)
        own_doc = lax.dynamic_slice_in_dim(block_doc.astype(jnp.int32), block.astype(jnp.int32), 1, 0)
        visible = near & (key_docs[None, :] == own_doc[0])
        scores = jnp.einsum('tkgd,skd->kgts', query_block, key_block) * query_scale
        scores = jnp.where(visible[None, None], scores, -jnp.inf)
        top = jnp.max(scores, axis=-1, keepdims=True)
        expo = jnp.exp(scores - top)
        probs = expo / jnp.sum(expo, axis=-1, keepdims=True)
        probs_low = probs.astype(jnp.bfloat16).astype(jnp.float32)
        attn = jnp.einsum('kgts,skd->tkgd', probs_low, value_block).astype(jnp.bfloat16)
        grad_rows = lax.dynamic_slice_in_dim(out_grad, start, TOK_DEV, 0)
        d_attn = jnp.dot(grad_rows, out_weight.T, preferred_element_type=jnp.float32).astype(jnp.bfloat16)
        d_attn_h = d_attn.astype(jnp.float32).reshape(TOK_DEV, KV_HEADS, group_size, HEAD)
        d_probs = jnp.einsum('tkgd,skd->kgts', d_attn_h, value_block)
        delta = jnp.einsum('tkgd,tkgd->kgt', attn.astype(jnp.float32), d_attn_h)
        d_scores = (probs * (d_probs - delta[..., None])).astype(jnp.bfloat16).astype(jnp.float32)
        query_grad = (jnp.einsum('kgts,skd->tkgd', d_scores, key_block) * query_scale).astype(jnp.bfloat16)
        key_part = jnp.einsum('kgts,tkgd->skd', d_scores, query_block) * query_scale
        value_part = jnp.einsum('kgts,tkgd->skd', probs_low, d_attn_h)
        key_acc = lax.dynamic_update_slice(key_acc, lax.dynamic_slice_in_dim(key_acc, start, window_rows, 0) + key_part.reshape(window_rows, key_width), (start, zero_index))
        value_acc = lax.dynamic_update_slice(value_acc, lax.dynamic_slice_in_dim(value_acc, start, window_rows, 0) + value_part.reshape(window_rows, key_width), (start, zero_index))
        return (key_acc, value_acc), (attn.reshape(TOK_DEV, Q_HEADS * HEAD), query_grad.reshape(TOK_DEV, Q_HEADS * HEAD))

    initial = (jnp.zeros((TOKENS + lead_rows, key_width), jnp.float32), jnp.zeros((TOKENS + lead_rows, key_width), jnp.float32))
    (key_acc, value_acc), (attn_blocks, qgrad_blocks) = lax.scan(per_block, initial, jnp.arange(TOKENS // TOK_DEV, dtype=jnp.int32))
    attn_all = attn_blocks.reshape(TOKENS, Q_HEADS * HEAD)
    attn_output = jnp.dot(attn_all, out_weight, preferred_element_type=jnp.float32).astype(jnp.bfloat16)
    out_weight_grad = jnp.dot(attn_all.T, out_grad, preferred_element_type=jnp.float32)
    query_grad = qgrad_blocks.reshape(TOKENS, Q_HEADS * HEAD)
    key_grad = key_acc[lead_rows:].astype(jnp.bfloat16)
    value_grad = value_acc[lead_rows:].astype(jnp.bfloat16)
    return (attn_output, query_grad, key_grad, value_grad, out_weight_grad)
```

```python
import functools

import jax
import jax.numpy as jnp
from jax import lax
from jax.experimental import pallas as pl
from jax.experimental.pallas import tpu as pltpu
from jax.sharding import PartitionSpec as P

HEAD = 128
WINDOW = 1024
GROUP = 4


query_scale = 168.0 ** (-0.5)
LOG2E = 1.4426950408889634
HIDDEN = -1e30


def shifted(shard, axis, by):
    size = lax.axis_size(axis)
    pairs = [(i, i + by) for i in range(size) if 0 <= i + by < size]
    return lax.ppermute(shard, axis, pairs)


def swapped(shard, axis, by):
    return lax.ppermute(shard, axis, [(i, i ^ by) for i in range(lax.axis_size(axis))])


def attention_kernel(rows, info, *refs):
    q_refs, g_refs = refs[:GROUP], refs[GROUP : 2 * GROUP]
    k_own, v_own, k_far, v_far = refs[2 * GROUP : 2 * GROUP + 4]
    outs = refs[2 * GROUP + 4 :]
    back_refs = outs[:GROUP]
    attn_cat, kv_own, kv_far = outs[GROUP : GROUP + 3]
    q_all, g_all, k_all, v_all, k_tr, v_tr, k_acc, v_acc, back = outs[GROUP + 3 :]
    r, tp = info[0], info[1]
    heads = q_refs[0].shape[1] // HEAD
    half = rows // 2
    for m in range(GROUP):
        q_all[m] = q_refs[m][...]
        g_all[m] = g_refs[m][...]
        spot = r ^ m
        for place, k, v in ((spot, k_far, v_far), (spot + GROUP, k_own, v_own)):
            k_all[place] = k[m]
            v_all[place] = v[m]
            k_tr[place] = k[m].T
            v_tr[place] = v[m].T
    k_acc[...] = jnp.zeros_like(k_acc)
    v_acc[...] = jnp.zeros_like(v_acc)
    key_at = lax.broadcasted_iota(jnp.int32, (rows, rows), 0)
    query_at = lax.broadcasted_iota(jnp.int32, (rows, rows), 1)
    nt = (((1,), (1,)), ((), ()))

    def dot(a, b):
        return jnp.dot(a, b, preferred_element_type=jnp.float32)

    def block(m, carry):
        first = r ^ m
        own_doc = info[2 + first + GROUP]
        for h in range(heads):
            cols = slice(h * HEAD, (h + 1) * HEAD)
            q = q_all[m, :, cols]
            g = g_all[m, :, cols]
            scores = []
            for j in range(GROUP + 1):
                s = lax.dot_general(k_all[first + j], q, nt, preferred_element_type=jnp.float32)
                if j == 0:
                    s = jnp.where(key_at > query_at, s, HIDDEN)
                if j == GROUP:
                    s = jnp.where(key_at <= query_at, s, HIDDEN)
                else:
                    s = s + jnp.where(info[2 + first + j] == own_doc, 0.0, HIDDEN)
                scores.append(s)
            top = functools.reduce(jnp.maximum, [jnp.max(s, axis=0, keepdims=True) for s in scores])
            top = top * (query_scale * LOG2E)
            expo = [jnp.exp2(s * (query_scale * LOG2E) - top) for s in scores]
            whole = functools.reduce(jnp.add, [jnp.sum(e, axis=0, keepdims=True) for e in expo])
            inverse = 1.0 / whole
            probs = [e * inverse for e in expo]
            low = [p.astype(jnp.bfloat16) for p in probs]
            attn_tr = functools.reduce(
                jnp.add, [dot(v_tr[first + j], low[j]) for j in range(GROUP + 1)]
            )
            attn_tr = attn_tr.astype(jnp.bfloat16).astype(jnp.float32)
            g_tr = g.astype(jnp.float32).T
            delta = jnp.sum(attn_tr * g_tr, axis=0, keepdims=True)
            dq_tr = None
            for j in range(GROUP + 1):
                d_p = lax.dot_general(v_all[first + j], g, nt, preferred_element_type=jnp.float32)
                d_s = (probs[j] * (d_p - delta)).astype(jnp.bfloat16)
                term = dot(k_tr[first + j], d_s)
                dq_tr = term if dq_tr is None else dq_tr + term
                k_acc[first + j] += dot(d_s, q)
                v_acc[first + j] += dot(low[j], g)
            back[m, 0, :, cols] = attn_tr.T.astype(jnp.bfloat16)
            back[m, 1, :, cols] = (dq_tr * query_scale).T.astype(jnp.bfloat16)
        return carry

    lax.fori_loop(0, GROUP, block, 0)
    for m in range(GROUP):
        back_refs[m][...] = back[m]
        spot = r ^ m
        kv_far[0, m] = (k_acc[spot] * query_scale).astype(kv_far.dtype)
        kv_far[1, m] = v_acc[spot].astype(kv_far.dtype)
        kv_own[0, m] = k_acc[spot + GROUP] * query_scale
        kv_own[1, m] = v_acc[spot + GROUP]
    attn_cat[0:rows] = back[0, 0]
    near = pl.multiple_of(tp * half, half)
    away = pl.multiple_of((1 - tp) * half, half)
    for m in range(1, GROUP):
        at = rows + (m - 1) * half
        attn_cat[at : at + half] = back[m, 0, pl.ds(near, half), :]
        at += (GROUP - 1) * half
        attn_cat[at : at + half] = back[m, 0, pl.ds(away, half), :]


def attention(info, queries, d_attn, kv_own, kv_far):
    rows, q_width = queries[0].shape
    kv_heads = kv_own.shape[2] // HEAD // 2
    q_block = q_width // kv_heads
    q_spec = pl.BlockSpec((rows, q_block), lambda g: (0, g))
    k_spec = pl.BlockSpec((GROUP, rows, HEAD), lambda g: (0, 0, g))
    v_spec = pl.BlockSpec((GROUP, rows, HEAD), lambda g: (0, 0, g + kv_heads))
    back_spec = pl.BlockSpec((2, rows, q_block), lambda g: (0, 0, g))
    kv_spec = pl.BlockSpec((2, GROUP, rows, HEAD), lambda g: (0, 0, 0, g))
    kv_shape = (2, GROUP, rows, kv_heads * HEAD)
    bf16 = jnp.bfloat16
    blocks = 2 * GROUP
    return pl.pallas_call(
        functools.partial(attention_kernel, rows),
        grid=(kv_heads,),
        in_specs=[pl.BlockSpec(memory_space=pltpu.SMEM)]
        + [q_spec] * (2 * GROUP)
        + [k_spec, v_spec, k_spec, v_spec],
        out_specs=[back_spec] * GROUP
        + [pl.BlockSpec((GROUP * rows, q_block), lambda g: (0, g)), kv_spec, kv_spec],
        out_shape=[jax.ShapeDtypeStruct((2, rows, q_width), bf16)] * GROUP
        + [
            jax.ShapeDtypeStruct((GROUP * rows, q_width), bf16),
            jax.ShapeDtypeStruct(kv_shape, jnp.float32),
            jax.ShapeDtypeStruct(kv_shape, bf16),
        ],
        scratch_shapes=[
            pltpu.VMEM((GROUP, rows, q_block), bf16),
            pltpu.VMEM((GROUP, rows, q_block), bf16),
            pltpu.VMEM((blocks, rows, HEAD), bf16),
            pltpu.VMEM((blocks, rows, HEAD), bf16),
            pltpu.VMEM((blocks, HEAD, rows), bf16),
            pltpu.VMEM((blocks, HEAD, rows), bf16),
            pltpu.VMEM((blocks, rows, HEAD), jnp.float32),
            pltpu.VMEM((blocks, rows, HEAD), jnp.float32),
            pltpu.VMEM((GROUP, 2, rows, q_block), bf16),
        ],
        compiler_params=pltpu.CompilerParams(vmem_limit_bytes=40 * 1024 * 1024),
        cost_estimate=pl.CostEstimate(
            flops=12 * q_width * GROUP * rows * (GROUP + 1) * rows,
            bytes_accessed=10 * 1024 * 1024,
            transcendentals=0,
        ),
    )(info, *queries, *d_attn, kv_own, kv_own, kv_far, kv_far)


def grouped(queries, keys, values, out_weight, out_grad, block_doc):
    f32, bf16 = jnp.float32, jnp.bfloat16
    rows = queries.shape[0]
    me, tp = lax.axis_index("ctx"), lax.axis_index("tp")
    r, layer = me % GROUP, me // GROUP
    members = range(GROUP)
    q_width, kv_width = queries.shape[1] // GROUP, keys.shape[1] // GROUP
    d_out = out_grad.shape[1]

    def part(array, m, width, dim):
        return lax.dynamic_slice_in_dim(array, (r ^ m) * width, width, dim)

    def traded(blocks):
        return [blocks[0]] + [swapped(blocks[m], "ctx", m) for m in members[1:]]

    def in_order(blocks, dim):
        width = blocks[0].shape[dim]
        shape = list(blocks[0].shape)
        shape[dim] = width * GROUP
        whole = jnp.zeros(shape, blocks[0].dtype)
        for m in members:
            whole = lax.dynamic_update_slice_in_dim(whole, blocks[m], (r ^ m) * width, dim)
        return whole

    kv = traded(
        [
            jnp.concatenate([part(keys, m, kv_width, 1), part(values, m, kv_width, 1)], axis=1)
            for m in members
        ]
    )
    kv_own = jnp.stack(kv)
    kv_far = shifted(kv_own, "ctx", GROUP)
    q = traded([part(queries, m, q_width, 1) for m in members])
    d_attn = traded(
        [
            jnp.einsum(
                "te,re->tr", out_grad, part(out_weight, m, q_width, 0), preferred_element_type=f32
            ).astype(bf16)
            for m in members
        ]
    )
    half = lax.dynamic_slice_in_dim(out_grad, tp * (rows // 2), rows // 2, 0)
    near = jnp.concatenate([swapped(half, "ctx", m) for m in members[1:]], axis=0)
    away = swapped(near, "tp", 1)
    grad_cat = jnp.concatenate([out_grad, near, away], axis=0)

    doc_padded = jnp.concatenate([jnp.full((GROUP,), -1, jnp.int32), block_doc])
    docs = lax.dynamic_slice_in_dim(doc_padded, layer * GROUP, 2 * GROUP, 0)
    info = jnp.concatenate([jnp.stack([r, tp]).astype(jnp.int32), docs])
    *back, attn_cat, own_grad, far_grad = attention(info, q, d_attn, kv_own, kv_far)

    weight_terms = jnp.einsum("te,th->eh", grad_cat, attn_cat, preferred_element_type=f32)
    layers = lax.axis_size("ctx") // GROUP
    columns = [[i * GROUP + j for i in range(layers)] for j in members]
    weight_sums = lax.psum_scatter(
        weight_terms.astype(bf16),
        "ctx",
        scatter_dimension=0,
        axis_index_groups=columns,
        tiled=True,
    )
    cut = weight_sums.shape[0] // GROUP
    weight_blocks = traded([part(weight_sums, m, cut, 0) for m in members])
    out_weight_grad = in_order([b.astype(f32) for b in weight_blocks], 1).T

    back = in_order(traded(back), 2)
    attn, query_grad = back[0], back[1]
    terms = jnp.einsum("re,tr->et", out_weight, attn, preferred_element_type=f32)
    mine = lax.dynamic_slice_in_dim(terms, tp * (d_out // 2), d_out // 2, 0)
    theirs = lax.dynamic_slice_in_dim(terms, (1 - tp) * (d_out // 2), d_out // 2, 0)
    attn_output = (mine + swapped(theirs.astype(bf16), "tp", 1).astype(f32)).astype(bf16).T

    total = (own_grad + shifted(far_grad, "ctx", -GROUP).astype(f32)).astype(bf16)
    total = in_order(traded([total[:, m] for m in members]), 2)
    return (attn_output, query_grad, total[0], total[1], out_weight_grad)


def single(queries, keys, values, out_weight, out_grad, block_doc):
    tok_rows = queries.shape[0]
    head_size = HEAD
    kv_count = keys.shape[1] // head_size
    group_size = queries.shape[1] // keys.shape[1]
    key_width = keys.shape[1]
    span_blocks = WINDOW // tok_rows
    reach_blocks = min(span_blocks, lax.axis_size("ctx") - 1)
    own_block = lax.axis_index("ctx")
    paired = jnp.stack([keys, values])
    by_distance = jnp.stack(
        [paired] + [shifted(paired, "ctx", distance) for distance in range(1, reach_blocks + 1)]
    )
    ordered = by_distance[::-1]
    missing = span_blocks - reach_blocks
    window_rows = (span_blocks + 1) * tok_rows
    key_window = ordered[:, 0].reshape(window_rows, kv_count, head_size)
    value_window = ordered[:, 1].reshape(window_rows, kv_count, head_size)
    doc_padded = jnp.concatenate([jnp.full((span_blocks,), -1, jnp.int32), block_doc])
    window_docs = lax.dynamic_slice_in_dim(doc_padded, own_block, span_blocks + 1, 0)
    key_docs = jnp.repeat(window_docs, tok_rows)
    own_doc = lax.dynamic_slice_in_dim(block_doc, own_block, 1, 0)
    rel_key = jnp.arange(window_rows, dtype=jnp.int32)
    rel_query = jnp.arange(tok_rows, dtype=jnp.int32) + span_blocks * tok_rows
    visible = (rel_key[None, :] <= rel_query[:, None]) & (
        rel_key[None, :] > rel_query[:, None] - WINDOW
    )
    visible = visible & (key_docs[None, :] == own_doc[0])
    query_heads = queries.reshape(tok_rows, kv_count, group_size, head_size)
    scores = (
        jnp.einsum("tkgd,skd->kgts", query_heads, key_window, preferred_element_type=jnp.float32)
        * query_scale
    )
    scores = jnp.where(visible[None, None], scores, -jnp.inf)
    top = jnp.max(scores, axis=-1, keepdims=True)
    expo = jnp.exp(scores - top)
    probs = expo / jnp.sum(expo, axis=-1, keepdims=True)
    probs_low = probs.astype(jnp.bfloat16)
    attn_heads = jnp.einsum(
        "kgts,skd->tkgd", probs_low, value_window, preferred_element_type=jnp.float32
    ).astype(jnp.bfloat16)
    attn = attn_heads.reshape(tok_rows, queries.shape[1])
    output_terms = jnp.dot(attn, out_weight, preferred_element_type=jnp.float32)
    attn_output = lax.psum_scatter(output_terms, "tp", scatter_dimension=1, tiled=True).astype(
        jnp.bfloat16
    )
    weight_terms = jnp.einsum("tr,tc->rc", attn, out_grad, preferred_element_type=jnp.float32)
    out_weight_grad = lax.psum_scatter(weight_terms, "ctx", scatter_dimension=1, tiled=True)
    d_attn = jnp.einsum(
        "te,re->tr", out_grad, out_weight, preferred_element_type=jnp.float32
    ).astype(jnp.bfloat16)
    d_attn_heads = d_attn.reshape(tok_rows, kv_count, group_size, head_size)
    d_probs = jnp.einsum(
        "tkgd,skd->kgts", d_attn_heads, value_window, preferred_element_type=jnp.float32
    )
    delta = jnp.einsum(
        "tkgd,tkgd->kgt", attn_heads, d_attn_heads, preferred_element_type=jnp.float32
    )
    d_scores = (probs * (d_probs - delta[..., None])).astype(jnp.bfloat16)
    query_grad = (
        jnp.einsum("kgts,skd->tkgd", d_scores, key_window, preferred_element_type=jnp.float32)
        * query_scale
    ).astype(jnp.bfloat16)
    query_grad = query_grad.reshape(tok_rows, queries.shape[1])
    key_part = (
        jnp.einsum("kgts,tkgd->skd", d_scores, query_heads, preferred_element_type=jnp.float32)
        * query_scale
    )
    value_part = jnp.einsum(
        "kgts,tkgd->skd", probs_low, d_attn_heads, preferred_element_type=jnp.float32
    )
    by_position = jnp.stack(
        [
            key_part.reshape(span_blocks + 1, tok_rows, key_width),
            value_part.reshape(span_blocks + 1, tok_rows, key_width),
        ],
        axis=1,
    )
    terms_near = by_position[::-1]
    total = terms_near[0] + sum(
        [shifted(terms_near[distance], "ctx", -distance) for distance in range(1, reach_blocks + 1)]
    )
    key_grad = total[0].astype(jnp.bfloat16)
    value_grad = total[1].astype(jnp.bfloat16)
    return (attn_output, query_grad, key_grad, value_grad, out_weight_grad)


def local(queries, keys, values, out_weight, out_grad, block_doc):
    fits = (
        lax.axis_size("ctx") % GROUP == 0
        and queries.shape[0] * GROUP == WINDOW
        and keys.shape[1] % (GROUP * HEAD) == 0
        and lax.axis_size("tp") == 2
    )
    step = grouped if fits else single
    return step(queries, keys, values, out_weight, out_grad, block_doc)


def solution(mesh):
    placed = (P("ctx", "tp"), P("ctx", "tp"), P("ctx", "tp"), P("tp", None), P("ctx", None), P())
    return jax.shard_map(
        local,
        mesh=mesh,
        in_specs=placed,
        out_specs=(P("ctx", "tp"), P("ctx", "tp"), P("ctx", "tp"), P("ctx", "tp"), P("tp", "ctx")),
        check_vma=False,
    )
```

```python
import functools

import jax
import jax.numpy as jnp
from jax import lax
from jax.experimental import pallas as pl
from jax.experimental.pallas import tpu as pltpu
from jax.sharding import PartitionSpec as P

HEAD = 128
WINDOW = 1024
GROUP = 4


query_scale = 168.0 ** (-0.5)
LOG2E = 1.4426950408889634
HIDDEN = -1e30


def shifted(shard, axis, by):
    size = lax.axis_size(axis)
    pairs = [(i, i + by) for i in range(size) if 0 <= i + by < size]
    return lax.ppermute(shard, axis, pairs)


def swapped(shard, axis, by):
    return lax.ppermute(shard, axis, [(i, i ^ by) for i in range(lax.axis_size(axis))])


SMEM = pl.BlockSpec(memory_space=pltpu.SMEM)
ANY = pl.BlockSpec(memory_space=pl.ANY)


def attention_kernel(rows, skip, info, *refs):
    q_refs = refs[:GROUP]
    k_own, v_own, k_far, v_far = refs[GROUP : GROUP + 4]
    outs = refs[GROUP + 4 + skip :]
    back_refs = outs[:GROUP]
    attn_cat, kv_own, kv_far = outs[GROUP : GROUP + 3]
    q_all, g_all, k_all, v_all, k_tr, v_tr, k_acc, v_acc, back = outs[GROUP + 3 :]
    r, tp = info[0], info[1]
    width = q_refs[0].shape[1] // 2
    heads = width // HEAD
    half = rows // 2
    for m in range(GROUP):
        q_all[m] = q_refs[m][:, :width]
        g_all[m] = q_refs[m][:, width:]
        spot = r ^ m
        for place, k, v in ((spot, k_far, v_far), (spot + GROUP, k_own, v_own)):
            k_all[place] = k[m]
            v_all[place] = v[m]
            k_tr[place] = k[m].T
            v_tr[place] = v[m].T
    k_acc[...] = jnp.zeros_like(k_acc)
    v_acc[...] = jnp.zeros_like(v_acc)
    key_at = lax.broadcasted_iota(jnp.int32, (rows, rows), 0)
    query_at = lax.broadcasted_iota(jnp.int32, (rows, rows), 1)
    nt = (((1,), (1,)), ((), ()))

    def dot(a, b):
        return jnp.dot(a, b, preferred_element_type=jnp.float32)

    def block(m, carry):
        first = r ^ m
        own_doc = info[3 + first + GROUP]
        for h in range(heads):
            cols = slice(h * HEAD, (h + 1) * HEAD)
            q = q_all[m, :, cols]
            g = g_all[m, :, cols]
            scores = []
            for j in range(GROUP + 1):
                s = lax.dot_general(k_all[first + j], q, nt, preferred_element_type=jnp.float32)
                if j == 0:
                    s = jnp.where(key_at > query_at, s, HIDDEN)
                if j == GROUP:
                    s = jnp.where(key_at <= query_at, s, HIDDEN)
                else:
                    s = s + jnp.where(info[3 + first + j] == own_doc, 0.0, HIDDEN)
                scores.append(s)
            top = functools.reduce(jnp.maximum, [jnp.max(s, axis=0, keepdims=True) for s in scores])
            top = top * (query_scale * LOG2E)
            expo = [jnp.exp2(s * (query_scale * LOG2E) - top) for s in scores]
            whole = functools.reduce(jnp.add, [jnp.sum(e, axis=0, keepdims=True) for e in expo])
            inverse = 1.0 / whole
            probs = [e * inverse for e in expo]
            low = [p.astype(jnp.bfloat16) for p in probs]
            attn_tr = functools.reduce(
                jnp.add, [dot(v_tr[first + j], low[j]) for j in range(GROUP + 1)]
            )
            attn_tr = attn_tr.astype(jnp.bfloat16).astype(jnp.float32)
            g_tr = g.astype(jnp.float32).T
            delta = jnp.sum(attn_tr * g_tr, axis=0, keepdims=True)
            dq_tr = None
            for j in range(GROUP + 1):
                d_p = lax.dot_general(v_all[first + j], g, nt, preferred_element_type=jnp.float32)
                d_s = (probs[j] * (d_p - delta)).astype(jnp.bfloat16)
                term = dot(k_tr[first + j], d_s)
                dq_tr = term if dq_tr is None else dq_tr + term
                k_acc[first + j] += dot(d_s, q)
                v_acc[first + j] += dot(low[j], g)
            back[m, 0, :, cols] = attn_tr.T.astype(jnp.bfloat16)
            back[m, 1, :, cols] = (dq_tr * query_scale).T.astype(jnp.bfloat16)
        return carry

    lax.fori_loop(0, GROUP, block, 0)
    for m in range(GROUP):
        back_refs[m][...] = back[m]
        spot = r ^ m
        kv_far[0, m] = (k_acc[spot] * query_scale).astype(kv_far.dtype)
        kv_far[1, m] = v_acc[spot].astype(kv_far.dtype)
        kv_own[0, m] = k_acc[spot + GROUP] * query_scale
        kv_own[1, m] = v_acc[spot + GROUP]
    attn_cat[0:rows] = back[0, 0]
    near = pl.multiple_of(tp * half, half)
    away = pl.multiple_of((1 - tp) * half, half)
    for m in range(1, GROUP):
        at = rows + (m - 1) * half
        attn_cat[at : at + half] = back[m, 0, pl.ds(near, half), :]
        at += (GROUP - 1) * half
        attn_cat[at : at + half] = back[m, 0, pl.ds(away, half), :]


def entire(array):
    return pl.BlockSpec(array.shape, lambda i: (0,) * len(array.shape))


def attention(info, q_and_d, kv_own, kv_far, after=()):
    rows, q_block = q_and_d[0].shape[0], q_and_d[0].shape[1] // 2
    k_spec = pl.BlockSpec((GROUP, rows, HEAD), lambda i: (0, 0, 0))
    v_spec = pl.BlockSpec((GROUP, rows, HEAD), lambda i: (0, 0, 1))
    kv_shape = (2, GROUP, rows, HEAD)
    bf16 = jnp.bfloat16
    blocks = 2 * GROUP
    out = [jax.ShapeDtypeStruct((2, rows, q_block), bf16)] * GROUP + [
        jax.ShapeDtypeStruct((GROUP * rows, q_block), bf16),
        jax.ShapeDtypeStruct(kv_shape, jnp.float32),
        jax.ShapeDtypeStruct(kv_shape, bf16),
    ]
    return pl.pallas_call(
        functools.partial(attention_kernel, rows, len(after)),
        grid=(1,),
        in_specs=[SMEM]
        + [entire(a) for a in q_and_d]
        + [k_spec, v_spec, k_spec, v_spec]
        + [ANY] * len(after),
        out_specs=[entire(a) for a in out],
        out_shape=out,
        scratch_shapes=[
            pltpu.VMEM((GROUP, rows, q_block), bf16),
            pltpu.VMEM((GROUP, rows, q_block), bf16),
            pltpu.VMEM((blocks, rows, HEAD), bf16),
            pltpu.VMEM((blocks, rows, HEAD), bf16),
            pltpu.VMEM((blocks, HEAD, rows), bf16),
            pltpu.VMEM((blocks, HEAD, rows), bf16),
            pltpu.VMEM((blocks, rows, HEAD), jnp.float32),
            pltpu.VMEM((blocks, rows, HEAD), jnp.float32),
            pltpu.VMEM((GROUP, 2, rows, q_block), bf16),
        ],
        compiler_params=pltpu.CompilerParams(vmem_limit_bytes=32 * 1024 * 1024),
        cost_estimate=pl.CostEstimate(
            flops=12 * q_block * GROUP * rows * (GROUP + 1) * rows,
            bytes_accessed=5 * 1024 * 1024,
            transcendentals=0,
        ),
    )(info, *q_and_d, kv_own, kv_own, kv_far, kv_far, *after)


def moved(body, info, arrays, out, after=()):
    n = len(arrays)

    def kernel(info_ref, *refs):
        body(info_ref, refs[:n], refs[n + len(after) :])

    size = sum(a.size * a.dtype.itemsize for a in list(arrays) + list(out))
    return pl.pallas_call(
        kernel,
        grid=(1,),
        in_specs=[SMEM] + [entire(a) for a in arrays] + [ANY] * len(after),
        out_specs=[entire(a) for a in out],
        out_shape=list(out),
        compiler_params=pltpu.CompilerParams(vmem_limit_bytes=32 * 1024 * 1024),
        cost_estimate=pl.CostEstimate(flops=0, bytes_accessed=size, transcendentals=0),
    )(info, *arrays, *after)


def columns(ref, start, width):
    return ref[:, pl.ds(pl.multiple_of(start, HEAD), width)]


def project_back(info, out_grad, out_weight):
    rows, d_out = out_grad.shape
    per = 2
    steps = GROUP * per
    block = out_weight.shape[0] // steps

    def kernel(info_ref, grad, weight, *outs):
        step = pl.program_id(0)
        part = lax.dot_general(
            grad[...], weight[...], (((1,), (1,)), ((), ())), preferred_element_type=jnp.float32
        ).astype(jnp.bfloat16)
        for at in range(steps):

            @pl.when(step == at)
            def _():
                outs[at][...] = part

    def weight_block(step, info_ref):
        return ((info_ref[0] ^ (step % GROUP)) * per + step // GROUP, 0)

    outs = pl.pallas_call(
        kernel,
        grid_spec=pltpu.PrefetchScalarGridSpec(
            num_scalar_prefetch=1,
            grid=(steps,),
            in_specs=[
                pl.BlockSpec((rows, d_out), lambda i, info_ref: (0, 0)),
                pl.BlockSpec((block, d_out), weight_block),
            ],
            out_specs=[pl.BlockSpec((rows, block), lambda i, info_ref: (0, 0))] * steps,
        ),
        out_shape=[jax.ShapeDtypeStruct((rows, block), jnp.bfloat16)] * steps,
        compiler_params=pltpu.CompilerParams(vmem_limit_bytes=32 * 1024 * 1024),
        cost_estimate=pl.CostEstimate(
            flops=2 * rows * out_weight.size, bytes_accessed=2 * out_weight.size, transcendentals=0
        ),
    )(info, out_grad, out_weight)
    return [outs[g * GROUP : (g + 1) * GROUP] for g in range(per)]


def weight_terms(info, pieces, attn_cat):
    d_out, width = pieces[0].shape[1], attn_cat.shape[1]
    block = 3 * HEAD if d_out % (3 * HEAD) == 0 else d_out
    steps, cut = d_out // block, d_out // GROUP

    def kernel(info_ref, *refs):
        inputs, attn = refs[: len(pieces)], refs[len(pieces)]
        own, other, away, whole = refs[len(pieces) + 1 :]
        total, at = None, 0
        for piece in inputs:
            rows = piece.shape[0]
            term = lax.dot_general(
                piece[...],
                attn[at : at + rows],
                (((0,), (0,)), ((), ())),
                preferred_element_type=jnp.float32,
            )
            total, at = term if total is None else total + term, at + rows
        step = pl.program_id(0)
        whole[pl.ds(pl.multiple_of(step * block, block), block)] = total.astype(whole.dtype)

        @pl.when(step == steps - 1)
        def _():
            def chunk(m):
                return whole[pl.ds(pl.multiple_of((info_ref[2] ^ m) * cut, 16), cut)]

            own[...] = chunk(0)
            other[...] = chunk(2)
            away[0] = chunk(1)
            away[1] = chunk(3)

    shapes = [(cut, width), (cut, width), (2, cut, width)]
    out = [jax.ShapeDtypeStruct(s, jnp.bfloat16) for s in shapes]
    return pl.pallas_call(
        kernel,
        grid=(steps,),
        in_specs=[SMEM]
        + [pl.BlockSpec((p.shape[0], block), lambda i: (0, i)) for p in pieces]
        + [entire(attn_cat)],
        out_specs=[entire(a) for a in out],
        out_shape=out,
        scratch_shapes=[pltpu.VMEM((d_out, width), jnp.bfloat16)],
        compiler_params=pltpu.CompilerParams(vmem_limit_bytes=32 * 1024 * 1024),
        cost_estimate=pl.CostEstimate(
            flops=2 * attn_cat.size * d_out,
            bytes_accessed=2 * (attn_cat.shape[0] + width) * d_out,
            transcendentals=0,
        ),
    )(info, *pieces, attn_cat)


def split_sum(info, own, met):
    rows, width = own.shape
    cut = rows // GROUP

    def kernel(info_ref, own_ref, met_ref, *refs):
        outs, total = refs[:GROUP], refs[GROUP]
        total[...] = own_ref[...].astype(jnp.float32) + met_ref[...].astype(jnp.float32)
        for m in range(GROUP):
            start = pl.multiple_of((info_ref[0] ^ m) * cut, 8)
            outs[m][...] = total[pl.ds(start, cut)].astype(outs[m].dtype)

    out = [jax.ShapeDtypeStruct((cut, width), jnp.bfloat16)] * GROUP
    return pl.pallas_call(
        kernel,
        grid=(1,),
        in_specs=[SMEM, entire(own), entire(met)],
        out_specs=[entire(a) for a in out],
        out_shape=out,
        scratch_shapes=[pltpu.VMEM((rows, width), jnp.float32)],
        compiler_params=pltpu.CompilerParams(vmem_limit_bytes=32 * 1024 * 1024),
    )(info, own, met)


def project(info, attn, out_weight):
    rows, depth = attn.shape
    d_out = out_weight.shape[1]
    block = 3 * HEAD if d_out % (3 * HEAD) == 0 else d_out
    steps, half = d_out // block, d_out // 2

    def kernel(info_ref, attn_ref, weight, mine, theirs, whole):
        step = pl.program_id(0)
        part = jnp.dot(attn_ref[...], weight[...], preferred_element_type=jnp.float32)
        whole[pl.ds(pl.multiple_of(step * block, block), block)] = part.T

        @pl.when(step == steps - 1)
        def _():
            tp = info_ref[1]
            mine[...] = whole[pl.ds(pl.multiple_of(tp * half, 8), half)]
            other = whole[pl.ds(pl.multiple_of((1 - tp) * half, 8), half)]
            theirs[...] = other.astype(theirs.dtype)

    out = [jax.ShapeDtypeStruct((half, rows), d) for d in (jnp.float32, jnp.bfloat16)]
    return pl.pallas_call(
        kernel,
        grid=(steps,),
        in_specs=[SMEM, entire(attn), pl.BlockSpec((depth, block), lambda i: (0, i))],
        out_specs=[entire(a) for a in out],
        out_shape=out,
        scratch_shapes=[pltpu.VMEM((d_out, rows), jnp.float32)],
        compiler_params=pltpu.CompilerParams(vmem_limit_bytes=32 * 1024 * 1024),
        cost_estimate=pl.CostEstimate(
            flops=2 * attn.size * d_out, bytes_accessed=2 * out_weight.size, transcendentals=0
        ),
    )(info, attn, out_weight)


def grouped(queries, keys, values, out_weight, out_grad, block_doc):
    f32, bf16 = jnp.float32, jnp.bfloat16
    rows = queries.shape[0]
    me, tp = lax.axis_index("ctx"), lax.axis_index("tp")
    r, layer = me % GROUP, me // GROUP
    members = range(GROUP)
    q_width, kv_width = queries.shape[1] // GROUP, keys.shape[1] // GROUP
    kv_heads = kv_width // HEAD
    head_width = q_width // kv_heads
    d_out = out_grad.shape[1]
    doc_padded = jnp.concatenate([jnp.full((GROUP,), -1, jnp.int32), block_doc])
    docs = lax.dynamic_slice_in_dim(doc_padded, layer * GROUP, 2 * GROUP, 0)
    info = jnp.concatenate([jnp.stack([r, tp, layer]).astype(jnp.int32), docs])

    def shape(*dims, dtype=bf16):
        return jax.ShapeDtypeStruct(dims, dtype)

    def traded(blocks):
        return [blocks[0]] + [swapped(blocks[m], "ctx", m) for m in members[1:]]

    def pack_kv(info_ref, ins, outs):
        for m in members:
            start = (info_ref[0] ^ m) * kv_width
            for i in range(2):
                outs[m][:, i * kv_width : (i + 1) * kv_width] = columns(ins[i], start, kv_width)

    kv = traded(moved(pack_kv, info, [keys, values], [shape(rows, 2 * kv_width)] * GROUP))

    def pack_heads(info_ref, ins, outs):
        for m in members:
            for g in range(kv_heads):
                for i in range(2):
                    at = (i * kv_heads + g) * HEAD
                    outs[g][m, :, i * HEAD : (i + 1) * HEAD] = ins[m][:, at : at + HEAD]

    d_attn = project_back(info, out_grad, out_weight)
    heads_shape = [shape(GROUP, rows, 2 * HEAD)] * kv_heads
    kv_own = moved(pack_heads, info, kv, heads_shape, d_attn[0])
    kv_far = [shifted(a, "ctx", GROUP) for a in kv_own]

    def pack_queries(g, after):
        def body(info_ref, ins, outs):
            for m in members:
                start = (info_ref[0] ^ m) * q_width + g * head_width
                outs[m][:, :head_width] = columns(ins[0], start, head_width)
                outs[m][:, head_width:] = ins[1 + m][...]

        return traded(
            moved(body, info, [queries, *d_attn[g]], [shape(rows, 2 * head_width)] * GROUP, after)
        )

    def pack_half(info_ref, ins, outs):
        outs[0][...] = ins[0][pl.ds(pl.multiple_of(info_ref[1] * (rows // 2), 16), rows // 2), :]

    q_and_d = [pack_queries(0, kv[1:])]
    half = moved(pack_half, info, [out_grad], [shape(rows // 2, d_out)], [*q_and_d[0][1:], kv_far[0]])[0]
    near = traded([half] * GROUP)[1:]
    q_and_d += [pack_queries(g, near) for g in range(1, kv_heads)]

    def pack_near(info_ref, ins, outs):
        for i in range(GROUP - 1):
            outs[0][i * (rows // 2) : (i + 1) * (rows // 2)] = ins[i][...]

    back, own_grads, far_grads, all_terms = [], [], [], []
    pieces, after = None, kv_far[1:]
    for g in range(kv_heads):
        *blocks, attn_cat, own_grad, far_grad = attention(
            info, q_and_d[g], kv_own[g], kv_far[g], after
        )
        far_grads.append(shifted(far_grad, "ctx", -GROUP))
        if pieces is None:
            near_shape = shape((GROUP - 1) * (rows // 2), d_out)
            near = moved(pack_near, info, near, [near_shape], [attn_cat])[0]
            pieces = [out_grad, near, swapped(near, "tp", 1)]
        terms = weight_terms(info, pieces, attn_cat)
        after = [*terms, *far_grads]
        all_terms.append(terms)
        back += traded(blocks)
        own_grads.append(own_grad)

    def add_pair(info_ref, ins, outs):
        for i in range(2):
            outs[i][...] = (ins[i][...].astype(f32) + ins[2][i].astype(f32)).astype(outs[i].dtype)

    weight_blocks = []
    for own, other, away in all_terms:
        met = swapped(away, "ctx", GROUP)
        pair_shape = [shape(*own.shape, dtype=f32), shape(*own.shape)]
        own, other = moved(add_pair, info, [own, other, met], pair_shape, all_terms[-1][:1])
        weight_blocks += traded(split_sum(info, own, swapped(other, "ctx", 2 * GROUP)))

    def lay_out(info_ref, ins, outs):
        for g in range(kv_heads):
            for m in members:
                start = pl.multiple_of((info_ref[0] ^ m) * q_width + g * head_width, HEAD)
                block = ins[g * GROUP + m]
                for i, out in enumerate(outs):
                    piece = block[...] if len(block.shape) == 2 else block[i]
                    out[:, pl.ds(start, head_width)] = piece.astype(out.dtype)

    attn, query_grad = moved(lay_out, info, back, [shape(rows, GROUP * q_width)] * 2, [other])
    mine, theirs = project(info, attn, out_weight)

    def add_shares(info_ref, ins, outs):
        outs[0][...] = (ins[0][...] + ins[1][...].astype(f32)).astype(bf16)

    theirs = swapped(theirs, "tp", 1)
    attn_output = moved(add_shares, info, [mine, theirs], [shape(d_out // 2, rows)])[0]

    def add_up(info_ref, ins, outs):
        for g in range(kv_heads):
            for m in members:
                for i in range(2):
                    at = (i * kv_heads + g) * HEAD
                    total = ins[g][i, m] + ins[kv_heads + g][i, m].astype(f32)
                    outs[m][:, at : at + HEAD] = total.astype(bf16)

    def lay_out_kv(info_ref, ins, outs):
        for m in members:
            start = pl.multiple_of((info_ref[0] ^ m) * kv_width, HEAD)
            for i in range(2):
                outs[i][:, pl.ds(start, kv_width)] = ins[m][:, i * kv_width : (i + 1) * kv_width]

    totals = moved(add_up, info, own_grads + far_grads, [shape(rows, 2 * kv_width)] * GROUP)
    key_grad, value_grad = moved(lay_out_kv, info, traded(totals), [shape(rows, GROUP * kv_width)] * 2)
    out_weight_grad = moved(
        lay_out, info, weight_blocks, [shape(d_out // GROUP // GROUP, GROUP * q_width, dtype=f32)]
    )[0].T
    return (attn_output.T, query_grad, key_grad, value_grad, out_weight_grad)


def single(queries, keys, values, out_weight, out_grad, block_doc):
    tok_rows = queries.shape[0]
    head_size = HEAD
    kv_count = keys.shape[1] // head_size
    group_size = queries.shape[1] // keys.shape[1]
    key_width = keys.shape[1]
    span_blocks = WINDOW // tok_rows
    reach_blocks = min(span_blocks, lax.axis_size("ctx") - 1)
    own_block = lax.axis_index("ctx")
    paired = jnp.stack([keys, values])
    by_distance = jnp.stack(
        [paired] + [shifted(paired, "ctx", distance) for distance in range(1, reach_blocks + 1)]
    )
    ordered = by_distance[::-1]
    missing = span_blocks - reach_blocks
    window_rows = (span_blocks + 1) * tok_rows
    key_window = ordered[:, 0].reshape(window_rows, kv_count, head_size)
    value_window = ordered[:, 1].reshape(window_rows, kv_count, head_size)
    doc_padded = jnp.concatenate([jnp.full((span_blocks,), -1, jnp.int32), block_doc])
    window_docs = lax.dynamic_slice_in_dim(doc_padded, own_block, span_blocks + 1, 0)
    key_docs = jnp.repeat(window_docs, tok_rows)
    own_doc = lax.dynamic_slice_in_dim(block_doc, own_block, 1, 0)
    rel_key = jnp.arange(window_rows, dtype=jnp.int32)
    rel_query = jnp.arange(tok_rows, dtype=jnp.int32) + span_blocks * tok_rows
    visible = (rel_key[None, :] <= rel_query[:, None]) & (
        rel_key[None, :] > rel_query[:, None] - WINDOW
    )
    visible = visible & (key_docs[None, :] == own_doc[0])
    query_heads = queries.reshape(tok_rows, kv_count, group_size, head_size)
    scores = (
        jnp.einsum("tkgd,skd->kgts", query_heads, key_window, preferred_element_type=jnp.float32)
        * query_scale
    )
    scores = jnp.where(visible[None, None], scores, -jnp.inf)
    top = jnp.max(scores, axis=-1, keepdims=True)
    expo = jnp.exp(scores - top)
    probs = expo / jnp.sum(expo, axis=-1, keepdims=True)
    probs_low = probs.astype(jnp.bfloat16)
    attn_heads = jnp.einsum(
        "kgts,skd->tkgd", probs_low, value_window, preferred_element_type=jnp.float32
    ).astype(jnp.bfloat16)
    attn = attn_heads.reshape(tok_rows, queries.shape[1])
    output_terms = jnp.dot(attn, out_weight, preferred_element_type=jnp.float32)
    attn_output = lax.psum_scatter(output_terms, "tp", scatter_dimension=1, tiled=True).astype(
        jnp.bfloat16
    )
    weight_terms = jnp.einsum("tr,tc->rc", attn, out_grad, preferred_element_type=jnp.float32)
    out_weight_grad = lax.psum_scatter(weight_terms, "ctx", scatter_dimension=1, tiled=True)
    d_attn = jnp.einsum(
        "te,re->tr", out_grad, out_weight, preferred_element_type=jnp.float32
    ).astype(jnp.bfloat16)
    d_attn_heads = d_attn.reshape(tok_rows, kv_count, group_size, head_size)
    d_probs = jnp.einsum(
        "tkgd,skd->kgts", d_attn_heads, value_window, preferred_element_type=jnp.float32
    )
    delta = jnp.einsum(
        "tkgd,tkgd->kgt", attn_heads, d_attn_heads, preferred_element_type=jnp.float32
    )
    d_scores = (probs * (d_probs - delta[..., None])).astype(jnp.bfloat16)
    query_grad = (
        jnp.einsum("kgts,skd->tkgd", d_scores, key_window, preferred_element_type=jnp.float32)
        * query_scale
    ).astype(jnp.bfloat16)
    query_grad = query_grad.reshape(tok_rows, queries.shape[1])
    key_part = (
        jnp.einsum("kgts,tkgd->skd", d_scores, query_heads, preferred_element_type=jnp.float32)
        * query_scale
    )
    value_part = jnp.einsum(
        "kgts,tkgd->skd", probs_low, d_attn_heads, preferred_element_type=jnp.float32
    )
    by_position = jnp.stack(
        [
            key_part.reshape(span_blocks + 1, tok_rows, key_width),
            value_part.reshape(span_blocks + 1, tok_rows, key_width),
        ],
        axis=1,
    )
    terms_near = by_position[::-1]
    total = terms_near[0] + sum(
        [shifted(terms_near[distance], "ctx", -distance) for distance in range(1, reach_blocks + 1)]
    )
    key_grad = total[0].astype(jnp.bfloat16)
    value_grad = total[1].astype(jnp.bfloat16)
    return (attn_output, query_grad, key_grad, value_grad, out_weight_grad)


def local(queries, keys, values, out_weight, out_grad, block_doc):
    fits = (
        lax.axis_size("ctx") == GROUP * GROUP
        and queries.shape[0] * GROUP == WINDOW
        and keys.shape[1] == 2 * GROUP * HEAD
        and lax.axis_size("tp") == 2
    )
    step = grouped if fits else single
    return step(queries, keys, values, out_weight, out_grad, block_doc)


def solution(mesh):
    placed = (P("ctx", "tp"), P("ctx", "tp"), P("ctx", "tp"), P("tp", None), P("ctx", None), P())
    return jax.shard_map(
        local,
        mesh=mesh,
        in_specs=placed,
        out_specs=(P("ctx", "tp"), P("ctx", "tp"), P("ctx", "tp"), P("ctx", "tp"), P("tp", "ctx")),
        check_vma=False,
    )
```

```python
import functools

import jax
import jax.numpy as jnp
from jax import lax
from jax.experimental import pallas as pl
from jax.experimental.pallas import tpu as pltpu
from jax.sharding import PartitionSpec as P

HEAD = 128
WINDOW = 1024
GROUP = 4


query_scale = 168.0 ** (-0.5)
LOG2E = 1.4426950408889634
HIDDEN = -1e30


def shifted(shard, axis, by):
    size = lax.axis_size(axis)
    pairs = [(i, i + by) for i in range(size) if 0 <= i + by < size]
    return lax.ppermute(shard, axis, pairs)


def swapped(shard, axis, by):
    return lax.ppermute(shard, axis, [(i, i ^ by) for i in range(lax.axis_size(axis))])


SMEM = pl.BlockSpec(memory_space=pltpu.SMEM)
ANY = pl.BlockSpec(memory_space=pl.ANY)


def attention_kernel(rows, held, info, *refs):
    q_refs, g_refs = refs[:GROUP], refs[GROUP : 2 * GROUP]
    k_own, v_own, k_far, v_far = refs[2 * GROUP : 2 * GROUP + 4]
    held_refs = refs[2 * GROUP + 4 : 2 * GROUP + 4 + held]
    outs = refs[2 * GROUP + 4 + held :]
    back_refs = outs[: 2 * GROUP]
    attn_cat, kv_own, kv_far = outs[2 * GROUP : 2 * GROUP + 3]
    q_all, g_all, k_all, v_all, k_tr, v_tr, k_acc, v_acc, back = outs[2 * GROUP + 3 :]
    r, tp = info[0], info[1]
    heads = q_refs[0].shape[1] // HEAD
    half = rows // 2
    for m in range(GROUP):
        q_all[m] = q_refs[m][...]
        g_all[m] = g_refs[m][...]
        spot = r ^ m
        for place, k, v in ((spot, k_far, v_far), (spot + GROUP, k_own, v_own)):
            k_all[place] = k[m]
            v_all[place] = v[m]
            k_tr[place] = k[m].T
            v_tr[place] = v[m].T
    k_acc[...] = jnp.zeros_like(k_acc)
    v_acc[...] = jnp.zeros_like(v_acc)
    key_at = lax.broadcasted_iota(jnp.int32, (rows, heads * rows), 0)
    query_at = lax.broadcasted_iota(jnp.int32, (rows, heads * rows), 1) % rows
    far_seen, own_seen = key_at > query_at, key_at <= query_at
    nt = (((1,), (1,)), ((), ()))

    def dot(a, b):
        return jnp.dot(a, b, preferred_element_type=jnp.float32)

    def block(m, carry):
        first = r ^ m
        own_doc = info[3 + first + GROUP]
        q = jnp.concatenate([q_all[m, :, h * HEAD : (h + 1) * HEAD] for h in range(heads)], axis=0)
        g = jnp.concatenate([g_all[m, :, h * HEAD : (h + 1) * HEAD] for h in range(heads)], axis=0)
        scores, hidden = [], []
        for j in range(GROUP + 1):
            s = lax.dot_general(k_all[first + j], q, nt, preferred_element_type=jnp.float32)
            if j == 0:
                s = jnp.where(far_seen, s, HIDDEN)
            if j == GROUP:
                s = jnp.where(own_seen, s, HIDDEN)
            scores.append(s)
            hidden.append(jnp.where(info[3 + first + j] == own_doc, 0.0, HIDDEN))
        tops = [jnp.max(s, axis=0, keepdims=True) + b for s, b in zip(scores, hidden)]
        top = functools.reduce(jnp.maximum, tops) * (query_scale * LOG2E)
        expo = [
            jnp.exp2(s * (query_scale * LOG2E) - (top - b)) for s, b in zip(scores, hidden)
        ]
        whole = functools.reduce(jnp.add, [jnp.sum(e, axis=0, keepdims=True) for e in expo])
        inverse = 1.0 / whole
        probs = [e * inverse for e in expo]
        low = [p.astype(jnp.bfloat16) for p in probs]
        attn_tr = functools.reduce(jnp.add, [dot(v_tr[first + j], low[j]) for j in range(GROUP + 1)])
        attn_tr = attn_tr.astype(jnp.bfloat16).astype(jnp.float32)
        delta = jnp.sum(attn_tr * g.astype(jnp.float32).T, axis=0, keepdims=True)
        dq_tr, d_scores = None, []
        for j in range(GROUP + 1):
            d_p = lax.dot_general(v_all[first + j], g, nt, preferred_element_type=jnp.float32)
            d_s = (probs[j] * (d_p - delta)).astype(jnp.bfloat16)
            term = dot(k_tr[first + j], d_s)
            dq_tr = term if dq_tr is None else dq_tr + term
            d_scores.append(d_s)
        for j in range(GROUP + 1):
            k_acc[first + j] += dot(d_scores[j], q)
            v_acc[first + j] += dot(low[j], g)
        attn = attn_tr.T.astype(jnp.bfloat16)
        dq = (dq_tr * query_scale).T.astype(jnp.bfloat16)
        for h in range(heads):
            back[m, 0, :, h * HEAD : (h + 1) * HEAD] = attn[h * rows : (h + 1) * rows]
            back[m, 1, :, h * HEAD : (h + 1) * HEAD] = dq[h * rows : (h + 1) * rows]
        return carry

    lax.fori_loop(0, GROUP, block, 0)
    for m in range(GROUP):
        width = back.shape[3]
        for i in range(2):
            out = back_refs[i * GROUP + m]
            at = out.shape[1] - width
            out[:, at:] = back[m, i]
            if held:
                out[:, :at] = held_refs[i * GROUP + m][...]
        spot = r ^ m
        kv_far[0, m] = (k_acc[spot] * query_scale).astype(kv_far.dtype)
        kv_far[1, m] = v_acc[spot].astype(kv_far.dtype)
        kv_own[0, m] = k_acc[spot + GROUP] * query_scale
        kv_own[1, m] = v_acc[spot + GROUP]
    attn_cat[0:rows] = back[0, 0]
    near = pl.multiple_of(tp * half, half)
    away = pl.multiple_of((1 - tp) * half, half)
    for m in range(1, GROUP):
        at = rows + (m - 1) * half
        attn_cat[at : at + half] = back[m, 0, pl.ds(near, half), :]
        at += (GROUP - 1) * half
        attn_cat[at : at + half] = back[m, 0, pl.ds(away, half), :]


def entire(array):
    return pl.BlockSpec(array.shape, lambda i: (0,) * len(array.shape))


def attention(info, q_and_d, kv_own, kv_far, g, held):
    kv_heads = kv_own.shape[0] // GROUP
    rows, q_block = q_and_d[0].shape[0], q_and_d[0].shape[1] // 2 // kv_heads
    q_spec = pl.BlockSpec((rows, q_block), lambda i: (0, g))
    g_spec = pl.BlockSpec((rows, q_block), lambda i: (0, g + kv_heads))
    k_spec = pl.BlockSpec((GROUP, rows, HEAD), lambda i: (g, 0, 0))
    v_spec = pl.BlockSpec((GROUP, rows, HEAD), lambda i: (g, 0, 1))
    kv_shape = (2, GROUP, rows, HEAD)
    bf16 = jnp.bfloat16
    blocks = 2 * GROUP
    out = [jax.ShapeDtypeStruct((rows, (g + 1) * q_block), bf16)] * (2 * GROUP) + [
        jax.ShapeDtypeStruct((GROUP * rows, q_block), bf16),
        jax.ShapeDtypeStruct(kv_shape, jnp.float32),
        jax.ShapeDtypeStruct(kv_shape, bf16),
    ]
    return pl.pallas_call(
        functools.partial(attention_kernel, rows, len(held)),
        grid=(1,),
        in_specs=[SMEM]
        + [q_spec] * GROUP
        + [g_spec] * GROUP
        + [k_spec, v_spec, k_spec, v_spec]
        + [entire(a) for a in held],
        out_specs=[entire(a) for a in out],
        out_shape=out,
        scratch_shapes=[
            pltpu.VMEM((GROUP, rows, q_block), bf16),
            pltpu.VMEM((GROUP, rows, q_block), bf16),
            pltpu.VMEM((blocks, rows, HEAD), bf16),
            pltpu.VMEM((blocks, rows, HEAD), bf16),
            pltpu.VMEM((blocks, HEAD, rows), bf16),
            pltpu.VMEM((blocks, HEAD, rows), bf16),
            pltpu.VMEM((blocks, rows, HEAD), jnp.float32),
            pltpu.VMEM((blocks, rows, HEAD), jnp.float32),
            pltpu.VMEM((GROUP, 2, rows, q_block), bf16),
        ],
        compiler_params=pltpu.CompilerParams(vmem_limit_bytes=32 * 1024 * 1024),
        cost_estimate=pl.CostEstimate(
            flops=12 * q_block * GROUP * rows * (GROUP + 1) * rows,
            bytes_accessed=5 * 1024 * 1024,
            transcendentals=0,
        ),
    )(info, *q_and_d, *q_and_d, kv_own, kv_own, kv_far, kv_far, *held)


def moved(body, info, arrays, out, after=()):
    n = len(arrays)

    def kernel(info_ref, *refs):
        body(info_ref, refs[:n], refs[n + len(after) :])

    size = sum(a.size * a.dtype.itemsize for a in list(arrays) + list(out))
    return pl.pallas_call(
        kernel,
        grid=(1,),
        in_specs=[SMEM] + [entire(a) for a in arrays] + [ANY] * len(after),
        out_specs=[entire(a) for a in out],
        out_shape=list(out),
        compiler_params=pltpu.CompilerParams(vmem_limit_bytes=32 * 1024 * 1024),
        cost_estimate=pl.CostEstimate(flops=0, bytes_accessed=size, transcendentals=0),
    )(info, *arrays, *after)


def columns(ref, start, width):
    return ref[:, pl.ds(pl.multiple_of(start, HEAD), width)]


def pack_kv(keys, values):
    rows, width = keys.shape[0], keys.shape[1] // GROUP

    def kernel(k_ref, v_ref, *refs):
        outs, sems = refs[:GROUP], refs[GROUP]
        r = lax.axis_index("ctx") % GROUP
        copies = []
        for m in range(GROUP):
            for i, ref in enumerate((k_ref, v_ref)):
                start = pl.multiple_of((r ^ m) * width, HEAD)
                copies.append(
                    pltpu.make_async_copy(
                        ref.at[:, pl.ds(start, width)],
                        outs[m].at[:, i * width : (i + 1) * width],
                        sems.at[2 * m + i],
                    )
                )
        for copy in copies:
            copy.start()
        for copy in copies:
            copy.wait()

    out = [jax.ShapeDtypeStruct((rows, 2 * width), keys.dtype)] * GROUP
    return pl.pallas_call(
        kernel,
        in_specs=[ANY, ANY],
        out_specs=[pl.BlockSpec(memory_space=pltpu.VMEM)] * GROUP,
        out_shape=out,
        scratch_shapes=[pltpu.SemaphoreType.DMA((2 * GROUP,))],
        compiler_params=pltpu.CompilerParams(vmem_limit_bytes=32 * 1024 * 1024),
        cost_estimate=pl.CostEstimate(
            flops=0, bytes_accessed=4 * keys.size, transcendentals=0
        ),
    )(keys, values)


def project_back(info, out_grad, out_weight):
    rows, d_out = out_grad.shape
    steps = GROUP
    block = out_weight.shape[0] // steps

    def kernel(info_ref, grad, weight, *outs):
        step = pl.program_id(0)
        part = lax.dot_general(
            grad[...], weight[...], (((1,), (1,)), ((), ())), preferred_element_type=jnp.float32
        ).astype(jnp.bfloat16)
        for at in range(steps):

            @pl.when(step == at)
            def _():
                outs[at][...] = part

    def weight_block(step, info_ref):
        return (info_ref[0] ^ step, 0)

    return pl.pallas_call(
        kernel,
        grid_spec=pltpu.PrefetchScalarGridSpec(
            num_scalar_prefetch=1,
            grid=(steps,),
            in_specs=[
                pl.BlockSpec((rows, d_out), lambda i, info_ref: (0, 0)),
                pl.BlockSpec((block, d_out), weight_block),
            ],
            out_specs=[pl.BlockSpec((rows, block), lambda i, info_ref: (0, 0))] * steps,
        ),
        out_shape=[jax.ShapeDtypeStruct((rows, block), jnp.bfloat16)] * steps,
        compiler_params=pltpu.CompilerParams(vmem_limit_bytes=32 * 1024 * 1024),
        cost_estimate=pl.CostEstimate(
            flops=2 * rows * out_weight.size, bytes_accessed=2 * out_weight.size, transcendentals=0
        ),
    )(info, out_grad, out_weight)

def weight_terms(info, pieces, attn_cat, after=()):
    d_out, width = pieces[0].shape[1], attn_cat.shape[1]
    block = 3 * HEAD if d_out % (3 * HEAD) == 0 else d_out
    steps, cut = d_out // block, d_out // GROUP

    def kernel(info_ref, *refs):
        inputs, attn = refs[: len(pieces)], refs[len(pieces)]
        own, other, away, whole = refs[len(pieces) + 1 + len(after) :]
        total, at = None, 0
        for piece in inputs:
            rows = piece.shape[0]
            term = lax.dot_general(
                piece[...],
                attn[at : at + rows],
                (((0,), (0,)), ((), ())),
                preferred_element_type=jnp.float32,
            )
            total, at = term if total is None else total + term, at + rows
        step = pl.program_id(0)
        whole[pl.ds(pl.multiple_of(step * block, block), block)] = total.astype(whole.dtype)

        @pl.when(step == steps - 1)
        def _():
            def chunk(m):
                return whole[pl.ds(pl.multiple_of((info_ref[2] ^ m) * cut, 16), cut)]

            own[...] = chunk(0)
            other[...] = chunk(2)
            away[0] = chunk(1)
            away[1] = chunk(3)

    shapes = [(cut, width), (cut, width), (2, cut, width)]
    out = [jax.ShapeDtypeStruct(s, jnp.bfloat16) for s in shapes]
    return pl.pallas_call(
        kernel,
        grid=(steps,),
        in_specs=[SMEM]
        + [pl.BlockSpec((p.shape[0], block), lambda i: (0, i)) for p in pieces]
        + [entire(attn_cat)]
        + [ANY] * len(after),
        out_specs=[entire(a) for a in out],
        out_shape=out,
        scratch_shapes=[pltpu.VMEM((d_out, width), jnp.bfloat16)],
        compiler_params=pltpu.CompilerParams(vmem_limit_bytes=32 * 1024 * 1024),
        cost_estimate=pl.CostEstimate(
            flops=2 * attn_cat.size * d_out,
            bytes_accessed=2 * (attn_cat.shape[0] + width) * d_out,
            transcendentals=0,
        ),
    )(info, *pieces, attn_cat, *after)


def split_sums(info, pairs):
    rows, width = pairs[0][0].shape
    cut, count = rows // GROUP, len(pairs)

    def kernel(info_ref, *refs):
        outs, total = refs[2 * count : 2 * count + GROUP], refs[2 * count + GROUP]
        for g in range(count):
            total[...] = refs[2 * g][...].astype(jnp.float32) + refs[2 * g + 1][...].astype(jnp.float32)
            for m in range(GROUP):
                start = pl.multiple_of((info_ref[0] ^ m) * cut, 8)
                block = total[pl.ds(start, cut)].astype(outs[m].dtype)
                outs[m][:, g * width : (g + 1) * width] = block

    flat = [a for pair in pairs for a in pair]
    out = [jax.ShapeDtypeStruct((cut, count * width), jnp.bfloat16)] * GROUP
    return pl.pallas_call(
        kernel,
        grid=(1,),
        in_specs=[SMEM] + [entire(a) for a in flat],
        out_specs=[entire(a) for a in out],
        out_shape=out,
        scratch_shapes=[pltpu.VMEM((rows, width), jnp.float32)],
        compiler_params=pltpu.CompilerParams(vmem_limit_bytes=32 * 1024 * 1024),
    )(info, *flat)


def project(info, attn, out_weight, after):
    rows, depth = attn.shape
    d_out = out_weight.shape[1]
    block = 3 * HEAD if d_out % (3 * HEAD) == 0 else d_out
    steps, half = d_out // block, d_out // 2

    def kernel(info_ref, attn_ref, weight, *refs):
        mine, theirs, whole = refs[len(after) :]
        step = pl.program_id(0)
        part = jnp.dot(attn_ref[...], weight[...], preferred_element_type=jnp.float32)
        whole[pl.ds(pl.multiple_of(step * block, block), block)] = part.T

        @pl.when(step == steps - 1)
        def _():
            tp = info_ref[1]
            mine[...] = whole[pl.ds(pl.multiple_of(tp * half, 8), half)]
            other = whole[pl.ds(pl.multiple_of((1 - tp) * half, 8), half)]
            theirs[...] = other.astype(theirs.dtype)

    out = [jax.ShapeDtypeStruct((half, rows), d) for d in (jnp.float32, jnp.bfloat16)]
    return pl.pallas_call(
        kernel,
        grid=(steps,),
        in_specs=[SMEM, entire(attn), pl.BlockSpec((depth, block), lambda i: (0, i))]
        + [ANY] * len(after),
        out_specs=[entire(a) for a in out],
        out_shape=out,
        scratch_shapes=[pltpu.VMEM((d_out, rows), jnp.float32)],
        compiler_params=pltpu.CompilerParams(vmem_limit_bytes=32 * 1024 * 1024),
        cost_estimate=pl.CostEstimate(
            flops=2 * attn.size * d_out, bytes_accessed=2 * out_weight.size, transcendentals=0
        ),
    )(info, attn, out_weight, *after)


def grouped(queries, keys, values, out_weight, out_grad, block_doc):
    f32, bf16 = jnp.float32, jnp.bfloat16
    rows = queries.shape[0]
    me, tp = lax.axis_index("ctx"), lax.axis_index("tp")
    r, layer = me % GROUP, me // GROUP
    members = range(GROUP)
    q_width, kv_width = queries.shape[1] // GROUP, keys.shape[1] // GROUP
    kv_heads = kv_width // HEAD
    head_width = q_width // kv_heads
    d_out = out_grad.shape[1]
    doc_padded = jnp.concatenate([jnp.full((GROUP,), -1, jnp.int32), block_doc])
    docs = lax.dynamic_slice_in_dim(doc_padded, layer * GROUP, 2 * GROUP, 0)
    info = jnp.concatenate([jnp.stack([r, tp, layer]).astype(jnp.int32), docs])

    def shape(*dims, dtype=bf16):
        return jax.ShapeDtypeStruct(dims, dtype)

    def traded(blocks):
        return [blocks[0]] + [swapped(blocks[m], "ctx", m) for m in members[1:]]

    kv = traded(pack_kv(keys, values))
    d_attn = project_back(info, out_grad, out_weight)

    def pack_queries(info_ref, ins, outs):
        for m in members:
            outs[m][:, :q_width] = columns(ins[0], (info_ref[0] ^ m) * q_width, q_width)
            outs[m][:, q_width:] = ins[1 + m][...]

    packed = moved(pack_queries, info, [queries, *d_attn], [shape(rows, 2 * q_width)] * GROUP)
    q_and_d = traded(packed)

    def pack_heads(info_ref, ins, outs):
        for m in members:
            for g in range(kv_heads):
                for i in range(2):
                    at = (i * kv_heads + g) * HEAD
                    outs[0][g * GROUP + m, :, i * HEAD : (i + 1) * HEAD] = ins[m][:, at : at + HEAD]

    kv_own = moved(pack_heads, info, kv, [shape(kv_heads * GROUP, rows, 2 * HEAD)], packed)[0]
    kv_far = shifted(kv_own, "ctx", GROUP)

    def pack_half(info_ref, ins, outs):
        outs[0][...] = ins[0][pl.ds(pl.multiple_of(info_ref[1] * (rows // 2), 16), rows // 2), :]

    half = moved(pack_half, info, [out_grad], [shape(rows // 2, d_out)], q_and_d[1:])[0]
    near = traded([half] * GROUP)[1:]

    def pack_near(info_ref, ins, outs):
        for i in range(GROUP - 1):
            outs[0][i * (rows // 2) : (i + 1) * (rows // 2)] = ins[i][...]

    parts, held = [], []
    for g in range(kv_heads):
        parts.append(attention(info, q_and_d, kv_own, kv_far, g, held))
        held = parts[-1][: 2 * GROUP]
    far_grads = [shifted(p[-1], "ctx", -GROUP) for p in parts]
    own_grads = [p[-2] for p in parts]
    attn_cats = [p[-3] for p in parts]
    attn, query_grad = traded(held[:GROUP]), traded(held[GROUP:])
    near_shape = shape((GROUP - 1) * (rows // 2), d_out)
    near = moved(pack_near, info, near, [near_shape], [*attn_cats, far_grads[0]])[0]
    pieces = [out_grad, near, swapped(near, "tp", 1)]
    all_terms = [weight_terms(info, pieces, attn_cats[0])]
    for g in range(1, kv_heads):
        all_terms.append(weight_terms(info, pieces, attn_cats[g], [far_grads[g]]))

    def add_pair(info_ref, ins, outs):
        for i in range(2):
            outs[i][...] = (ins[i][...].astype(f32) + ins[2][i].astype(f32)).astype(outs[i].dtype)

    def add_layers(terms, after):
        own, other, away = terms
        met = swapped(away, "ctx", GROUP)
        pair_shape = [shape(*own.shape, dtype=f32), shape(*own.shape)]
        own, other = moved(add_pair, info, [own, other, met], pair_shape, after)
        return own, other, swapped(other, "ctx", 2 * GROUP)

    sums = [add_layers(all_terms[0], all_terms[-1][:1])]

    def add_up(info_ref, ins, outs):
        for g in range(kv_heads):
            for m in members:
                for i in range(2):
                    at = (i * kv_heads + g) * HEAD
                    total = ins[g][i, m] + ins[kv_heads + g][i, m].astype(f32)
                    outs[m][:, at : at + HEAD] = total.astype(bf16)

    def lay_out_kv(info_ref, ins, outs):
        for m in members:
            start = pl.multiple_of((info_ref[0] ^ m) * kv_width, HEAD)
            for i in range(2):
                outs[i][:, pl.ds(start, kv_width)] = ins[m][:, i * kv_width : (i + 1) * kv_width]

    total_shape = [shape(rows, 2 * kv_width)] * GROUP
    totals = moved(add_up, info, own_grads + far_grads, total_shape, [*attn[1:], *query_grad[1:], sums[0][1]])
    key_grad, value_grad = moved(lay_out_kv, info, traded(totals), [shape(rows, GROUP * kv_width)] * 2)

    def lay_out(info_ref, ins, outs):
        for m in members:
            start = pl.multiple_of((info_ref[0] ^ m) * q_width, HEAD)
            outs[0][:, pl.ds(start, q_width)] = ins[m][...]

    attn = moved(lay_out, info, attn, [shape(rows, GROUP * q_width)], sums[0][1:2])[0]
    mine, theirs = project(info, attn, out_weight, [])
    for terms in all_terms[1:]:
        sums.append(add_layers(terms, [sums[-1][2], theirs]))
    query_grad = moved(lay_out, info, query_grad, [shape(rows, GROUP * q_width)], totals)[0]

    def add_shares(info_ref, ins, outs):
        outs[0][...] = (ins[0][...] + ins[1][...].astype(f32)).astype(bf16)

    theirs = swapped(theirs, "tp", 1)
    attn_output = moved(add_shares, info, [mine, theirs], [shape(d_out // 2, rows)])[0]

    def lay_out_weight(info_ref, ins, outs):
        for m in members:
            start = pl.multiple_of((info_ref[0] ^ m) * q_width, HEAD)
            outs[0][:, pl.ds(start, q_width)] = ins[m][...].astype(f32)

    blocks = traded(split_sums(info, [(own, met) for own, other, met in sums]))
    grad_shape = [shape(d_out // GROUP // GROUP, GROUP * q_width, dtype=f32)]
    late = [attn_output, key_grad, query_grad]
    out_weight_grad = moved(lay_out_weight, info, blocks, grad_shape, late)[0].T
    return (attn_output.T, query_grad, key_grad, value_grad, out_weight_grad)


def single(queries, keys, values, out_weight, out_grad, block_doc):
    tok_rows = queries.shape[0]
    head_size = HEAD
    kv_count = keys.shape[1] // head_size
    group_size = queries.shape[1] // keys.shape[1]
    key_width = keys.shape[1]
    span_blocks = WINDOW // tok_rows
    reach_blocks = min(span_blocks, lax.axis_size("ctx") - 1)
    own_block = lax.axis_index("ctx")
    paired = jnp.stack([keys, values])
    by_distance = jnp.stack(
        [paired] + [shifted(paired, "ctx", distance) for distance in range(1, reach_blocks + 1)]
    )
    ordered = by_distance[::-1]
    missing = span_blocks - reach_blocks
    window_rows = (span_blocks + 1) * tok_rows
    key_window = ordered[:, 0].reshape(window_rows, kv_count, head_size)
    value_window = ordered[:, 1].reshape(window_rows, kv_count, head_size)
    doc_padded = jnp.concatenate([jnp.full((span_blocks,), -1, jnp.int32), block_doc])
    window_docs = lax.dynamic_slice_in_dim(doc_padded, own_block, span_blocks + 1, 0)
    key_docs = jnp.repeat(window_docs, tok_rows)
    own_doc = lax.dynamic_slice_in_dim(block_doc, own_block, 1, 0)
    rel_key = jnp.arange(window_rows, dtype=jnp.int32)
    rel_query = jnp.arange(tok_rows, dtype=jnp.int32) + span_blocks * tok_rows
    visible = (rel_key[None, :] <= rel_query[:, None]) & (
        rel_key[None, :] > rel_query[:, None] - WINDOW
    )
    visible = visible & (key_docs[None, :] == own_doc[0])
    query_heads = queries.reshape(tok_rows, kv_count, group_size, head_size)
    scores = (
        jnp.einsum("tkgd,skd->kgts", query_heads, key_window, preferred_element_type=jnp.float32)
        * query_scale
    )
    scores = jnp.where(visible[None, None], scores, -jnp.inf)
    top = jnp.max(scores, axis=-1, keepdims=True)
    expo = jnp.exp(scores - top)
    probs = expo / jnp.sum(expo, axis=-1, keepdims=True)
    probs_low = probs.astype(jnp.bfloat16)
    attn_heads = jnp.einsum(
        "kgts,skd->tkgd", probs_low, value_window, preferred_element_type=jnp.float32
    ).astype(jnp.bfloat16)
    attn = attn_heads.reshape(tok_rows, queries.shape[1])
    output_terms = jnp.dot(attn, out_weight, preferred_element_type=jnp.float32)
    attn_output = lax.psum_scatter(output_terms, "tp", scatter_dimension=1, tiled=True).astype(
        jnp.bfloat16
    )
    weight_terms = jnp.einsum("tr,tc->rc", attn, out_grad, preferred_element_type=jnp.float32)
    out_weight_grad = lax.psum_scatter(weight_terms, "ctx", scatter_dimension=1, tiled=True)
    d_attn = jnp.einsum(
        "te,re->tr", out_grad, out_weight, preferred_element_type=jnp.float32
    ).astype(jnp.bfloat16)
    d_attn_heads = d_attn.reshape(tok_rows, kv_count, group_size, head_size)
    d_probs = jnp.einsum(
        "tkgd,skd->kgts", d_attn_heads, value_window, preferred_element_type=jnp.float32
    )
    delta = jnp.einsum(
        "tkgd,tkgd->kgt", attn_heads, d_attn_heads, preferred_element_type=jnp.float32
    )
    d_scores = (probs * (d_probs - delta[..., None])).astype(jnp.bfloat16)
    query_grad = (
        jnp.einsum("kgts,skd->tkgd", d_scores, key_window, preferred_element_type=jnp.float32)
        * query_scale
    ).astype(jnp.bfloat16)
    query_grad = query_grad.reshape(tok_rows, queries.shape[1])
    key_part = (
        jnp.einsum("kgts,tkgd->skd", d_scores, query_heads, preferred_element_type=jnp.float32)
        * query_scale
    )
    value_part = jnp.einsum(
        "kgts,tkgd->skd", probs_low, d_attn_heads, preferred_element_type=jnp.float32
    )
    by_position = jnp.stack(
        [
            key_part.reshape(span_blocks + 1, tok_rows, key_width),
            value_part.reshape(span_blocks + 1, tok_rows, key_width),
        ],
        axis=1,
    )
    terms_near = by_position[::-1]
    total = terms_near[0] + sum(
        [shifted(terms_near[distance], "ctx", -distance) for distance in range(1, reach_blocks + 1)]
    )
    key_grad = total[0].astype(jnp.bfloat16)
    value_grad = total[1].astype(jnp.bfloat16)
    return (attn_output, query_grad, key_grad, value_grad, out_weight_grad)


def local(queries, keys, values, out_weight, out_grad, block_doc):
    fits = (
        lax.axis_size("ctx") == GROUP * GROUP
        and queries.shape[0] * GROUP == WINDOW
        and keys.shape[1] == 2 * GROUP * HEAD
        and lax.axis_size("tp") == 2
    )
    step = grouped if fits else single
    return step(queries, keys, values, out_weight, out_grad, block_doc)


def solution(mesh):
    placed = (P("ctx", "tp"), P("ctx", "tp"), P("ctx", "tp"), P("tp", None), P("ctx", None), P())
    return jax.shard_map(
        local,
        mesh=mesh,
        in_specs=placed,
        out_specs=(P("ctx", "tp"), P("ctx", "tp"), P("ctx", "tp"), P("ctx", "tp"), P("tp", "ctx")),
        check_vma=False,
    )
```

```python
import functools

import jax
import jax.numpy as jnp
from jax import lax
from jax.experimental import pallas as pl
from jax.experimental.pallas import tpu as pltpu
from jax.sharding import PartitionSpec as P

HEAD = 128
WINDOW = 1024
GROUP = 4


query_scale = 168.0 ** (-0.5)
LOG2E = 1.4426950408889634
HIDDEN = -1e30


def shifted(shard, axis, by):
    size = lax.axis_size(axis)
    pairs = [(i, i + by) for i in range(size) if 0 <= i + by < size]
    return lax.ppermute(shard, axis, pairs)


def swapped(shard, axis, by):
    return lax.ppermute(shard, axis, [(i, i ^ by) for i in range(lax.axis_size(axis))])


SMEM = pl.BlockSpec(memory_space=pltpu.SMEM)
ANY = pl.BlockSpec(memory_space=pl.ANY)


def attention_kernel(rows, held, info, *refs):
    q_refs, g_refs = refs[:GROUP], refs[GROUP : 2 * GROUP]
    k_own, v_own, k_far, v_far = refs[2 * GROUP : 2 * GROUP + 4]
    held_refs = refs[2 * GROUP + 4 : 2 * GROUP + 4 + held]
    outs = refs[2 * GROUP + 4 + held :]
    back_refs = outs[: 2 * GROUP]
    attn_cat, kv_own, kv_far = outs[2 * GROUP : 2 * GROUP + 3]
    q_all, g_all, k_all, v_all, k_tr, v_tr, k_acc, v_acc, back = outs[2 * GROUP + 3 :]
    r, tp = info[0], info[1]
    heads = q_refs[0].shape[1] // HEAD
    half = rows // 2
    for m in range(GROUP):
        q_all[m] = q_refs[m][...]
        g_all[m] = g_refs[m][...]
        spot = r ^ m
        for place, k, v in ((spot, k_far, v_far), (spot + GROUP, k_own, v_own)):
            k_all[place] = k[m]
            v_all[place] = v[m]
            k_tr[place] = k[m].T
            v_tr[place] = v[m].T
    k_acc[...] = jnp.zeros_like(k_acc)
    v_acc[...] = jnp.zeros_like(v_acc)
    key_at = lax.broadcasted_iota(jnp.int32, (rows, heads * rows), 0)
    query_at = lax.broadcasted_iota(jnp.int32, (rows, heads * rows), 1) % rows
    far_seen, own_seen = key_at > query_at, key_at <= query_at
    nt = (((1,), (1,)), ((), ()))

    def dot(a, b):
        return jnp.dot(a, b, preferred_element_type=jnp.float32)

    def block(m, carry):
        first = r ^ m
        own_doc = info[3 + first + GROUP]
        q = jnp.concatenate([q_all[m, :, h * HEAD : (h + 1) * HEAD] for h in range(heads)], axis=0)
        g = jnp.concatenate([g_all[m, :, h * HEAD : (h + 1) * HEAD] for h in range(heads)], axis=0)
        scores, hidden = [], []
        for j in range(GROUP + 1):
            s = lax.dot_general(k_all[first + j], q, nt, preferred_element_type=jnp.float32)
            if j == 0:
                s = jnp.where(far_seen, s, HIDDEN)
            if j == GROUP:
                s = jnp.where(own_seen, s, HIDDEN)
            scores.append(s)
            hidden.append(jnp.where(info[3 + first + j] == own_doc, 0.0, HIDDEN))
        tops = [jnp.max(s, axis=0, keepdims=True) + b for s, b in zip(scores, hidden)]
        top = functools.reduce(jnp.maximum, tops) * (query_scale * LOG2E)
        expo = [
            jnp.exp2(s * (query_scale * LOG2E) - (top - b)) for s, b in zip(scores, hidden)
        ]
        whole = functools.reduce(jnp.add, [jnp.sum(e, axis=0, keepdims=True) for e in expo])
        inverse = 1.0 / whole
        probs = [e * inverse for e in expo]
        low = [p.astype(jnp.bfloat16) for p in probs]
        attn_tr = functools.reduce(jnp.add, [dot(v_tr[first + j], low[j]) for j in range(GROUP + 1)])
        attn_tr = attn_tr.astype(jnp.bfloat16).astype(jnp.float32)
        delta = jnp.sum(attn_tr * g.astype(jnp.float32).T, axis=0, keepdims=True)
        dq_tr, d_scores = None, []
        for j in range(GROUP + 1):
            d_p = lax.dot_general(v_all[first + j], g, nt, preferred_element_type=jnp.float32)
            d_s = (probs[j] * (d_p - delta)).astype(jnp.bfloat16)
            term = dot(k_tr[first + j], d_s)
            dq_tr = term if dq_tr is None else dq_tr + term
            d_scores.append(d_s)
        for j in range(GROUP + 1):
            k_acc[first + j] += dot(d_scores[j], q)
            v_acc[first + j] += dot(low[j], g)
        attn = attn_tr.T.astype(jnp.bfloat16)
        dq = (dq_tr * query_scale).T.astype(jnp.bfloat16)
        for h in range(heads):
            back[m, 0, :, h * HEAD : (h + 1) * HEAD] = attn[h * rows : (h + 1) * rows]
            back[m, 1, :, h * HEAD : (h + 1) * HEAD] = dq[h * rows : (h + 1) * rows]
        return carry

    for m in range(GROUP):
        block(m, 0)
    for m in range(GROUP):
        width = back.shape[3]
        for i in range(2):
            out = back_refs[i * GROUP + m]
            at = out.shape[1] - width
            out[:, at:] = back[m, i]
            if held:
                out[:, :at] = held_refs[i * GROUP + m][...]
        spot = r ^ m
        kv_far[0, m] = (k_acc[spot] * query_scale).astype(kv_far.dtype)
        kv_far[1, m] = v_acc[spot].astype(kv_far.dtype)
        kv_own[0, m] = k_acc[spot + GROUP] * query_scale
        kv_own[1, m] = v_acc[spot + GROUP]
    attn_cat[0:rows] = back[0, 0]
    near = pl.multiple_of(tp * half, half)
    away = pl.multiple_of((1 - tp) * half, half)
    for m in range(1, GROUP):
        at = rows + (m - 1) * half
        attn_cat[at : at + half] = back[m, 0, pl.ds(near, half), :]
        at += (GROUP - 1) * half
        attn_cat[at : at + half] = back[m, 0, pl.ds(away, half), :]


def entire(array):
    return pl.BlockSpec(array.shape, lambda i: (0,) * len(array.shape))


def attention(info, q_and_d, kv_own, kv_far, g, held):
    kv_heads = kv_own.shape[0] // GROUP
    rows, q_block = q_and_d[0].shape[0], q_and_d[0].shape[1] // 2 // kv_heads
    q_spec = pl.BlockSpec((rows, q_block), lambda i: (0, g))
    g_spec = pl.BlockSpec((rows, q_block), lambda i: (0, g + kv_heads))
    k_spec = pl.BlockSpec((GROUP, rows, HEAD), lambda i: (g, 0, 0))
    v_spec = pl.BlockSpec((GROUP, rows, HEAD), lambda i: (g, 0, 1))
    kv_shape = (2, GROUP, rows, HEAD)
    bf16 = jnp.bfloat16
    blocks = 2 * GROUP
    out = [jax.ShapeDtypeStruct((rows, (g + 1) * q_block), bf16)] * (2 * GROUP) + [
        jax.ShapeDtypeStruct((GROUP * rows, q_block), bf16),
        jax.ShapeDtypeStruct(kv_shape, jnp.float32),
        jax.ShapeDtypeStruct(kv_shape, bf16),
    ]
    return pl.pallas_call(
        functools.partial(attention_kernel, rows, len(held)),
        grid=(1,),
        in_specs=[SMEM]
        + [q_spec] * GROUP
        + [g_spec] * GROUP
        + [k_spec, v_spec, k_spec, v_spec]
        + [entire(a) for a in held],
        out_specs=[entire(a) for a in out],
        out_shape=out,
        scratch_shapes=[
            pltpu.VMEM((GROUP, rows, q_block), bf16),
            pltpu.VMEM((GROUP, rows, q_block), bf16),
            pltpu.VMEM((blocks, rows, HEAD), bf16),
            pltpu.VMEM((blocks, rows, HEAD), bf16),
            pltpu.VMEM((blocks, HEAD, rows), bf16),
            pltpu.VMEM((blocks, HEAD, rows), bf16),
            pltpu.VMEM((blocks, rows, HEAD), jnp.float32),
            pltpu.VMEM((blocks, rows, HEAD), jnp.float32),
            pltpu.VMEM((GROUP, 2, rows, q_block), bf16),
        ],
        compiler_params=pltpu.CompilerParams(vmem_limit_bytes=32 * 1024 * 1024),
        cost_estimate=pl.CostEstimate(
            flops=12 * q_block * GROUP * rows * (GROUP + 1) * rows,
            bytes_accessed=5 * 1024 * 1024,
            transcendentals=0,
        ),
    )(info, *q_and_d, *q_and_d, kv_own, kv_own, kv_far, kv_far, *held)


def moved(body, info, arrays, out, after=()):
    n = len(arrays)

    def kernel(info_ref, *refs):
        body(info_ref, refs[:n], refs[n + len(after) :])

    size = sum(a.size * a.dtype.itemsize for a in list(arrays) + list(out))
    return pl.pallas_call(
        kernel,
        grid=(1,),
        in_specs=[SMEM] + [entire(a) for a in arrays] + [ANY] * len(after),
        out_specs=[entire(a) for a in out],
        out_shape=list(out),
        compiler_params=pltpu.CompilerParams(vmem_limit_bytes=32 * 1024 * 1024),
        cost_estimate=pl.CostEstimate(flops=0, bytes_accessed=size, transcendentals=0),
    )(info, *arrays, *after)


def columns(ref, start, width):
    return ref[:, pl.ds(pl.multiple_of(start, HEAD), width)]


def pack_kv(keys, values):
    rows, width = keys.shape[0], keys.shape[1] // GROUP

    def kernel(k_ref, v_ref, *refs):
        outs, sems = refs[:GROUP], refs[GROUP]
        r = lax.axis_index("ctx") % GROUP
        copies = []
        for m in range(GROUP):
            for i, ref in enumerate((k_ref, v_ref)):
                start = pl.multiple_of((r ^ m) * width, HEAD)
                copies.append(
                    pltpu.make_async_copy(
                        ref.at[:, pl.ds(start, width)],
                        outs[m].at[:, i * width : (i + 1) * width],
                        sems.at[2 * m + i],
                    )
                )
        for copy in copies:
            copy.start()
        for copy in copies:
            copy.wait()

    out = [jax.ShapeDtypeStruct((rows, 2 * width), keys.dtype)] * GROUP
    return pl.pallas_call(
        kernel,
        in_specs=[ANY, ANY],
        out_specs=[pl.BlockSpec(memory_space=pltpu.VMEM)] * GROUP,
        out_shape=out,
        scratch_shapes=[pltpu.SemaphoreType.DMA((2 * GROUP,))],
        compiler_params=pltpu.CompilerParams(vmem_limit_bytes=32 * 1024 * 1024),
        cost_estimate=pl.CostEstimate(
            flops=0, bytes_accessed=4 * keys.size, transcendentals=0
        ),
    )(keys, values)


def project_back(info, out_grad, out_weight):
    rows, d_out = out_grad.shape
    steps = GROUP
    block = out_weight.shape[0] // steps

    def kernel(info_ref, grad, weight, *outs):
        step = pl.program_id(0)
        part = lax.dot_general(
            grad[...], weight[...], (((1,), (1,)), ((), ())), preferred_element_type=jnp.float32
        ).astype(jnp.bfloat16)
        for at in range(steps):

            @pl.when(step == at)
            def _():
                outs[at][...] = part

    def weight_block(step, info_ref):
        return (info_ref[0] ^ step, 0)

    return pl.pallas_call(
        kernel,
        grid_spec=pltpu.PrefetchScalarGridSpec(
            num_scalar_prefetch=1,
            grid=(steps,),
            in_specs=[
                pl.BlockSpec((rows, d_out), lambda i, info_ref: (0, 0)),
                pl.BlockSpec((block, d_out), weight_block),
            ],
            out_specs=[pl.BlockSpec((rows, block), lambda i, info_ref: (0, 0))] * steps,
        ),
        out_shape=[jax.ShapeDtypeStruct((rows, block), jnp.bfloat16)] * steps,
        compiler_params=pltpu.CompilerParams(vmem_limit_bytes=32 * 1024 * 1024),
        cost_estimate=pl.CostEstimate(
            flops=2 * rows * out_weight.size, bytes_accessed=2 * out_weight.size, transcendentals=0
        ),
    )(info, out_grad, out_weight)

def weight_terms(info, pieces, attn_cat, near, after=()):
    d_out, width = pieces[0].shape[1], attn_cat.shape[1]
    block = 3 * HEAD if d_out % (3 * HEAD) == 0 else d_out
    steps, cut = d_out // block, d_out // GROUP

    def kernel(info_ref, *refs):
        inputs, attn = refs[: len(pieces)], refs[len(pieces)]
        own, other, away, whole = refs[len(pieces) + 1 + len(after) :]
        total, at = None, 0
        for piece in inputs:
            rows = piece.shape[0]
            term = lax.dot_general(
                piece[...],
                attn[at : at + rows],
                (((0,), (0,)), ((), ())),
                preferred_element_type=jnp.float32,
            )
            total, at = term if total is None else total + term, at + rows
        step = pl.program_id(0)
        whole[pl.ds(pl.multiple_of(step * block, block), block)] = total.astype(whole.dtype)

        @pl.when(step == steps - 1)
        def _():
            def chunk(m):
                return whole[pl.ds(pl.multiple_of((info_ref[2] ^ m) * cut, 16), cut)]

            own[...] = chunk(0)
            other[...] = chunk(3 ^ near)
            away[0] = chunk(near)
            away[1] = chunk(3)

    shapes = [(cut, width), (cut, width), (2, cut, width)]
    out = [jax.ShapeDtypeStruct(s, jnp.bfloat16) for s in shapes]
    return pl.pallas_call(
        kernel,
        grid=(steps,),
        in_specs=[SMEM]
        + [pl.BlockSpec((p.shape[0], block), lambda i: (0, i)) for p in pieces]
        + [entire(attn_cat)]
        + [ANY] * len(after),
        out_specs=[entire(a) for a in out],
        out_shape=out,
        scratch_shapes=[pltpu.VMEM((d_out, width), jnp.bfloat16)],
        compiler_params=pltpu.CompilerParams(vmem_limit_bytes=32 * 1024 * 1024),
        cost_estimate=pl.CostEstimate(
            flops=2 * attn_cat.size * d_out,
            bytes_accessed=2 * (attn_cat.shape[0] + width) * d_out,
            transcendentals=0,
        ),
    )(info, *pieces, attn_cat, *after)


def split_sums(info, pairs, after):
    rows, width = pairs[0][0].shape
    cut, count = rows // GROUP, len(pairs)

    def kernel(info_ref, *refs):
        outs, total = refs[-1 - GROUP : -1], refs[-1]
        for g in range(count):
            total[...] = refs[2 * g][...].astype(jnp.float32) + refs[2 * g + 1][...].astype(jnp.float32)
            for m in range(GROUP):
                start = pl.multiple_of((info_ref[0] ^ m) * cut, 8)
                block = total[pl.ds(start, cut)].astype(outs[m].dtype)
                outs[m][:, g * width : (g + 1) * width] = block

    flat = [a for pair in pairs for a in pair]
    out = [jax.ShapeDtypeStruct((cut, count * width), jnp.bfloat16)] * GROUP
    return pl.pallas_call(
        kernel,
        grid=(1,),
        in_specs=[SMEM] + [entire(a) for a in flat] + [ANY] * len(after),
        out_specs=[entire(a) for a in out],
        out_shape=out,
        scratch_shapes=[pltpu.VMEM((rows, width), jnp.float32)],
        compiler_params=pltpu.CompilerParams(vmem_limit_bytes=32 * 1024 * 1024),
    )(info, *flat, *after)


def project(info, attn, out_weight, after):
    rows, depth = attn.shape
    d_out = out_weight.shape[1]
    block = 3 * HEAD if d_out % (3 * HEAD) == 0 else d_out
    steps, half = d_out // block, d_out // 2

    def kernel(info_ref, attn_ref, weight, *refs):
        mine, theirs, whole = refs[len(after) :]
        step = pl.program_id(0)
        part = jnp.dot(attn_ref[...], weight[...], preferred_element_type=jnp.float32)
        whole[pl.ds(pl.multiple_of(step * block, block), block)] = part.T

        @pl.when(step == steps - 1)
        def _():
            tp = info_ref[1]
            mine[...] = whole[pl.ds(pl.multiple_of(tp * half, 8), half)]
            other = whole[pl.ds(pl.multiple_of((1 - tp) * half, 8), half)]
            theirs[...] = other.astype(theirs.dtype)

    out = [jax.ShapeDtypeStruct((half, rows), d) for d in (jnp.float32, jnp.bfloat16)]
    return pl.pallas_call(
        kernel,
        grid=(steps,),
        in_specs=[SMEM, entire(attn), pl.BlockSpec((depth, block), lambda i: (0, i))]
        + [ANY] * len(after),
        out_specs=[entire(a) for a in out],
        out_shape=out,
        scratch_shapes=[pltpu.VMEM((d_out, rows), jnp.float32)],
        compiler_params=pltpu.CompilerParams(vmem_limit_bytes=32 * 1024 * 1024),
        cost_estimate=pl.CostEstimate(
            flops=2 * attn.size * d_out, bytes_accessed=2 * out_weight.size, transcendentals=0
        ),
    )(info, attn, out_weight, *after)


def grouped(queries, keys, values, out_weight, out_grad, block_doc):
    f32, bf16 = jnp.float32, jnp.bfloat16
    rows = queries.shape[0]
    me, tp = lax.axis_index("ctx"), lax.axis_index("tp")
    r, layer = me % GROUP, me // GROUP
    members = range(GROUP)
    q_width, kv_width = queries.shape[1] // GROUP, keys.shape[1] // GROUP
    kv_heads = kv_width // HEAD
    head_width = q_width // kv_heads
    d_out = out_grad.shape[1]
    doc_padded = jnp.concatenate([jnp.full((GROUP,), -1, jnp.int32), block_doc])
    docs = lax.dynamic_slice_in_dim(doc_padded, layer * GROUP, 2 * GROUP, 0)
    info = jnp.concatenate([jnp.stack([r, tp, layer]).astype(jnp.int32), docs])

    def shape(*dims, dtype=bf16):
        return jax.ShapeDtypeStruct(dims, dtype)

    def traded(blocks):
        return [blocks[0]] + [swapped(blocks[m], "ctx", m) for m in members[1:]]

    kv = traded(pack_kv(keys, values))
    d_attn = project_back(info, out_grad, out_weight)

    def pack_queries(info_ref, ins, outs):
        for m in members:
            outs[m][:, :q_width] = columns(ins[0], (info_ref[0] ^ m) * q_width, q_width)
            outs[m][:, q_width:] = ins[1 + m][...]

    packed = moved(pack_queries, info, [queries, *d_attn], [shape(rows, 2 * q_width)] * GROUP)
    q_and_d = traded(packed)

    def pack_heads(info_ref, ins, outs):
        for m in members:
            for g in range(kv_heads):
                for i in range(2):
                    at = (i * kv_heads + g) * HEAD
                    outs[0][g * GROUP + m, :, i * HEAD : (i + 1) * HEAD] = ins[m][:, at : at + HEAD]

    kv_own = moved(pack_heads, info, kv, [shape(kv_heads * GROUP, rows, 2 * HEAD)], packed)[0]
    kv_far = shifted(kv_own, "ctx", GROUP)

    def pack_half(info_ref, ins, outs):
        outs[0][...] = ins[0][pl.ds(pl.multiple_of(info_ref[1] * (rows // 2), 16), rows // 2), :]

    half = moved(pack_half, info, [out_grad], [shape(rows // 2, d_out)], q_and_d[1:])[0]
    near = traded([half] * GROUP)[1:]

    def pack_near(info_ref, ins, outs):
        for i in range(GROUP - 1):
            outs[0][i * (rows // 2) : (i + 1) * (rows // 2)] = ins[i][...]

    parts, held = [], []
    for g in range(kv_heads):
        parts.append(attention(info, q_and_d, kv_own, kv_far, g, held))
        held = parts[-1][: 2 * GROUP]
    far_grads = [shifted(p[-1], "ctx", -GROUP) for p in parts]
    own_grads = [p[-2] for p in parts]
    attn_cats = [p[-3] for p in parts]
    attn, query_grad = traded(held[:GROUP]), traded(held[GROUP:])
    near_shape = shape((GROUP - 1) * (rows // 2), d_out)
    near = moved(pack_near, info, near, [near_shape], [*attn_cats, far_grads[0]])[0]
    pieces = [out_grad, near, swapped(near, "tp", 1)]
    steps = [1, 2]
    all_terms = [weight_terms(info, pieces, attn_cats[0], steps[0])]
    for g in range(1, kv_heads):
        all_terms.append(weight_terms(info, pieces, attn_cats[g], steps[g], [far_grads[g], all_terms[0][0]]))

    def add_pair(info_ref, ins, outs):
        for i in range(2):
            outs[i][...] = (ins[i][...].astype(f32) + ins[2][i].astype(f32)).astype(outs[i].dtype)

    def add_layers(terms, near, after):
        own, other, away = terms
        met = swapped(away, "ctx", near * GROUP)
        pair_shape = [shape(*own.shape, dtype=f32), shape(*own.shape)]
        own, other = moved(add_pair, info, [own, other, met], pair_shape, after)
        return own, other, swapped(other, "ctx", (3 ^ near) * GROUP)

    def lay_out(info_ref, ins, outs):
        for m in members:
            start = pl.multiple_of((info_ref[0] ^ m) * q_width, HEAD)
            outs[0][:, pl.ds(start, q_width)] = ins[m][...]

    attn = moved(lay_out, info, attn, [shape(rows, GROUP * q_width)], all_terms[-1][:1])[0]
    mine, theirs = project(info, attn, out_weight, [])
    sums, after = [], [theirs]
    for terms, near in zip(all_terms, steps):
        sums.append(add_layers(terms, near, after))
        after = [sums[-1][1]]

    def add_up(info_ref, ins, outs):
        for g in range(kv_heads):
            for m in members:
                for i in range(2):
                    at = (i * kv_heads + g) * HEAD
                    total = ins[g][i, m] + ins[kv_heads + g][i, m].astype(f32)
                    outs[m][:, at : at + HEAD] = total.astype(bf16)

    def lay_out_kv(info_ref, ins, outs):
        for m in members:
            start = pl.multiple_of((info_ref[0] ^ m) * kv_width, HEAD)
            for i in range(2):
                outs[i][:, pl.ds(start, kv_width)] = ins[m][:, i * kv_width : (i + 1) * kv_width]

    total_shape = [shape(rows, 2 * kv_width)] * GROUP
    totals = moved(add_up, info, own_grads + far_grads, total_shape, [*query_grad[1:], sums[0][1]])
    handed = traded(totals)
    key_grad, value_grad = moved(lay_out_kv, info, handed, [shape(rows, GROUP * kv_width)] * 2)

    query_grad = moved(lay_out, info, query_grad, [shape(rows, GROUP * q_width)], totals)[0]

    def add_shares(info_ref, ins, outs):
        outs[0][...] = (ins[0][...] + ins[1][...].astype(f32)).astype(bf16)

    theirs = swapped(theirs, "tp", 1)
    attn_output = moved(add_shares, info, [mine, theirs], [shape(d_out // 2, rows)])[0]

    def lay_out_weight(info_ref, ins, outs):
        for m in members:
            start = pl.multiple_of((info_ref[0] ^ m) * q_width, HEAD)
            outs[0][:, pl.ds(start, q_width)] = ins[m][...].astype(f32)

    blocks = traded(split_sums(info, [(own, met) for own, other, met in sums], handed[1:]))
    grad_shape = [shape(d_out // GROUP // GROUP, GROUP * q_width, dtype=f32)]
    late = []
    out_weight_grad = moved(lay_out_weight, info, blocks, grad_shape, late)[0].T
    return (attn_output.T, query_grad, key_grad, value_grad, out_weight_grad)


def single(queries, keys, values, out_weight, out_grad, block_doc):
    tok_rows = queries.shape[0]
    head_size = HEAD
    kv_count = keys.shape[1] // head_size
    group_size = queries.shape[1] // keys.shape[1]
    key_width = keys.shape[1]
    span_blocks = WINDOW // tok_rows
    reach_blocks = min(span_blocks, lax.axis_size("ctx") - 1)
    own_block = lax.axis_index("ctx")
    paired = jnp.stack([keys, values])
    by_distance = jnp.stack(
        [paired] + [shifted(paired, "ctx", distance) for distance in range(1, reach_blocks + 1)]
    )
    ordered = by_distance[::-1]
    missing = span_blocks - reach_blocks
    window_rows = (span_blocks + 1) * tok_rows
    key_window = ordered[:, 0].reshape(window_rows, kv_count, head_size)
    value_window = ordered[:, 1].reshape(window_rows, kv_count, head_size)
    doc_padded = jnp.concatenate([jnp.full((span_blocks,), -1, jnp.int32), block_doc])
    window_docs = lax.dynamic_slice_in_dim(doc_padded, own_block, span_blocks + 1, 0)
    key_docs = jnp.repeat(window_docs, tok_rows)
    own_doc = lax.dynamic_slice_in_dim(block_doc, own_block, 1, 0)
    rel_key = jnp.arange(window_rows, dtype=jnp.int32)
    rel_query = jnp.arange(tok_rows, dtype=jnp.int32) + span_blocks * tok_rows
    visible = (rel_key[None, :] <= rel_query[:, None]) & (
        rel_key[None, :] > rel_query[:, None] - WINDOW
    )
    visible = visible & (key_docs[None, :] == own_doc[0])
    query_heads = queries.reshape(tok_rows, kv_count, group_size, head_size)
    scores = (
        jnp.einsum("tkgd,skd->kgts", query_heads, key_window, preferred_element_type=jnp.float32)
        * query_scale
    )
    scores = jnp.where(visible[None, None], scores, -jnp.inf)
    top = jnp.max(scores, axis=-1, keepdims=True)
    expo = jnp.exp(scores - top)
    probs = expo / jnp.sum(expo, axis=-1, keepdims=True)
    probs_low = probs.astype(jnp.bfloat16)
    attn_heads = jnp.einsum(
        "kgts,skd->tkgd", probs_low, value_window, preferred_element_type=jnp.float32
    ).astype(jnp.bfloat16)
    attn = attn_heads.reshape(tok_rows, queries.shape[1])
    output_terms = jnp.dot(attn, out_weight, preferred_element_type=jnp.float32)
    attn_output = lax.psum_scatter(output_terms, "tp", scatter_dimension=1, tiled=True).astype(
        jnp.bfloat16
    )
    weight_terms = jnp.einsum("tr,tc->rc", attn, out_grad, preferred_element_type=jnp.float32)
    out_weight_grad = lax.psum_scatter(weight_terms, "ctx", scatter_dimension=1, tiled=True)
    d_attn = jnp.einsum(
        "te,re->tr", out_grad, out_weight, preferred_element_type=jnp.float32
    ).astype(jnp.bfloat16)
    d_attn_heads = d_attn.reshape(tok_rows, kv_count, group_size, head_size)
    d_probs = jnp.einsum(
        "tkgd,skd->kgts", d_attn_heads, value_window, preferred_element_type=jnp.float32
    )
    delta = jnp.einsum(
        "tkgd,tkgd->kgt", attn_heads, d_attn_heads, preferred_element_type=jnp.float32
    )
    d_scores = (probs * (d_probs - delta[..., None])).astype(jnp.bfloat16)
    query_grad = (
        jnp.einsum("kgts,skd->tkgd", d_scores, key_window, preferred_element_type=jnp.float32)
        * query_scale
    ).astype(jnp.bfloat16)
    query_grad = query_grad.reshape(tok_rows, queries.shape[1])
    key_part = (
        jnp.einsum("kgts,tkgd->skd", d_scores, query_heads, preferred_element_type=jnp.float32)
        * query_scale
    )
    value_part = jnp.einsum(
        "kgts,tkgd->skd", probs_low, d_attn_heads, preferred_element_type=jnp.float32
    )
    by_position = jnp.stack(
        [
            key_part.reshape(span_blocks + 1, tok_rows, key_width),
            value_part.reshape(span_blocks + 1, tok_rows, key_width),
        ],
        axis=1,
    )
    terms_near = by_position[::-1]
    total = terms_near[0] + sum(
        [shifted(terms_near[distance], "ctx", -distance) for distance in range(1, reach_blocks + 1)]
    )
    key_grad = total[0].astype(jnp.bfloat16)
    value_grad = total[1].astype(jnp.bfloat16)
    return (attn_output, query_grad, key_grad, value_grad, out_weight_grad)


def local(queries, keys, values, out_weight, out_grad, block_doc):
    fits = (
        lax.axis_size("ctx") == GROUP * GROUP
        and queries.shape[0] * GROUP == WINDOW
        and keys.shape[1] == 2 * GROUP * HEAD
        and lax.axis_size("tp") == 2
    )
    step = grouped if fits else single
    return step(queries, keys, values, out_weight, out_grad, block_doc)


def solution(mesh):
    placed = (P("ctx", "tp"), P("ctx", "tp"), P("ctx", "tp"), P("tp", None), P("ctx", None), P())
    return jax.shard_map(
        local,
        mesh=mesh,
        in_specs=placed,
        out_specs=(P("ctx", "tp"), P("ctx", "tp"), P("ctx", "tp"), P("ctx", "tp"), P("tp", "ctx")),
        check_vma=False,
    )
```

```python
import functools

import jax
import jax.numpy as jnp
from jax import lax
from jax.experimental import pallas as pl
from jax.experimental.pallas import tpu as pltpu
from jax.sharding import PartitionSpec as P

HEAD = 128
WINDOW = 1024
GROUP = 4


query_scale = 168.0 ** (-0.5)
LOG2E = 1.4426950408889634
HIDDEN = -1e30


def shifted(shard, axis, by):
    size = lax.axis_size(axis)
    pairs = [(i, i + by) for i in range(size) if 0 <= i + by < size]
    return lax.ppermute(shard, axis, pairs)


def swapped(shard, axis, by):
    return lax.ppermute(shard, axis, [(i, i ^ by) for i in range(lax.axis_size(axis))])


SMEM = pl.BlockSpec(memory_space=pltpu.SMEM)
ANY = pl.BlockSpec(memory_space=pl.ANY)


def attention_kernel(rows, held, info, *refs):
    q_refs, g_refs = refs[:GROUP], refs[GROUP : 2 * GROUP]
    k_own, v_own, k_far, v_far = refs[2 * GROUP : 2 * GROUP + 4]
    held_refs = refs[2 * GROUP + 4 : 2 * GROUP + 4 + held]
    outs = refs[2 * GROUP + 4 + held :]
    back_refs = outs[: 2 * GROUP]
    attn_cat, kv_own, kv_far = outs[2 * GROUP : 2 * GROUP + 3]
    q_all, g_all, k_all, v_all, k_tr, v_tr, k_acc, v_acc, back = outs[2 * GROUP + 3 :]
    r, tp = info[0], info[1]
    heads = q_refs[0].shape[1] // HEAD
    half = rows // 2
    for m in range(GROUP):
        q_all[m] = q_refs[m][...]
        g_all[m] = g_refs[m][...]
        spot = r ^ m
        for place, k, v in ((spot, k_far, v_far), (spot + GROUP, k_own, v_own)):
            k_all[place] = k[m]
            v_all[place] = v[m]
            k_tr[place] = k[m].T
            v_tr[place] = v[m].T
    k_acc[...] = jnp.zeros_like(k_acc)
    v_acc[...] = jnp.zeros_like(v_acc)
    key_at = lax.broadcasted_iota(jnp.int32, (rows, heads * rows), 0)
    query_at = lax.broadcasted_iota(jnp.int32, (rows, heads * rows), 1) % rows
    far_seen, own_seen = key_at > query_at, key_at <= query_at
    nt = (((1,), (1,)), ((), ()))

    def dot(a, b):
        return jnp.dot(a, b, preferred_element_type=jnp.float32)

    def block(m, carry):
        first = r ^ m
        own_doc = info[3 + first + GROUP]
        q = jnp.concatenate([q_all[m, :, h * HEAD : (h + 1) * HEAD] for h in range(heads)], axis=0)
        g = jnp.concatenate([g_all[m, :, h * HEAD : (h + 1) * HEAD] for h in range(heads)], axis=0)
        scores, hidden = [], []
        for j in range(GROUP + 1):
            s = lax.dot_general(k_all[first + j], q, nt, preferred_element_type=jnp.float32)
            if j == 0:
                s = jnp.where(far_seen, s, HIDDEN)
            if j == GROUP:
                s = jnp.where(own_seen, s, HIDDEN)
            scores.append(s)
            hidden.append(jnp.where(info[3 + first + j] == own_doc, 0.0, HIDDEN))
        tops = [jnp.max(s, axis=0, keepdims=True) + b for s, b in zip(scores, hidden)]
        top = functools.reduce(jnp.maximum, tops) * (query_scale * LOG2E)
        expo = [
            jnp.exp2(s * (query_scale * LOG2E) - (top - b)) for s, b in zip(scores, hidden)
        ]
        whole = functools.reduce(jnp.add, [jnp.sum(e, axis=0, keepdims=True) for e in expo])
        inverse = 1.0 / whole
        probs = [e * inverse for e in expo]
        low = [p.astype(jnp.bfloat16) for p in probs]
        attn_tr = functools.reduce(jnp.add, [dot(v_tr[first + j], low[j]) for j in range(GROUP + 1)])
        attn_tr = attn_tr.astype(jnp.bfloat16).astype(jnp.float32)
        delta = jnp.sum(attn_tr * g.astype(jnp.float32).T, axis=0, keepdims=True)
        dq_tr, d_scores = None, []
        for j in range(GROUP + 1):
            d_p = lax.dot_general(v_all[first + j], g, nt, preferred_element_type=jnp.float32)
            d_s = (probs[j] * (d_p - delta)).astype(jnp.bfloat16)
            term = dot(k_tr[first + j], d_s)
            dq_tr = term if dq_tr is None else dq_tr + term
            d_scores.append(d_s)
        for j in range(GROUP + 1):
            k_acc[first + j] += dot(d_scores[j], q)
            v_acc[first + j] += dot(low[j], g)
        attn = attn_tr.T.astype(jnp.bfloat16)
        dq = (dq_tr * query_scale).T.astype(jnp.bfloat16)
        for h in range(heads):
            back[m, 0, :, h * HEAD : (h + 1) * HEAD] = attn[h * rows : (h + 1) * rows]
            back[m, 1, :, h * HEAD : (h + 1) * HEAD] = dq[h * rows : (h + 1) * rows]
        return carry

    for m in range(GROUP):
        block(m, 0)
    for m in range(GROUP):
        width = back.shape[3]
        for i in range(2):
            out = back_refs[i * GROUP + m]
            at = out.shape[1] - width
            out[:, at:] = back[m, i]
            if held:
                out[:, :at] = held_refs[i * GROUP + m][...]
        spot = r ^ m
        kv_far[0, m] = (k_acc[spot] * query_scale).astype(kv_far.dtype)
        kv_far[1, m] = v_acc[spot].astype(kv_far.dtype)
        kv_own[0, m] = k_acc[spot + GROUP] * query_scale
        kv_own[1, m] = v_acc[spot + GROUP]
    attn_cat[0:rows] = back[0, 0]
    near = pl.multiple_of(tp * half, half)
    away = pl.multiple_of((1 - tp) * half, half)
    for m in range(1, GROUP):
        at = rows + (m - 1) * half
        attn_cat[at : at + half] = back[m, 0, pl.ds(near, half), :]
        at += (GROUP - 1) * half
        attn_cat[at : at + half] = back[m, 0, pl.ds(away, half), :]


def entire(array):
    return pl.BlockSpec(array.shape, lambda i: (0,) * len(array.shape))


def attention(info, q_and_d, kv_own, kv_far, g, kv_heads, held):
    rows, q_block = q_and_d[0].shape[0], q_and_d[0].shape[1] // 2 // kv_heads
    q_spec = pl.BlockSpec((rows, q_block), lambda i: (0, g))
    g_spec = pl.BlockSpec((rows, q_block), lambda i: (0, g + kv_heads))
    k_spec = pl.BlockSpec((GROUP, rows, HEAD), lambda i: (0, 0, 0))
    v_spec = pl.BlockSpec((GROUP, rows, HEAD), lambda i: (0, 0, 1))
    kv_shape = (2, GROUP, rows, HEAD)
    bf16 = jnp.bfloat16
    blocks = 2 * GROUP
    out = [jax.ShapeDtypeStruct((rows, (g + 1) * q_block), bf16)] * (2 * GROUP) + [
        jax.ShapeDtypeStruct((GROUP * rows, q_block), bf16),
        jax.ShapeDtypeStruct(kv_shape, jnp.float32),
        jax.ShapeDtypeStruct(kv_shape, bf16),
    ]
    return pl.pallas_call(
        functools.partial(attention_kernel, rows, len(held)),
        grid=(1,),
        in_specs=[SMEM]
        + [q_spec] * GROUP
        + [g_spec] * GROUP
        + [k_spec, v_spec, k_spec, v_spec]
        + [entire(a) for a in held],
        out_specs=[entire(a) for a in out],
        out_shape=out,
        scratch_shapes=[
            pltpu.VMEM((GROUP, rows, q_block), bf16),
            pltpu.VMEM((GROUP, rows, q_block), bf16),
            pltpu.VMEM((blocks, rows, HEAD), bf16),
            pltpu.VMEM((blocks, rows, HEAD), bf16),
            pltpu.VMEM((blocks, HEAD, rows), bf16),
            pltpu.VMEM((blocks, HEAD, rows), bf16),
            pltpu.VMEM((blocks, rows, HEAD), jnp.float32),
            pltpu.VMEM((blocks, rows, HEAD), jnp.float32),
            pltpu.VMEM((GROUP, 2, rows, q_block), bf16),
        ],
        compiler_params=pltpu.CompilerParams(vmem_limit_bytes=32 * 1024 * 1024),
        cost_estimate=pl.CostEstimate(
            flops=12 * q_block * GROUP * rows * (GROUP + 1) * rows,
            bytes_accessed=5 * 1024 * 1024,
            transcendentals=0,
        ),
    )(info, *q_and_d, *q_and_d, kv_own, kv_own, kv_far, kv_far, *held)


def moved(body, info, arrays, out, after=()):
    n = len(arrays)

    def kernel(info_ref, *refs):
        body(info_ref, refs[:n], refs[n + len(after) :])

    size = sum(a.size * a.dtype.itemsize for a in list(arrays) + list(out))
    return pl.pallas_call(
        kernel,
        grid=(1,),
        in_specs=[SMEM] + [entire(a) for a in arrays] + [ANY] * len(after),
        out_specs=[entire(a) for a in out],
        out_shape=list(out),
        compiler_params=pltpu.CompilerParams(vmem_limit_bytes=32 * 1024 * 1024),
        cost_estimate=pl.CostEstimate(flops=0, bytes_accessed=size, transcendentals=0),
    )(info, *arrays, *after)


def columns(ref, start, width):
    return ref[:, pl.ds(pl.multiple_of(start, HEAD), width)]


def pack_kv(keys, values):
    rows, width = keys.shape[0], keys.shape[1] // GROUP

    def kernel(k_ref, v_ref, *refs):
        outs, sems = refs[:GROUP], refs[GROUP]
        r = lax.axis_index("ctx") % GROUP
        copies = []
        for m in range(GROUP):
            for i, ref in enumerate((k_ref, v_ref)):
                start = pl.multiple_of((r ^ m) * width, HEAD)
                copies.append(
                    pltpu.make_async_copy(
                        ref.at[:, pl.ds(start, width)],
                        outs[m].at[:, i * width : (i + 1) * width],
                        sems.at[2 * m + i],
                    )
                )
        for copy in copies:
            copy.start()
        for copy in copies:
            copy.wait()

    out = [jax.ShapeDtypeStruct((rows, 2 * width), keys.dtype)] * GROUP
    return pl.pallas_call(
        kernel,
        in_specs=[ANY, ANY],
        out_specs=[pl.BlockSpec(memory_space=pltpu.VMEM)] * GROUP,
        out_shape=out,
        scratch_shapes=[pltpu.SemaphoreType.DMA((2 * GROUP,))],
        compiler_params=pltpu.CompilerParams(vmem_limit_bytes=32 * 1024 * 1024),
        cost_estimate=pl.CostEstimate(
            flops=0, bytes_accessed=4 * keys.size, transcendentals=0
        ),
    )(keys, values)


def project_back(info, out_grad, out_weight):
    rows, d_out = out_grad.shape
    steps = GROUP
    block = out_weight.shape[0] // steps

    def kernel(info_ref, grad, weight, *outs):
        step = pl.program_id(0)
        part = lax.dot_general(
            grad[...], weight[...], (((1,), (1,)), ((), ())), preferred_element_type=jnp.float32
        ).astype(jnp.bfloat16)
        for at in range(steps):

            @pl.when(step == at)
            def _():
                outs[at][...] = part

    def weight_block(step, info_ref):
        return (info_ref[0] ^ step, 0)

    return pl.pallas_call(
        kernel,
        grid_spec=pltpu.PrefetchScalarGridSpec(
            num_scalar_prefetch=1,
            grid=(steps,),
            in_specs=[
                pl.BlockSpec((rows, d_out), lambda i, info_ref: (0, 0)),
                pl.BlockSpec((block, d_out), weight_block),
            ],
            out_specs=[pl.BlockSpec((rows, block), lambda i, info_ref: (0, 0))] * steps,
        ),
        out_shape=[jax.ShapeDtypeStruct((rows, block), jnp.bfloat16)] * steps,
        compiler_params=pltpu.CompilerParams(vmem_limit_bytes=32 * 1024 * 1024),
        cost_estimate=pl.CostEstimate(
            flops=2 * rows * out_weight.size, bytes_accessed=2 * out_weight.size, transcendentals=0
        ),
    )(info, out_grad, out_weight)

def weight_terms(info, pieces, attn_cat, near, after=()):
    d_out, width = pieces[0].shape[1], attn_cat.shape[1]
    block = 3 * HEAD if d_out % (3 * HEAD) == 0 else d_out
    steps, cut = d_out // block, d_out // GROUP

    def kernel(info_ref, *refs):
        inputs, attn = refs[: len(pieces)], refs[len(pieces)]
        own, other, away, whole = refs[len(pieces) + 1 + len(after) :]
        total, at = None, 0
        for piece in inputs:
            rows = piece.shape[0]
            term = lax.dot_general(
                piece[...],
                attn[at : at + rows],
                (((0,), (0,)), ((), ())),
                preferred_element_type=jnp.float32,
            )
            total, at = term if total is None else total + term, at + rows
        step = pl.program_id(0)
        whole[pl.ds(pl.multiple_of(step * block, block), block)] = total.astype(whole.dtype)

        @pl.when(step == steps - 1)
        def _():
            def chunk(m):
                return whole[pl.ds(pl.multiple_of((info_ref[2] ^ m) * cut, 16), cut)]

            own[...] = chunk(0)
            other[...] = chunk(3 ^ near)
            away[0] = chunk(near)
            away[1] = chunk(3)

    shapes = [(cut, width), (cut, width), (2, cut, width)]
    out = [jax.ShapeDtypeStruct(s, jnp.bfloat16) for s in shapes]
    return pl.pallas_call(
        kernel,
        grid=(steps,),
        in_specs=[SMEM]
        + [pl.BlockSpec((p.shape[0], block), lambda i: (0, i)) for p in pieces]
        + [entire(attn_cat)]
        + [ANY] * len(after),
        out_specs=[entire(a) for a in out],
        out_shape=out,
        scratch_shapes=[pltpu.VMEM((d_out, width), jnp.bfloat16)],
        compiler_params=pltpu.CompilerParams(vmem_limit_bytes=32 * 1024 * 1024),
        cost_estimate=pl.CostEstimate(
            flops=2 * attn_cat.size * d_out,
            bytes_accessed=2 * (attn_cat.shape[0] + width) * d_out,
            transcendentals=0,
        ),
    )(info, *pieces, attn_cat, *after)


def split_sums(info, pairs, after):
    rows, width = pairs[0][0].shape
    cut, count = rows // GROUP, len(pairs)

    def kernel(info_ref, *refs):
        outs, total = refs[-1 - GROUP : -1], refs[-1]
        for g in range(count):
            total[...] = refs[2 * g][...].astype(jnp.float32) + refs[2 * g + 1][...].astype(jnp.float32)
            for m in range(GROUP):
                start = pl.multiple_of((info_ref[0] ^ m) * cut, 8)
                block = total[pl.ds(start, cut)].astype(outs[m].dtype)
                outs[m][:, g * width : (g + 1) * width] = block

    flat = [a for pair in pairs for a in pair]
    out = [jax.ShapeDtypeStruct((cut, count * width), jnp.bfloat16)] * GROUP
    return pl.pallas_call(
        kernel,
        grid=(1,),
        in_specs=[SMEM] + [entire(a) for a in flat] + [ANY] * len(after),
        out_specs=[entire(a) for a in out],
        out_shape=out,
        scratch_shapes=[pltpu.VMEM((rows, width), jnp.float32)],
        compiler_params=pltpu.CompilerParams(vmem_limit_bytes=32 * 1024 * 1024),
    )(info, *flat, *after)


def project(info, attn, out_weight, after):
    rows, depth = attn.shape
    d_out = out_weight.shape[1]
    block = 3 * HEAD if d_out % (3 * HEAD) == 0 else d_out
    steps, half = d_out // block, d_out // 2

    def kernel(info_ref, attn_ref, weight, *refs):
        mine, theirs, whole = refs[len(after) :]
        step = pl.program_id(0)
        part = jnp.dot(attn_ref[...], weight[...], preferred_element_type=jnp.float32)
        whole[pl.ds(pl.multiple_of(step * block, block), block)] = part.T

        @pl.when(step == steps - 1)
        def _():
            tp = info_ref[1]
            mine[...] = whole[pl.ds(pl.multiple_of(tp * half, 8), half)]
            other = whole[pl.ds(pl.multiple_of((1 - tp) * half, 8), half)]
            theirs[...] = other.astype(theirs.dtype)

    out = [jax.ShapeDtypeStruct((half, rows), d) for d in (jnp.float32, jnp.bfloat16)]
    return pl.pallas_call(
        kernel,
        grid=(steps,),
        in_specs=[SMEM, entire(attn), pl.BlockSpec((depth, block), lambda i: (0, i))]
        + [ANY] * len(after),
        out_specs=[entire(a) for a in out],
        out_shape=out,
        scratch_shapes=[pltpu.VMEM((d_out, rows), jnp.float32)],
        compiler_params=pltpu.CompilerParams(vmem_limit_bytes=32 * 1024 * 1024),
        cost_estimate=pl.CostEstimate(
            flops=2 * attn.size * d_out, bytes_accessed=2 * out_weight.size, transcendentals=0
        ),
    )(info, attn, out_weight, *after)


def grouped(queries, keys, values, out_weight, out_grad, block_doc):
    f32, bf16 = jnp.float32, jnp.bfloat16
    rows = queries.shape[0]
    me, tp = lax.axis_index("ctx"), lax.axis_index("tp")
    r, layer = me % GROUP, me // GROUP
    members = range(GROUP)
    q_width, kv_width = queries.shape[1] // GROUP, keys.shape[1] // GROUP
    kv_heads = kv_width // HEAD
    head_width = q_width // kv_heads
    d_out = out_grad.shape[1]
    doc_padded = jnp.concatenate([jnp.full((GROUP,), -1, jnp.int32), block_doc])
    docs = lax.dynamic_slice_in_dim(doc_padded, layer * GROUP, 2 * GROUP, 0)
    info = jnp.concatenate([jnp.stack([r, tp, layer]).astype(jnp.int32), docs])

    def shape(*dims, dtype=bf16):
        return jax.ShapeDtypeStruct(dims, dtype)

    def traded(blocks):
        return [blocks[0]] + [swapped(blocks[m], "ctx", m) for m in members[1:]]

    kv = traded(pack_kv(keys, values))
    d_attn = project_back(info, out_grad, out_weight)

    def pack_queries(info_ref, ins, outs):
        for m in members:
            outs[m][:, :q_width] = columns(ins[0], (info_ref[0] ^ m) * q_width, q_width)
            outs[m][:, q_width:] = ins[1 + m][...]

    packed = moved(pack_queries, info, [queries, *d_attn], [shape(rows, 2 * q_width)] * GROUP)
    q_and_d = traded(packed)

    def pack_heads(info_ref, ins, outs):
        for m in members:
            for g in range(kv_heads):
                for i in range(2):
                    at = (i * kv_heads + g) * HEAD
                    outs[g][m, :, i * HEAD : (i + 1) * HEAD] = ins[m][:, at : at + HEAD]

    kv_own = moved(pack_heads, info, kv, [shape(GROUP, rows, 2 * HEAD)] * kv_heads, packed)
    kv_far = [shifted(a, "ctx", GROUP) for a in kv_own]

    def pack_half(info_ref, ins, outs):
        outs[0][...] = ins[0][pl.ds(pl.multiple_of(info_ref[1] * (rows // 2), 16), rows // 2), :]

    half = moved(pack_half, info, [out_grad], [shape(rows // 2, d_out)], q_and_d[1:])[0]
    near = traded([half] * GROUP)[1:]

    def pack_near(info_ref, ins, outs):
        for i in range(GROUP - 1):
            outs[0][i * (rows // 2) : (i + 1) * (rows // 2)] = ins[i][...]

    parts, held = [], []
    for g in range(kv_heads):
        parts.append(attention(info, q_and_d, kv_own[g], kv_far[g], g, kv_heads, held))
        held = parts[-1][: 2 * GROUP]
    far_grads = [shifted(p[-1], "ctx", -GROUP) for p in parts]
    own_grads = [p[-2] for p in parts]
    attn_cats = [p[-3] for p in parts]
    attn, query_grad = traded(held[:GROUP]), traded(held[GROUP:])
    near_shape = shape((GROUP - 1) * (rows // 2), d_out)
    near = moved(pack_near, info, near, [near_shape], [*attn_cats, far_grads[0]])[0]
    pieces = [out_grad, near, swapped(near, "tp", 1)]
    steps = [1, 2]
    all_terms = [weight_terms(info, pieces, attn_cats[0], steps[0])]
    for g in range(1, kv_heads):
        all_terms.append(weight_terms(info, pieces, attn_cats[g], steps[g], [far_grads[g], all_terms[0][0]]))

    def add_pair(info_ref, ins, outs):
        for i in range(2):
            outs[i][...] = (ins[i][...].astype(f32) + ins[2][i].astype(f32)).astype(outs[i].dtype)

    def add_layers(terms, near, after):
        own, other, away = terms
        met = swapped(away, "ctx", near * GROUP)
        pair_shape = [shape(*own.shape, dtype=f32), shape(*own.shape)]
        own, other = moved(add_pair, info, [own, other, met], pair_shape, after)
        return own, other, swapped(other, "ctx", (3 ^ near) * GROUP)

    def lay_out(info_ref, ins, outs):
        for m in members:
            start = pl.multiple_of((info_ref[0] ^ m) * q_width, HEAD)
            outs[0][:, pl.ds(start, q_width)] = ins[m][...]

    attn = moved(lay_out, info, attn, [shape(rows, GROUP * q_width)], all_terms[-1][:1])[0]
    mine, theirs = project(info, attn, out_weight, [])
    sums, after = [], [theirs]
    for terms, near in zip(all_terms, steps):
        sums.append(add_layers(terms, near, after))
        after = [sums[-1][1]]

    def add_up(info_ref, ins, outs):
        for g in range(kv_heads):
            for m in members:
                for i in range(2):
                    at = (i * kv_heads + g) * HEAD
                    total = ins[g][i, m] + ins[kv_heads + g][i, m].astype(f32)
                    outs[m][:, at : at + HEAD] = total.astype(bf16)

    def lay_out_kv(info_ref, ins, outs):
        for m in members:
            start = pl.multiple_of((info_ref[0] ^ m) * kv_width, HEAD)
            for i in range(2):
                outs[i][:, pl.ds(start, kv_width)] = ins[m][:, i * kv_width : (i + 1) * kv_width]

    total_shape = [shape(rows, 2 * kv_width)] * GROUP
    totals = moved(add_up, info, own_grads + far_grads, total_shape, [*query_grad[1:], sums[0][1]])
    handed = traded(totals)
    key_grad, value_grad = moved(lay_out_kv, info, handed, [shape(rows, GROUP * kv_width)] * 2)

    query_grad = moved(lay_out, info, query_grad, [shape(rows, GROUP * q_width)], totals)[0]

    def add_shares(info_ref, ins, outs):
        outs[0][...] = (ins[0][...] + ins[1][...].astype(f32)).astype(bf16)

    theirs = swapped(theirs, "tp", 1)
    attn_output = moved(add_shares, info, [mine, theirs], [shape(d_out // 2, rows)])[0]

    def lay_out_weight(info_ref, ins, outs):
        for m in members:
            start = pl.multiple_of((info_ref[0] ^ m) * q_width, HEAD)
            outs[0][:, pl.ds(start, q_width)] = ins[m][...].astype(f32)

    blocks = traded(split_sums(info, [(own, met) for own, other, met in sums], handed[1:]))
    grad_shape = [shape(d_out // GROUP // GROUP, GROUP * q_width, dtype=f32)]
    late = []
    out_weight_grad = moved(lay_out_weight, info, blocks, grad_shape, late)[0].T
    return (attn_output.T, query_grad, key_grad, value_grad, out_weight_grad)


def single(queries, keys, values, out_weight, out_grad, block_doc):
    tok_rows = queries.shape[0]
    head_size = HEAD
    kv_count = keys.shape[1] // head_size
    group_size = queries.shape[1] // keys.shape[1]
    key_width = keys.shape[1]
    span_blocks = WINDOW // tok_rows
    reach_blocks = min(span_blocks, lax.axis_size("ctx") - 1)
    own_block = lax.axis_index("ctx")
    paired = jnp.stack([keys, values])
    by_distance = jnp.stack(
        [paired] + [shifted(paired, "ctx", distance) for distance in range(1, reach_blocks + 1)]
    )
    ordered = by_distance[::-1]
    missing = span_blocks - reach_blocks
    window_rows = (span_blocks + 1) * tok_rows
    key_window = ordered[:, 0].reshape(window_rows, kv_count, head_size)
    value_window = ordered[:, 1].reshape(window_rows, kv_count, head_size)
    doc_padded = jnp.concatenate([jnp.full((span_blocks,), -1, jnp.int32), block_doc])
    window_docs = lax.dynamic_slice_in_dim(doc_padded, own_block, span_blocks + 1, 0)
    key_docs = jnp.repeat(window_docs, tok_rows)
    own_doc = lax.dynamic_slice_in_dim(block_doc, own_block, 1, 0)
    rel_key = jnp.arange(window_rows, dtype=jnp.int32)
    rel_query = jnp.arange(tok_rows, dtype=jnp.int32) + span_blocks * tok_rows
    visible = (rel_key[None, :] <= rel_query[:, None]) & (
        rel_key[None, :] > rel_query[:, None] - WINDOW
    )
    visible = visible & (key_docs[None, :] == own_doc[0])
    query_heads = queries.reshape(tok_rows, kv_count, group_size, head_size)
    scores = (
        jnp.einsum("tkgd,skd->kgts", query_heads, key_window, preferred_element_type=jnp.float32)
        * query_scale
    )
    scores = jnp.where(visible[None, None], scores, -jnp.inf)
    top = jnp.max(scores, axis=-1, keepdims=True)
    expo = jnp.exp(scores - top)
    probs = expo / jnp.sum(expo, axis=-1, keepdims=True)
    probs_low = probs.astype(jnp.bfloat16)
    attn_heads = jnp.einsum(
        "kgts,skd->tkgd", probs_low, value_window, preferred_element_type=jnp.float32
    ).astype(jnp.bfloat16)
    attn = attn_heads.reshape(tok_rows, queries.shape[1])
    output_terms = jnp.dot(attn, out_weight, preferred_element_type=jnp.float32)
    attn_output = lax.psum_scatter(output_terms, "tp", scatter_dimension=1, tiled=True).astype(
        jnp.bfloat16
    )
    weight_terms = jnp.einsum("tr,tc->rc", attn, out_grad, preferred_element_type=jnp.float32)
    out_weight_grad = lax.psum_scatter(weight_terms, "ctx", scatter_dimension=1, tiled=True)
    d_attn = jnp.einsum(
        "te,re->tr", out_grad, out_weight, preferred_element_type=jnp.float32
    ).astype(jnp.bfloat16)
    d_attn_heads = d_attn.reshape(tok_rows, kv_count, group_size, head_size)
    d_probs = jnp.einsum(
        "tkgd,skd->kgts", d_attn_heads, value_window, preferred_element_type=jnp.float32
    )
    delta = jnp.einsum(
        "tkgd,tkgd->kgt", attn_heads, d_attn_heads, preferred_element_type=jnp.float32
    )
    d_scores = (probs * (d_probs - delta[..., None])).astype(jnp.bfloat16)
    query_grad = (
        jnp.einsum("kgts,skd->tkgd", d_scores, key_window, preferred_element_type=jnp.float32)
        * query_scale
    ).astype(jnp.bfloat16)
    query_grad = query_grad.reshape(tok_rows, queries.shape[1])
    key_part = (
        jnp.einsum("kgts,tkgd->skd", d_scores, query_heads, preferred_element_type=jnp.float32)
        * query_scale
    )
    value_part = jnp.einsum(
        "kgts,tkgd->skd", probs_low, d_attn_heads, preferred_element_type=jnp.float32
    )
    by_position = jnp.stack(
        [
            key_part.reshape(span_blocks + 1, tok_rows, key_width),
            value_part.reshape(span_blocks + 1, tok_rows, key_width),
        ],
        axis=1,
    )
    terms_near = by_position[::-1]
    total = terms_near[0] + sum(
        [shifted(terms_near[distance], "ctx", -distance) for distance in range(1, reach_blocks + 1)]
    )
    key_grad = total[0].astype(jnp.bfloat16)
    value_grad = total[1].astype(jnp.bfloat16)
    return (attn_output, query_grad, key_grad, value_grad, out_weight_grad)


def local(queries, keys, values, out_weight, out_grad, block_doc):
    fits = (
        lax.axis_size("ctx") == GROUP * GROUP
        and queries.shape[0] * GROUP == WINDOW
        and keys.shape[1] == 2 * GROUP * HEAD
        and lax.axis_size("tp") == 2
    )
    step = grouped if fits else single
    return step(queries, keys, values, out_weight, out_grad, block_doc)


def solution(mesh):
    placed = (P("ctx", "tp"), P("ctx", "tp"), P("ctx", "tp"), P("tp", None), P("ctx", None), P())
    return jax.shard_map(
        local,
        mesh=mesh,
        in_specs=placed,
        out_specs=(P("ctx", "tp"), P("ctx", "tp"), P("ctx", "tp"), P("ctx", "tp"), P("tp", "ctx")),
        check_vma=False,
    )
```

```python
import functools

import jax
import jax.numpy as jnp
from jax import lax
from jax.experimental import pallas as pl
from jax.experimental.pallas import tpu as pltpu
from jax.sharding import PartitionSpec as P

HEAD = 128
WINDOW = 1024
GROUP = 4


query_scale = 168.0 ** (-0.5)
LOG2E = 1.4426950408889634
HIDDEN = -1e30


def shifted(shard, axis, by):
    size = lax.axis_size(axis)
    pairs = [(i, i + by) for i in range(size) if 0 <= i + by < size]
    return lax.ppermute(shard, axis, pairs)


def swapped(shard, axis, by):
    return lax.ppermute(shard, axis, [(i, i ^ by) for i in range(lax.axis_size(axis))])


SMEM = pl.BlockSpec(memory_space=pltpu.SMEM)
ANY = pl.BlockSpec(memory_space=pl.ANY)


def attention_kernel(rows, held, info, *refs):
    q_refs, g_refs = refs[:GROUP], refs[GROUP : 2 * GROUP]
    k_own, v_own, k_far, v_far = refs[2 * GROUP : 2 * GROUP + 4]
    held_refs = refs[2 * GROUP + 4 : 2 * GROUP + 4 + held]
    outs = refs[2 * GROUP + 4 + held :]
    back_refs = outs[: 2 * GROUP]
    attn_cat, kv_own, kv_far = outs[2 * GROUP : 2 * GROUP + 3]
    q_all, g_all, k_all, v_all, k_tr, v_tr, k_acc, v_acc, back = outs[2 * GROUP + 3 :]
    r, tp = info[0], info[1]
    heads = q_refs[0].shape[1] // HEAD
    half = rows // 2
    for m in range(GROUP):
        q_all[m] = q_refs[m][...]
        g_all[m] = g_refs[m][...]
        spot = r ^ m
        for place, k, v in ((spot, k_far, v_far), (spot + GROUP, k_own, v_own)):
            k_all[place] = k[m]
            v_all[place] = v[m]
            k_tr[place] = k[m].T
            v_tr[place] = v[m].T
    k_acc[...] = jnp.zeros_like(k_acc)
    v_acc[...] = jnp.zeros_like(v_acc)
    key_at = lax.broadcasted_iota(jnp.int32, (rows, heads * rows), 0)
    query_at = lax.broadcasted_iota(jnp.int32, (rows, heads * rows), 1) % rows
    far_seen, own_seen = key_at > query_at, key_at <= query_at
    nt = (((1,), (1,)), ((), ()))

    def dot(a, b):
        return jnp.dot(a, b, preferred_element_type=jnp.float32)

    def block(m, carry):
        first = r ^ m
        own_doc = info[3 + first + GROUP]
        q = jnp.concatenate([q_all[m, :, h * HEAD : (h + 1) * HEAD] for h in range(heads)], axis=0)
        g = jnp.concatenate([g_all[m, :, h * HEAD : (h + 1) * HEAD] for h in range(heads)], axis=0)
        scores, hidden = [], []
        for j in range(GROUP + 1):
            s = lax.dot_general(k_all[first + j], q, nt, preferred_element_type=jnp.float32)
            if j == 0:
                s = jnp.where(far_seen, s, HIDDEN)
            if j == GROUP:
                s = jnp.where(own_seen, s, HIDDEN)
            scores.append(s)
            hidden.append(jnp.where(info[3 + first + j] == own_doc, 0.0, HIDDEN))
        tops = [jnp.max(s, axis=0, keepdims=True) + b for s, b in zip(scores, hidden)]
        top = functools.reduce(jnp.maximum, tops) * (query_scale * LOG2E)
        expo = [
            jnp.exp2(s * (query_scale * LOG2E) - (top - b)) for s, b in zip(scores, hidden)
        ]
        whole = functools.reduce(jnp.add, [jnp.sum(e, axis=0, keepdims=True) for e in expo])
        inverse = 1.0 / whole
        probs = [e * inverse for e in expo]
        low = [p.astype(jnp.bfloat16) for p in probs]
        attn_tr = functools.reduce(jnp.add, [dot(v_tr[first + j], low[j]) for j in range(GROUP + 1)])
        attn_tr = attn_tr.astype(jnp.bfloat16).astype(jnp.float32)
        delta = jnp.sum(attn_tr * g.astype(jnp.float32).T, axis=0, keepdims=True)
        dq_tr, d_scores = None, []
        for j in range(GROUP + 1):
            d_p = lax.dot_general(v_all[first + j], g, nt, preferred_element_type=jnp.float32)
            d_s = (probs[j] * (d_p - delta)).astype(jnp.bfloat16)
            term = dot(k_tr[first + j], d_s)
            dq_tr = term if dq_tr is None else dq_tr + term
            d_scores.append(d_s)
        for j in range(GROUP + 1):
            k_acc[first + j] += dot(d_scores[j], q)
            v_acc[first + j] += dot(low[j], g)
        attn = attn_tr.T.astype(jnp.bfloat16)
        dq = (dq_tr * query_scale).T.astype(jnp.bfloat16)
        for h in range(heads):
            back[m, 0, :, h * HEAD : (h + 1) * HEAD] = attn[h * rows : (h + 1) * rows]
            back[m, 1, :, h * HEAD : (h + 1) * HEAD] = dq[h * rows : (h + 1) * rows]
        return carry

    for m in range(GROUP):
        block(m, 0)
    for m in range(GROUP):
        width = back.shape[3]
        for i in range(2):
            out = back_refs[i * GROUP + m]
            at = out.shape[1] - width
            out[:, at:] = back[m, i]
            if held:
                out[:, :at] = held_refs[i * GROUP + m][...]
        spot = r ^ m
        kv_far[0, m] = (k_acc[spot] * query_scale).astype(kv_far.dtype)
        kv_far[1, m] = v_acc[spot].astype(kv_far.dtype)
        kv_own[0, m] = k_acc[spot + GROUP] * query_scale
        kv_own[1, m] = v_acc[spot + GROUP]
    attn_cat[0:rows] = back[0, 0]
    near = pl.multiple_of(tp * half, half)
    away = pl.multiple_of((1 - tp) * half, half)
    for m in range(1, GROUP):
        at = rows + (m - 1) * half
        attn_cat[at : at + half] = back[m, 0, pl.ds(near, half), :]
        at += (GROUP - 1) * half
        attn_cat[at : at + half] = back[m, 0, pl.ds(away, half), :]


def entire(array):
    return pl.BlockSpec(array.shape, lambda i: (0,) * len(array.shape))


def attention(info, q_and_d, kv_own, kv_far, g, kv_heads, held):
    rows, q_block = q_and_d[0].shape[0], q_and_d[0].shape[1] // 2 // kv_heads
    q_spec = pl.BlockSpec((rows, q_block), lambda i: (0, g))
    g_spec = pl.BlockSpec((rows, q_block), lambda i: (0, g + kv_heads))
    k_spec = pl.BlockSpec((GROUP, rows, HEAD), lambda i: (0, 0, 0))
    v_spec = pl.BlockSpec((GROUP, rows, HEAD), lambda i: (0, 0, 1))
    kv_shape = (2, GROUP, rows, HEAD)
    bf16 = jnp.bfloat16
    blocks = 2 * GROUP
    out = [jax.ShapeDtypeStruct((rows, (g + 1) * q_block), bf16)] * (2 * GROUP) + [
        jax.ShapeDtypeStruct((GROUP * rows, q_block), bf16),
        jax.ShapeDtypeStruct(kv_shape, jnp.float32),
        jax.ShapeDtypeStruct(kv_shape, bf16),
    ]
    return pl.pallas_call(
        functools.partial(attention_kernel, rows, len(held)),
        grid=(1,),
        in_specs=[SMEM]
        + [q_spec] * GROUP
        + [g_spec] * GROUP
        + [k_spec, v_spec, k_spec, v_spec]
        + [entire(a) for a in held],
        out_specs=[entire(a) for a in out],
        out_shape=out,
        scratch_shapes=[
            pltpu.VMEM((GROUP, rows, q_block), bf16),
            pltpu.VMEM((GROUP, rows, q_block), bf16),
            pltpu.VMEM((blocks, rows, HEAD), bf16),
            pltpu.VMEM((blocks, rows, HEAD), bf16),
            pltpu.VMEM((blocks, HEAD, rows), bf16),
            pltpu.VMEM((blocks, HEAD, rows), bf16),
            pltpu.VMEM((blocks, rows, HEAD), jnp.float32),
            pltpu.VMEM((blocks, rows, HEAD), jnp.float32),
            pltpu.VMEM((GROUP, 2, rows, q_block), bf16),
        ],
        compiler_params=pltpu.CompilerParams(vmem_limit_bytes=32 * 1024 * 1024),
        cost_estimate=pl.CostEstimate(
            flops=12 * q_block * GROUP * rows * (GROUP + 1) * rows,
            bytes_accessed=5 * 1024 * 1024,
            transcendentals=0,
        ),
    )(info, *q_and_d, *q_and_d, kv_own, kv_own, kv_far, kv_far, *held)


def moved(body, info, arrays, out, after=()):
    n = len(arrays)

    def kernel(info_ref, *refs):
        body(info_ref, refs[:n], refs[n + len(after) :])

    size = sum(a.size * a.dtype.itemsize for a in list(arrays) + list(out))
    return pl.pallas_call(
        kernel,
        grid=(1,),
        in_specs=[SMEM] + [entire(a) for a in arrays] + [ANY] * len(after),
        out_specs=[entire(a) for a in out],
        out_shape=list(out),
        compiler_params=pltpu.CompilerParams(vmem_limit_bytes=32 * 1024 * 1024),
        cost_estimate=pl.CostEstimate(flops=0, bytes_accessed=size, transcendentals=0),
    )(info, *arrays, *after)


def columns(ref, start, width):
    return ref[:, pl.ds(pl.multiple_of(start, HEAD), width)]


def pack_kv(keys, values):
    rows, width = keys.shape[0], keys.shape[1] // GROUP

    def kernel(k_ref, v_ref, *refs):
        outs, sems = refs[:GROUP], refs[GROUP]
        r = lax.axis_index("ctx") % GROUP
        copies = []
        for m in range(GROUP):
            for i, ref in enumerate((k_ref, v_ref)):
                start = pl.multiple_of((r ^ m) * width, HEAD)
                copies.append(
                    pltpu.make_async_copy(
                        ref.at[:, pl.ds(start, width)],
                        outs[m].at[:, i * width : (i + 1) * width],
                        sems.at[2 * m + i],
                    )
                )
        for copy in copies:
            copy.start()
        for copy in copies:
            copy.wait()

    out = [jax.ShapeDtypeStruct((rows, 2 * width), keys.dtype)] * GROUP
    return pl.pallas_call(
        kernel,
        in_specs=[ANY, ANY],
        out_specs=[pl.BlockSpec(memory_space=pltpu.VMEM)] * GROUP,
        out_shape=out,
        scratch_shapes=[pltpu.SemaphoreType.DMA((2 * GROUP,))],
        compiler_params=pltpu.CompilerParams(vmem_limit_bytes=32 * 1024 * 1024),
        cost_estimate=pl.CostEstimate(
            flops=0, bytes_accessed=4 * keys.size, transcendentals=0
        ),
    )(keys, values)


def project_back(info, out_grad, out_weight):
    rows, d_out = out_grad.shape
    steps = GROUP
    block = out_weight.shape[0] // steps

    def kernel(info_ref, grad, weight, *outs):
        step = pl.program_id(0)
        part = lax.dot_general(
            grad[...], weight[...], (((1,), (1,)), ((), ())), preferred_element_type=jnp.float32
        ).astype(jnp.bfloat16)
        for at in range(steps):

            @pl.when(step == at)
            def _():
                outs[at][...] = part

    def weight_block(step, info_ref):
        return (info_ref[0] ^ step, 0)

    return pl.pallas_call(
        kernel,
        grid_spec=pltpu.PrefetchScalarGridSpec(
            num_scalar_prefetch=1,
            grid=(steps,),
            in_specs=[
                pl.BlockSpec((rows, d_out), lambda i, info_ref: (0, 0)),
                pl.BlockSpec((block, d_out), weight_block),
            ],
            out_specs=[pl.BlockSpec((rows, block), lambda i, info_ref: (0, 0))] * steps,
        ),
        out_shape=[jax.ShapeDtypeStruct((rows, block), jnp.bfloat16)] * steps,
        compiler_params=pltpu.CompilerParams(vmem_limit_bytes=32 * 1024 * 1024),
        cost_estimate=pl.CostEstimate(
            flops=2 * rows * out_weight.size, bytes_accessed=2 * out_weight.size, transcendentals=0
        ),
    )(info, out_grad, out_weight)

def early_terms(pieces, attn_cat):
    d_out, width = pieces[0].shape[1], attn_cat.shape[1]
    block = 3 * HEAD if d_out % (3 * HEAD) == 0 else d_out

    def kernel(*refs):
        attn, out = refs[-2:]
        total, at = None, 0
        for piece in refs[:-2]:
            rows = piece.shape[0]
            term = lax.dot_general(
                piece[...],
                attn[at : at + rows],
                (((0,), (0,)), ((), ())),
                preferred_element_type=jnp.float32,
            )
            total, at = term if total is None else total + term, at + rows
        out[...] = total

    return pl.pallas_call(
        kernel,
        grid=(d_out // block,),
        in_specs=[pl.BlockSpec((p.shape[0], block), lambda i: (0, i)) for p in pieces]
        + [entire(attn_cat)],
        out_specs=pl.BlockSpec((block, width), lambda i: (i, 0)),
        out_shape=jax.ShapeDtypeStruct((d_out, width), jnp.float32),
        compiler_params=pltpu.CompilerParams(vmem_limit_bytes=32 * 1024 * 1024),
        cost_estimate=pl.CostEstimate(
            flops=2 * sum(p.shape[0] for p in pieces) * width * d_out,
            bytes_accessed=2 * (attn_cat.shape[0] + 2 * width) * d_out,
            transcendentals=0,
        ),
    )(*pieces, attn_cat)


def weight_terms(info, pieces, attn_cat, near, after=(), base=()):
    d_out, width = pieces[0].shape[1], attn_cat.shape[1]
    block = 3 * HEAD if d_out % (3 * HEAD) == 0 else d_out
    steps, cut = d_out // block, d_out // GROUP

    def kernel(info_ref, *refs):
        inputs, attn = refs[: len(pieces)], refs[len(pieces)]
        bases = refs[len(pieces) + 1 : len(pieces) + 1 + len(base)]
        own, other, away, whole = refs[len(pieces) + 1 + len(base) + len(after) :]
        at = attn.shape[0] - sum(piece.shape[0] for piece in inputs)
        total = bases[0][...] if bases else None
        for piece in inputs:
            rows = piece.shape[0]
            term = lax.dot_general(
                piece[...],
                attn[at : at + rows],
                (((0,), (0,)), ((), ())),
                preferred_element_type=jnp.float32,
            )
            total, at = term if total is None else total + term, at + rows
        step = pl.program_id(0)
        whole[pl.ds(pl.multiple_of(step * block, block), block)] = total.astype(whole.dtype)

        @pl.when(step == steps - 1)
        def _():
            def chunk(m):
                return whole[pl.ds(pl.multiple_of((info_ref[2] ^ m) * cut, 16), cut)]

            own[...] = chunk(0)
            other[...] = chunk(3 ^ near)
            away[0] = chunk(near)
            away[1] = chunk(3)

    shapes = [(cut, width), (cut, width), (2, cut, width)]
    out = [jax.ShapeDtypeStruct(s, jnp.bfloat16) for s in shapes]
    return pl.pallas_call(
        kernel,
        grid=(steps,),
        in_specs=[SMEM]
        + [pl.BlockSpec((p.shape[0], block), lambda i: (0, i)) for p in pieces]
        + [entire(attn_cat)]
        + [pl.BlockSpec((block, width), lambda i: (i, 0))] * len(base)
        + [ANY] * len(after),
        out_specs=[entire(a) for a in out],
        out_shape=out,
        scratch_shapes=[pltpu.VMEM((d_out, width), jnp.bfloat16)],
        compiler_params=pltpu.CompilerParams(vmem_limit_bytes=32 * 1024 * 1024),
        cost_estimate=pl.CostEstimate(
            flops=2 * attn_cat.size * d_out,
            bytes_accessed=2 * (attn_cat.shape[0] + width) * d_out,
            transcendentals=0,
        ),
    )(info, *pieces, attn_cat, *base, *after)


def split_sums(info, pairs, after):
    rows, width = pairs[0][0].shape
    cut, count = rows // GROUP, len(pairs)

    def kernel(info_ref, *refs):
        outs, total = refs[-1 - GROUP : -1], refs[-1]
        for g in range(count):
            total[...] = refs[2 * g][...].astype(jnp.float32) + refs[2 * g + 1][...].astype(jnp.float32)
            for m in range(GROUP):
                start = pl.multiple_of((info_ref[0] ^ m) * cut, 8)
                block = total[pl.ds(start, cut)].astype(outs[m].dtype)
                outs[m][:, g * width : (g + 1) * width] = block

    flat = [a for pair in pairs for a in pair]
    out = [jax.ShapeDtypeStruct((cut, count * width), jnp.bfloat16)] * GROUP
    return pl.pallas_call(
        kernel,
        grid=(1,),
        in_specs=[SMEM] + [entire(a) for a in flat] + [ANY] * len(after),
        out_specs=[entire(a) for a in out],
        out_shape=out,
        scratch_shapes=[pltpu.VMEM((rows, width), jnp.float32)],
        compiler_params=pltpu.CompilerParams(vmem_limit_bytes=32 * 1024 * 1024),
    )(info, *flat, *after)


def project(info, attn, out_weight, after):
    rows, depth = attn.shape
    d_out = out_weight.shape[1]
    block = 3 * HEAD if d_out % (3 * HEAD) == 0 else d_out
    steps, half = d_out // block, d_out // 2

    def kernel(info_ref, attn_ref, weight, *refs):
        mine, theirs, whole = refs[len(after) :]
        step = pl.program_id(0)
        part = jnp.dot(attn_ref[...], weight[...], preferred_element_type=jnp.float32)
        whole[pl.ds(pl.multiple_of(step * block, block), block)] = part.T

        @pl.when(step == steps - 1)
        def _():
            tp = info_ref[1]
            mine[...] = whole[pl.ds(pl.multiple_of(tp * half, 8), half)]
            other = whole[pl.ds(pl.multiple_of((1 - tp) * half, 8), half)]
            theirs[...] = other.astype(theirs.dtype)

    out = [jax.ShapeDtypeStruct((half, rows), d) for d in (jnp.float32, jnp.bfloat16)]
    return pl.pallas_call(
        kernel,
        grid=(steps,),
        in_specs=[SMEM, entire(attn), pl.BlockSpec((depth, block), lambda i: (0, i))]
        + [ANY] * len(after),
        out_specs=[entire(a) for a in out],
        out_shape=out,
        scratch_shapes=[pltpu.VMEM((d_out, rows), jnp.float32)],
        compiler_params=pltpu.CompilerParams(vmem_limit_bytes=32 * 1024 * 1024),
        cost_estimate=pl.CostEstimate(
            flops=2 * attn.size * d_out, bytes_accessed=2 * out_weight.size, transcendentals=0
        ),
    )(info, attn, out_weight, *after)


def grouped(queries, keys, values, out_weight, out_grad, block_doc):
    f32, bf16 = jnp.float32, jnp.bfloat16
    rows = queries.shape[0]
    me, tp = lax.axis_index("ctx"), lax.axis_index("tp")
    r, layer = me % GROUP, me // GROUP
    members = range(GROUP)
    q_width, kv_width = queries.shape[1] // GROUP, keys.shape[1] // GROUP
    kv_heads = kv_width // HEAD
    head_width = q_width // kv_heads
    d_out = out_grad.shape[1]
    doc_padded = jnp.concatenate([jnp.full((GROUP,), -1, jnp.int32), block_doc])
    docs = lax.dynamic_slice_in_dim(doc_padded, layer * GROUP, 2 * GROUP, 0)
    info = jnp.concatenate([jnp.stack([r, tp, layer]).astype(jnp.int32), docs])

    def shape(*dims, dtype=bf16):
        return jax.ShapeDtypeStruct(dims, dtype)

    def traded(blocks):
        return [blocks[0]] + [swapped(blocks[m], "ctx", m) for m in members[1:]]

    kv = traded(pack_kv(keys, values))
    d_attn = project_back(info, out_grad, out_weight)

    def pack_queries(info_ref, ins, outs):
        for m in members:
            outs[m][:, :q_width] = columns(ins[0], (info_ref[0] ^ m) * q_width, q_width)
            outs[m][:, q_width:] = ins[1 + m][...]

    packed = moved(pack_queries, info, [queries, *d_attn], [shape(rows, 2 * q_width)] * GROUP)
    q_and_d = traded(packed)

    def pack_heads(info_ref, ins, outs):
        for m in members:
            for g in range(kv_heads):
                for i in range(2):
                    at = (i * kv_heads + g) * HEAD
                    outs[g][m, :, i * HEAD : (i + 1) * HEAD] = ins[m][:, at : at + HEAD]

    kv_own = moved(pack_heads, info, kv, [shape(GROUP, rows, 2 * HEAD)] * kv_heads, packed)
    kv_far = [shifted(a, "ctx", GROUP) for a in kv_own]

    def pack_half(info_ref, ins, outs):
        outs[0][...] = ins[0][pl.ds(pl.multiple_of(info_ref[1] * (rows // 2), 16), rows // 2), :]

    half = moved(pack_half, info, [out_grad], [shape(rows // 2, d_out)])[0]
    half, *_ = lax.optimization_barrier((half, *q_and_d[1:]))
    near = traded([half] * GROUP)[1:]

    def pack_near(info_ref, ins, outs):
        for i in range(GROUP - 1):
            outs[0][i * (rows // 2) : (i + 1) * (rows // 2)] = ins[i][...]

    parts, held = [], []
    for g in range(kv_heads):
        parts.append(attention(info, q_and_d, kv_own[g], kv_far[g], g, kv_heads, held))
        held = parts[-1][: 2 * GROUP]
    far_grads = [shifted(p[-1], "ctx", -GROUP) for p in parts]
    own_grads = [p[-2] for p in parts]
    attn_cats = [p[-3] for p in parts]
    attn, query_grad = traded(held[:GROUP]), traded(held[GROUP:])
    near_shape = shape((GROUP - 1) * (rows // 2), d_out)
    near = moved(pack_near, info, near, [near_shape], [*attn_cats, far_grads[0]])[0]
    pieces = [out_grad, near, swapped(near, "tp", 1)]
    steps = [2, 1]
    early = early_terms(pieces[:2], attn_cats[0])
    all_terms = [weight_terms(info, pieces[2:], attn_cats[0], steps[0], (), [early])]
    for g in range(1, kv_heads):
        all_terms.append(weight_terms(info, pieces, attn_cats[g], steps[g], [far_grads[g], all_terms[0][0]]))

    def add_pair(info_ref, ins, outs):
        for i in range(2):
            outs[i][...] = (ins[i][...].astype(f32) + ins[2][i].astype(f32)).astype(outs[i].dtype)

    def add_layers(terms, near, after):
        own, other, away = terms
        met = swapped(away, "ctx", near * GROUP)
        pair_shape = [shape(*own.shape, dtype=f32), shape(*own.shape)]
        own, other = moved(add_pair, info, [own, other, met], pair_shape, after)
        return own, other, swapped(other, "ctx", (3 ^ near) * GROUP)

    def lay_out(info_ref, ins, outs):
        for m in members:
            start = pl.multiple_of((info_ref[0] ^ m) * q_width, HEAD)
            outs[0][:, pl.ds(start, q_width)] = ins[m][...]

    attn = moved(lay_out, info, attn, [shape(rows, GROUP * q_width)], all_terms[-1][:1])[0]
    mine, theirs = project(info, attn, out_weight, [])
    sums, after = [], [theirs]
    for terms, near in zip(all_terms, steps):
        sums.append(add_layers(terms, near, after))
        after = [sums[-1][1]]

    def add_up(info_ref, ins, outs):
        for g in range(kv_heads):
            for m in members:
                for i in range(2):
                    at = (i * kv_heads + g) * HEAD
                    total = ins[g][i, m] + ins[kv_heads + g][i, m].astype(f32)
                    outs[m][:, at : at + HEAD] = total.astype(bf16)

    def lay_out_kv(info_ref, ins, outs):
        for m in members:
            start = pl.multiple_of((info_ref[0] ^ m) * kv_width, HEAD)
            for i in range(2):
                outs[i][:, pl.ds(start, kv_width)] = ins[m][:, i * kv_width : (i + 1) * kv_width]

    total_shape = [shape(rows, 2 * kv_width)] * GROUP
    totals = moved(add_up, info, own_grads + far_grads, total_shape, [*query_grad[1:], sums[0][1]])
    handed = traded(totals)
    key_grad, value_grad = moved(lay_out_kv, info, handed, [shape(rows, GROUP * kv_width)] * 2)

    query_grad = moved(lay_out, info, query_grad, [shape(rows, GROUP * q_width)], totals)[0]

    def add_shares(info_ref, ins, outs):
        outs[0][...] = (ins[0][...] + ins[1][...].astype(f32)).astype(bf16)

    theirs = swapped(theirs, "tp", 1)
    attn_output = moved(add_shares, info, [mine, theirs], [shape(d_out // 2, rows)])[0]

    def lay_out_weight(info_ref, ins, outs):
        for m in members:
            start = pl.multiple_of((info_ref[0] ^ m) * q_width, HEAD)
            outs[0][:, pl.ds(start, q_width)] = ins[m][...].astype(f32)

    blocks = traded(split_sums(info, [(own, met) for own, other, met in sums], handed[1:]))
    grad_shape = [shape(d_out // GROUP // GROUP, GROUP * q_width, dtype=f32)]
    late = []
    out_weight_grad = moved(lay_out_weight, info, blocks, grad_shape, late)[0].T
    return (attn_output.T, query_grad, key_grad, value_grad, out_weight_grad)


def single(queries, keys, values, out_weight, out_grad, block_doc):
    tok_rows = queries.shape[0]
    head_size = HEAD
    kv_count = keys.shape[1] // head_size
    group_size = queries.shape[1] // keys.shape[1]
    key_width = keys.shape[1]
    span_blocks = WINDOW // tok_rows
    reach_blocks = min(span_blocks, lax.axis_size("ctx") - 1)
    own_block = lax.axis_index("ctx")
    paired = jnp.stack([keys, values])
    by_distance = jnp.stack(
        [paired] + [shifted(paired, "ctx", distance) for distance in range(1, reach_blocks + 1)]
    )
    ordered = by_distance[::-1]
    missing = span_blocks - reach_blocks
    window_rows = (span_blocks + 1) * tok_rows
    key_window = ordered[:, 0].reshape(window_rows, kv_count, head_size)
    value_window = ordered[:, 1].reshape(window_rows, kv_count, head_size)
    doc_padded = jnp.concatenate([jnp.full((span_blocks,), -1, jnp.int32), block_doc])
    window_docs = lax.dynamic_slice_in_dim(doc_padded, own_block, span_blocks + 1, 0)
    key_docs = jnp.repeat(window_docs, tok_rows)
    own_doc = lax.dynamic_slice_in_dim(block_doc, own_block, 1, 0)
    rel_key = jnp.arange(window_rows, dtype=jnp.int32)
    rel_query = jnp.arange(tok_rows, dtype=jnp.int32) + span_blocks * tok_rows
    visible = (rel_key[None, :] <= rel_query[:, None]) & (
        rel_key[None, :] > rel_query[:, None] - WINDOW
    )
    visible = visible & (key_docs[None, :] == own_doc[0])
    query_heads = queries.reshape(tok_rows, kv_count, group_size, head_size)
    scores = (
        jnp.einsum("tkgd,skd->kgts", query_heads, key_window, preferred_element_type=jnp.float32)
        * query_scale
    )
    scores = jnp.where(visible[None, None], scores, -jnp.inf)
    top = jnp.max(scores, axis=-1, keepdims=True)
    expo = jnp.exp(scores - top)
    probs = expo / jnp.sum(expo, axis=-1, keepdims=True)
    probs_low = probs.astype(jnp.bfloat16)
    attn_heads = jnp.einsum(
        "kgts,skd->tkgd", probs_low, value_window, preferred_element_type=jnp.float32
    ).astype(jnp.bfloat16)
    attn = attn_heads.reshape(tok_rows, queries.shape[1])
    output_terms = jnp.dot(attn, out_weight, preferred_element_type=jnp.float32)
    attn_output = lax.psum_scatter(output_terms, "tp", scatter_dimension=1, tiled=True).astype(
        jnp.bfloat16
    )
    weight_terms = jnp.einsum("tr,tc->rc", attn, out_grad, preferred_element_type=jnp.float32)
    out_weight_grad = lax.psum_scatter(weight_terms, "ctx", scatter_dimension=1, tiled=True)
    d_attn = jnp.einsum(
        "te,re->tr", out_grad, out_weight, preferred_element_type=jnp.float32
    ).astype(jnp.bfloat16)
    d_attn_heads = d_attn.reshape(tok_rows, kv_count, group_size, head_size)
    d_probs = jnp.einsum(
        "tkgd,skd->kgts", d_attn_heads, value_window, preferred_element_type=jnp.float32
    )
    delta = jnp.einsum(
        "tkgd,tkgd->kgt", attn_heads, d_attn_heads, preferred_element_type=jnp.float32
    )
    d_scores = (probs * (d_probs - delta[..., None])).astype(jnp.bfloat16)
    query_grad = (
        jnp.einsum("kgts,skd->tkgd", d_scores, key_window, preferred_element_type=jnp.float32)
        * query_scale
    ).astype(jnp.bfloat16)
    query_grad = query_grad.reshape(tok_rows, queries.shape[1])
    key_part = (
        jnp.einsum("kgts,tkgd->skd", d_scores, query_heads, preferred_element_type=jnp.float32)
        * query_scale
    )
    value_part = jnp.einsum(
        "kgts,tkgd->skd", probs_low, d_attn_heads, preferred_element_type=jnp.float32
    )
    by_position = jnp.stack(
        [
            key_part.reshape(span_blocks + 1, tok_rows, key_width),
            value_part.reshape(span_blocks + 1, tok_rows, key_width),
        ],
        axis=1,
    )
    terms_near = by_position[::-1]
    total = terms_near[0] + sum(
        [shifted(terms_near[distance], "ctx", -distance) for distance in range(1, reach_blocks + 1)]
    )
    key_grad = total[0].astype(jnp.bfloat16)
    value_grad = total[1].astype(jnp.bfloat16)
    return (attn_output, query_grad, key_grad, value_grad, out_weight_grad)


def local(queries, keys, values, out_weight, out_grad, block_doc):
    fits = (
        lax.axis_size("ctx") == GROUP * GROUP
        and queries.shape[0] * GROUP == WINDOW
        and keys.shape[1] == 2 * GROUP * HEAD
        and lax.axis_size("tp") == 2
    )
    step = grouped if fits else single
    return step(queries, keys, values, out_weight, out_grad, block_doc)


def solution(mesh):
    placed = (P("ctx", "tp"), P("ctx", "tp"), P("ctx", "tp"), P("tp", None), P("ctx", None), P())
    return jax.shard_map(
        local,
        mesh=mesh,
        in_specs=placed,
        out_specs=(P("ctx", "tp"), P("ctx", "tp"), P("ctx", "tp"), P("ctx", "tp"), P("tp", "ctx")),
        check_vma=False,
    )
```

```python
import functools

import jax
import jax.numpy as jnp
from jax import lax
from jax.experimental import pallas as pl
from jax.experimental.pallas import tpu as pltpu
from jax.sharding import PartitionSpec as P

HEAD = 128
WINDOW = 1024
GROUP = 4


query_scale = 168.0 ** (-0.5)
LOG2E = 1.4426950408889634
HIDDEN = -1e30


def shifted(shard, axis, by):
    size = lax.axis_size(axis)
    pairs = [(i, i + by) for i in range(size) if 0 <= i + by < size]
    return lax.ppermute(shard, axis, pairs)


def swapped(shard, axis, by):
    return lax.ppermute(shard, axis, [(i, i ^ by) for i in range(lax.axis_size(axis))])


SMEM = pl.BlockSpec(memory_space=pltpu.SMEM)
ANY = pl.BlockSpec(memory_space=pl.ANY)


def attention_kernel(rows, held, info, *refs):
    q_refs, g_refs = refs[:GROUP], refs[GROUP : 2 * GROUP]
    k_own, v_own, k_far, v_far = refs[2 * GROUP : 2 * GROUP + 4]
    held_refs = refs[2 * GROUP + 4 : 2 * GROUP + 4 + held]
    outs = refs[2 * GROUP + 4 + held :]
    back_refs = outs[: 2 * GROUP]
    attn_cat, kv_own, kv_far = outs[2 * GROUP : 2 * GROUP + 3]
    q_all, g_all, k_all, v_all, k_tr, v_tr, k_acc, v_acc, back = outs[2 * GROUP + 3 :]
    r, tp = info[0], info[1]
    heads = q_refs[0].shape[1] // HEAD
    half = rows // 2
    for m in range(GROUP):
        q_all[m] = q_refs[m][...]
        g_all[m] = g_refs[m][...]
        spot = r ^ m
        for place, k, v in ((spot, k_far, v_far), (spot + GROUP, k_own, v_own)):
            k_all[place] = k[m]
            v_all[place] = v[m]
            k_tr[place] = k[m].T
            v_tr[place] = v[m].T
    k_acc[...] = jnp.zeros_like(k_acc)
    v_acc[...] = jnp.zeros_like(v_acc)
    key_at = lax.broadcasted_iota(jnp.int32, (rows, heads * rows), 0)
    query_at = lax.broadcasted_iota(jnp.int32, (rows, heads * rows), 1) % rows
    far_seen, own_seen = key_at > query_at, key_at <= query_at
    nt = (((1,), (1,)), ((), ()))

    def dot(a, b):
        return jnp.dot(a, b, preferred_element_type=jnp.float32)

    def block(m, carry):
        first = r ^ m
        own_doc = info[3 + first + GROUP]
        q = jnp.concatenate([q_all[m, :, h * HEAD : (h + 1) * HEAD] for h in range(heads)], axis=0)
        g = jnp.concatenate([g_all[m, :, h * HEAD : (h + 1) * HEAD] for h in range(heads)], axis=0)
        scores, hidden = [], []
        for j in range(GROUP + 1):
            s = lax.dot_general(k_all[first + j], q, nt, preferred_element_type=jnp.float32)
            if j == 0:
                s = jnp.where(far_seen, s, HIDDEN)
            if j == GROUP:
                s = jnp.where(own_seen, s, HIDDEN)
            scores.append(s)
            hidden.append(jnp.where(info[3 + first + j] == own_doc, 0.0, HIDDEN))
        tops = [jnp.max(s, axis=0, keepdims=True) + b for s, b in zip(scores, hidden)]
        top = functools.reduce(jnp.maximum, tops) * (query_scale * LOG2E)
        expo = [
            jnp.exp2(s * (query_scale * LOG2E) - (top - b)) for s, b in zip(scores, hidden)
        ]
        whole = functools.reduce(jnp.add, [jnp.sum(e, axis=0, keepdims=True) for e in expo])
        inverse = 1.0 / whole
        probs = [e * inverse for e in expo]
        low = [p.astype(jnp.bfloat16) for p in probs]
        attn_tr = functools.reduce(jnp.add, [dot(v_tr[first + j], low[j]) for j in range(GROUP + 1)])
        attn_tr = attn_tr.astype(jnp.bfloat16).astype(jnp.float32)
        delta = jnp.sum(attn_tr * g.astype(jnp.float32).T, axis=0, keepdims=True)
        dq_tr, d_scores = None, []
        for j in range(GROUP + 1):
            d_p = lax.dot_general(v_all[first + j], g, nt, preferred_element_type=jnp.float32)
            d_s = (probs[j] * (d_p - delta)).astype(jnp.bfloat16)
            term = dot(k_tr[first + j], d_s)
            dq_tr = term if dq_tr is None else dq_tr + term
            d_scores.append(d_s)
        for j in range(GROUP + 1):
            k_acc[first + j] += dot(d_scores[j], q)
            v_acc[first + j] += dot(low[j], g)
        attn = attn_tr.T.astype(jnp.bfloat16)
        dq = (dq_tr * query_scale).T.astype(jnp.bfloat16)
        for h in range(heads):
            back[m, 0, :, h * HEAD : (h + 1) * HEAD] = attn[h * rows : (h + 1) * rows]
            back[m, 1, :, h * HEAD : (h + 1) * HEAD] = dq[h * rows : (h + 1) * rows]
        return carry

    for m in range(GROUP):
        block(m, 0)
    for m in range(GROUP):
        width = back.shape[3]
        for i in range(2):
            out = back_refs[i * GROUP + m]
            at = out.shape[1] - width
            out[:, at:] = back[m, i]
            if held:
                out[:, :at] = held_refs[i * GROUP + m][...]
        spot = r ^ m
        kv_far[0, m] = (k_acc[spot] * query_scale).astype(kv_far.dtype)
        kv_far[1, m] = v_acc[spot].astype(kv_far.dtype)
        kv_own[0, m] = k_acc[spot + GROUP] * query_scale
        kv_own[1, m] = v_acc[spot + GROUP]
    attn_cat[0:rows] = back[0, 0]
    near = pl.multiple_of(tp * half, half)
    away = pl.multiple_of((1 - tp) * half, half)
    for m in range(1, GROUP):
        at = rows + (m - 1) * half
        attn_cat[at : at + half] = back[m, 0, pl.ds(near, half), :]
        at += (GROUP - 1) * half
        attn_cat[at : at + half] = back[m, 0, pl.ds(away, half), :]


def entire(array):
    return pl.BlockSpec(array.shape, lambda i: (0,) * len(array.shape))


def attention(info, q_and_d, kv_own, kv_far, g, kv_heads, held):
    rows, q_block = q_and_d[0].shape[0], q_and_d[0].shape[1] // 2 // kv_heads
    q_spec = pl.BlockSpec((rows, q_block), lambda i: (0, g))
    g_spec = pl.BlockSpec((rows, q_block), lambda i: (0, g + kv_heads))
    k_spec = pl.BlockSpec((GROUP, rows, HEAD), lambda i: (0, 0, 0))
    v_spec = pl.BlockSpec((GROUP, rows, HEAD), lambda i: (0, 0, 1))
    kv_shape = (2, GROUP, rows, HEAD)
    bf16 = jnp.bfloat16
    blocks = 2 * GROUP
    out = [jax.ShapeDtypeStruct((rows, (g + 1) * q_block), bf16)] * (2 * GROUP) + [
        jax.ShapeDtypeStruct((GROUP * rows, q_block), bf16),
        jax.ShapeDtypeStruct(kv_shape, jnp.float32),
        jax.ShapeDtypeStruct(kv_shape, bf16),
    ]
    return pl.pallas_call(
        functools.partial(attention_kernel, rows, len(held)),
        grid=(1,),
        in_specs=[SMEM]
        + [q_spec] * GROUP
        + [g_spec] * GROUP
        + [k_spec, v_spec, k_spec, v_spec]
        + [entire(a) for a in held],
        out_specs=[entire(a) for a in out],
        out_shape=out,
        scratch_shapes=[
            pltpu.VMEM((GROUP, rows, q_block), bf16),
            pltpu.VMEM((GROUP, rows, q_block), bf16),
            pltpu.VMEM((blocks, rows, HEAD), bf16),
            pltpu.VMEM((blocks, rows, HEAD), bf16),
            pltpu.VMEM((blocks, HEAD, rows), bf16),
            pltpu.VMEM((blocks, HEAD, rows), bf16),
            pltpu.VMEM((blocks, rows, HEAD), jnp.float32),
            pltpu.VMEM((blocks, rows, HEAD), jnp.float32),
            pltpu.VMEM((GROUP, 2, rows, q_block), bf16),
        ],
        compiler_params=pltpu.CompilerParams(vmem_limit_bytes=32 * 1024 * 1024),
        cost_estimate=pl.CostEstimate(
            flops=12 * q_block * GROUP * rows * (GROUP + 1) * rows,
            bytes_accessed=5 * 1024 * 1024,
            transcendentals=0,
        ),
    )(info, *q_and_d, *q_and_d, kv_own, kv_own, kv_far, kv_far, *held)


def moved(body, info, arrays, out, after=()):
    n = len(arrays)

    def kernel(info_ref, *refs):
        body(info_ref, refs[:n], refs[n + len(after) :])

    size = sum(a.size * a.dtype.itemsize for a in list(arrays) + list(out))
    return pl.pallas_call(
        kernel,
        grid=(1,),
        in_specs=[SMEM] + [entire(a) for a in arrays] + [ANY] * len(after),
        out_specs=[entire(a) for a in out],
        out_shape=list(out),
        compiler_params=pltpu.CompilerParams(vmem_limit_bytes=32 * 1024 * 1024),
        cost_estimate=pl.CostEstimate(flops=0, bytes_accessed=size, transcendentals=0),
    )(info, *arrays, *after)


def columns(ref, start, width):
    return ref[:, pl.ds(pl.multiple_of(start, HEAD), width)]


def pack_kv(keys, values):
    rows, width = keys.shape[0], keys.shape[1] // GROUP

    def kernel(k_ref, v_ref, *refs):
        outs, sems = refs[:GROUP], refs[GROUP]
        r = lax.axis_index("ctx") % GROUP
        copies = []
        for m in range(GROUP):
            for i, ref in enumerate((k_ref, v_ref)):
                start = pl.multiple_of((r ^ m) * width, HEAD)
                copies.append(
                    pltpu.make_async_copy(
                        ref.at[:, pl.ds(start, width)],
                        outs[m].at[:, i * width : (i + 1) * width],
                        sems.at[2 * m + i],
                    )
                )
        for copy in copies:
            copy.start()
        for copy in copies:
            copy.wait()

    out = [jax.ShapeDtypeStruct((rows, 2 * width), keys.dtype)] * GROUP
    return pl.pallas_call(
        kernel,
        in_specs=[ANY, ANY],
        out_specs=[pl.BlockSpec(memory_space=pltpu.VMEM)] * GROUP,
        out_shape=out,
        scratch_shapes=[pltpu.SemaphoreType.DMA((2 * GROUP,))],
        compiler_params=pltpu.CompilerParams(vmem_limit_bytes=32 * 1024 * 1024),
        cost_estimate=pl.CostEstimate(
            flops=0, bytes_accessed=4 * keys.size, transcendentals=0
        ),
    )(keys, values)


def project_back(info, out_grad, out_weight):
    rows, d_out = out_grad.shape
    steps = GROUP
    block = out_weight.shape[0] // steps

    def kernel(info_ref, grad, weight, *outs):
        step = pl.program_id(0)
        part = lax.dot_general(
            grad[...], weight[...], (((1,), (1,)), ((), ())), preferred_element_type=jnp.float32
        ).astype(jnp.bfloat16)
        for at in range(steps):

            @pl.when(step == at)
            def _():
                outs[at][...] = part

    def weight_block(step, info_ref):
        return (info_ref[0] ^ step, 0)

    return pl.pallas_call(
        kernel,
        grid_spec=pltpu.PrefetchScalarGridSpec(
            num_scalar_prefetch=1,
            grid=(steps,),
            in_specs=[
                pl.BlockSpec((rows, d_out), lambda i, info_ref: (0, 0)),
                pl.BlockSpec((block, d_out), weight_block),
            ],
            out_specs=[pl.BlockSpec((rows, block), lambda i, info_ref: (0, 0))] * steps,
        ),
        out_shape=[jax.ShapeDtypeStruct((rows, block), jnp.bfloat16)] * steps,
        compiler_params=pltpu.CompilerParams(vmem_limit_bytes=32 * 1024 * 1024),
        cost_estimate=pl.CostEstimate(
            flops=2 * rows * out_weight.size, bytes_accessed=2 * out_weight.size, transcendentals=0
        ),
    )(info, out_grad, out_weight)

def weight_terms(info, pieces, attn_cat, near, after=()):
    d_out, width = pieces[0].shape[1], attn_cat.shape[1]
    block = 3 * HEAD if d_out % (3 * HEAD) == 0 else d_out
    steps, cut = d_out // block, d_out // GROUP

    def kernel(info_ref, *refs):
        inputs, attn = refs[: len(pieces)], refs[len(pieces)]
        own, other, away, whole = refs[len(pieces) + 1 + len(after) :]
        total, at = None, 0
        for piece in inputs:
            rows = piece.shape[0]
            term = lax.dot_general(
                piece[...],
                attn[at : at + rows],
                (((0,), (0,)), ((), ())),
                preferred_element_type=jnp.float32,
            )
            total, at = term if total is None else total + term, at + rows
        step = pl.program_id(0)
        whole[pl.ds(pl.multiple_of(step * block, block), block)] = total.astype(whole.dtype)

        @pl.when(step == steps - 1)
        def _():
            def chunk(m):
                return whole[pl.ds(pl.multiple_of((info_ref[2] ^ m) * cut, 16), cut)]

            own[...] = chunk(0)
            other[...] = chunk(3 ^ near)
            away[0] = chunk(near)
            away[1] = chunk(3)

    shapes = [(cut, width), (cut, width), (2, cut, width)]
    out = [jax.ShapeDtypeStruct(s, jnp.bfloat16) for s in shapes]
    return pl.pallas_call(
        kernel,
        grid=(steps,),
        in_specs=[SMEM]
        + [pl.BlockSpec((p.shape[0], block), lambda i: (0, i)) for p in pieces]
        + [entire(attn_cat)]
        + [ANY] * len(after),
        out_specs=[entire(a) for a in out],
        out_shape=out,
        scratch_shapes=[pltpu.VMEM((d_out, width), jnp.bfloat16)],
        compiler_params=pltpu.CompilerParams(vmem_limit_bytes=32 * 1024 * 1024),
        cost_estimate=pl.CostEstimate(
            flops=2 * attn_cat.size * d_out,
            bytes_accessed=2 * (attn_cat.shape[0] + width) * d_out,
            transcendentals=0,
        ),
    )(info, *pieces, attn_cat, *after)


def split_sums(info, pairs, after):
    rows, width = pairs[0][0].shape
    cut, count = rows // GROUP, len(pairs)

    def kernel(info_ref, *refs):
        outs, total = refs[-1 - GROUP : -1], refs[-1]
        for g in range(count):
            total[...] = refs[2 * g][...].astype(jnp.float32) + refs[2 * g + 1][...].astype(jnp.float32)
            for m in range(GROUP):
                start = pl.multiple_of((info_ref[0] ^ m) * cut, 8)
                block = total[pl.ds(start, cut)].astype(outs[m].dtype)
                outs[m][:, g * width : (g + 1) * width] = block

    flat = [a for pair in pairs for a in pair]
    out = [jax.ShapeDtypeStruct((cut, count * width), jnp.bfloat16)] * GROUP
    return pl.pallas_call(
        kernel,
        grid=(1,),
        in_specs=[SMEM] + [entire(a) for a in flat] + [ANY] * len(after),
        out_specs=[entire(a) for a in out],
        out_shape=out,
        scratch_shapes=[pltpu.VMEM((rows, width), jnp.float32)],
        compiler_params=pltpu.CompilerParams(vmem_limit_bytes=32 * 1024 * 1024),
    )(info, *flat, *after)


def project(info, attn, out_weight, after):
    rows, depth = attn.shape
    d_out = out_weight.shape[1]
    block = 3 * HEAD if d_out % (3 * HEAD) == 0 else d_out
    steps, half = d_out // block, d_out // 2

    def kernel(info_ref, attn_ref, weight, *refs):
        mine, theirs, whole = refs[len(after) :]
        step = pl.program_id(0)
        part = jnp.dot(attn_ref[...], weight[...], preferred_element_type=jnp.float32)
        whole[pl.ds(pl.multiple_of(step * block, block), block)] = part.T

        @pl.when(step == steps - 1)
        def _():
            tp = info_ref[1]
            mine[...] = whole[pl.ds(pl.multiple_of(tp * half, 8), half)]
            other = whole[pl.ds(pl.multiple_of((1 - tp) * half, 8), half)]
            theirs[...] = other.astype(theirs.dtype)

    out = [jax.ShapeDtypeStruct((half, rows), d) for d in (jnp.float32, jnp.bfloat16)]
    return pl.pallas_call(
        kernel,
        grid=(steps,),
        in_specs=[SMEM, entire(attn), pl.BlockSpec((depth, block), lambda i: (0, i))]
        + [ANY] * len(after),
        out_specs=[entire(a) for a in out],
        out_shape=out,
        scratch_shapes=[pltpu.VMEM((d_out, rows), jnp.float32)],
        compiler_params=pltpu.CompilerParams(vmem_limit_bytes=32 * 1024 * 1024),
        cost_estimate=pl.CostEstimate(
            flops=2 * attn.size * d_out, bytes_accessed=2 * out_weight.size, transcendentals=0
        ),
    )(info, attn, out_weight, *after)


def grouped(queries, keys, values, out_weight, out_grad, block_doc):
    f32, bf16 = jnp.float32, jnp.bfloat16
    rows = queries.shape[0]
    me, tp = lax.axis_index("ctx"), lax.axis_index("tp")
    r, layer = me % GROUP, me // GROUP
    members = range(GROUP)
    q_width, kv_width = queries.shape[1] // GROUP, keys.shape[1] // GROUP
    kv_heads = kv_width // HEAD
    head_width = q_width // kv_heads
    d_out = out_grad.shape[1]
    doc_padded = jnp.concatenate([jnp.full((GROUP,), -1, jnp.int32), block_doc])
    docs = lax.dynamic_slice_in_dim(doc_padded, layer * GROUP, 2 * GROUP, 0)
    info = jnp.concatenate([jnp.stack([r, tp, layer]).astype(jnp.int32), docs])

    def shape(*dims, dtype=bf16):
        return jax.ShapeDtypeStruct(dims, dtype)

    def traded(blocks):
        return [blocks[0]] + [swapped(blocks[m], "ctx", m) for m in members[1:]]

    kv = traded(pack_kv(keys, values))
    d_attn = project_back(info, out_grad, out_weight)

    def pack_queries(info_ref, ins, outs):
        for m in members:
            outs[m][:, :q_width] = columns(ins[0], (info_ref[0] ^ m) * q_width, q_width)
            outs[m][:, q_width:] = ins[1 + m][...]

    packed = moved(pack_queries, info, [queries, *d_attn], [shape(rows, 2 * q_width)] * GROUP)
    q_and_d = traded(packed)

    def pack_heads(info_ref, ins, outs):
        for m in members:
            for g in range(kv_heads):
                for i in range(2):
                    at = (i * kv_heads + g) * HEAD
                    outs[g][m, :, i * HEAD : (i + 1) * HEAD] = ins[m][:, at : at + HEAD]

    kv_own = moved(pack_heads, info, kv, [shape(GROUP, rows, 2 * HEAD)] * kv_heads, packed)
    kv_far = [shifted(a, "ctx", GROUP) for a in kv_own]

    def pack_half(info_ref, ins, outs):
        outs[0][...] = ins[0][pl.ds(pl.multiple_of(info_ref[1] * (rows // 2), 16), rows // 2), :]

    half = moved(pack_half, info, [out_grad], [shape(rows // 2, d_out)])[0]
    half, *_ = lax.optimization_barrier((half, *q_and_d[1:]))
    near = traded([half] * GROUP)[1:]

    def pack_near(info_ref, ins, outs):
        for i in range(GROUP - 1):
            outs[0][i * (rows // 2) : (i + 1) * (rows // 2)] = ins[i][...]

    parts, held = [], []
    for g in range(kv_heads):
        parts.append(attention(info, q_and_d, kv_own[g], kv_far[g], g, kv_heads, held))
        held = parts[-1][: 2 * GROUP]
    far_grads = [shifted(p[-1], "ctx", -GROUP) for p in parts]
    own_grads = [p[-2] for p in parts]
    attn_cats = [p[-3] for p in parts]
    attn, query_grad = traded(held[:GROUP]), traded(held[GROUP:])
    near_shape = shape((GROUP - 1) * (rows // 2), d_out)
    near = moved(pack_near, info, near, [near_shape], [*attn_cats, far_grads[0]])[0]
    pieces = [out_grad, near, swapped(near, "tp", 1)]
    steps = [1, 2]
    all_terms = [weight_terms(info, pieces, attn_cats[0], steps[0])]
    for g in range(1, kv_heads):
        all_terms.append(weight_terms(info, pieces, attn_cats[g], steps[g], [far_grads[g], all_terms[0][0]]))

    def add_pair(info_ref, ins, outs):
        for i in range(2):
            outs[i][...] = (ins[i][...].astype(f32) + ins[2][i].astype(f32)).astype(outs[i].dtype)

    def add_layers(terms, near, after):
        own, other, away = terms
        met = swapped(away, "ctx", near * GROUP)
        pair_shape = [shape(*own.shape, dtype=f32), shape(*own.shape)]
        own, other = moved(add_pair, info, [own, other, met], pair_shape, after)
        return own, other, swapped(other, "ctx", (3 ^ near) * GROUP)

    def lay_out(info_ref, ins, outs):
        for m in members:
            start = pl.multiple_of((info_ref[0] ^ m) * q_width, HEAD)
            outs[0][:, pl.ds(start, q_width)] = ins[m][...]

    attn = moved(lay_out, info, attn, [shape(rows, GROUP * q_width)], all_terms[-1][:1])[0]
    mine, theirs = project(info, attn, out_weight, [])
    sums, after = [], [theirs]
    for terms, near in zip(all_terms, steps):
        sums.append(add_layers(terms, near, after))
        after = [sums[-1][1]]

    def add_up(info_ref, ins, outs):
        for g in range(kv_heads):
            for m in members:
                for i in range(2):
                    at = (i * kv_heads + g) * HEAD
                    total = ins[g][i, m] + ins[kv_heads + g][i, m].astype(f32)
                    outs[m][:, at : at + HEAD] = total.astype(bf16)

    def lay_out_kv(info_ref, ins, outs):
        for m in members:
            start = pl.multiple_of((info_ref[0] ^ m) * kv_width, HEAD)
            for i in range(2):
                outs[i][:, pl.ds(start, kv_width)] = ins[m][:, i * kv_width : (i + 1) * kv_width]

    total_shape = [shape(rows, 2 * kv_width)] * GROUP
    totals = moved(add_up, info, own_grads + far_grads, total_shape, [*query_grad[1:], sums[0][1]])
    handed = traded(totals)
    key_grad, value_grad = moved(lay_out_kv, info, handed, [shape(rows, GROUP * kv_width)] * 2)

    query_grad = moved(lay_out, info, query_grad, [shape(rows, GROUP * q_width)], totals)[0]

    def add_shares(info_ref, ins, outs):
        outs[0][...] = (ins[0][...] + ins[1][...].astype(f32)).astype(bf16)

    theirs = swapped(theirs, "tp", 1)
    attn_output = moved(add_shares, info, [mine, theirs], [shape(d_out // 2, rows)])[0]

    def lay_out_weight(info_ref, ins, outs):
        for m in members:
            start = pl.multiple_of((info_ref[0] ^ m) * q_width, HEAD)
            outs[0][:, pl.ds(start, q_width)] = ins[m][...].astype(f32)

    blocks = traded(split_sums(info, [(own, met) for own, other, met in sums], handed[1:]))
    grad_shape = [shape(d_out // GROUP // GROUP, GROUP * q_width, dtype=f32)]
    late = []
    out_weight_grad = moved(lay_out_weight, info, blocks, grad_shape, late)[0].T
    return (attn_output.T, query_grad, key_grad, value_grad, out_weight_grad)


def single(queries, keys, values, out_weight, out_grad, block_doc):
    tok_rows = queries.shape[0]
    head_size = HEAD
    kv_count = keys.shape[1] // head_size
    group_size = queries.shape[1] // keys.shape[1]
    key_width = keys.shape[1]
    span_blocks = WINDOW // tok_rows
    reach_blocks = min(span_blocks, lax.axis_size("ctx") - 1)
    own_block = lax.axis_index("ctx")
    paired = jnp.stack([keys, values])
    by_distance = jnp.stack(
        [paired] + [shifted(paired, "ctx", distance) for distance in range(1, reach_blocks + 1)]
    )
    ordered = by_distance[::-1]
    missing = span_blocks - reach_blocks
    window_rows = (span_blocks + 1) * tok_rows
    key_window = ordered[:, 0].reshape(window_rows, kv_count, head_size)
    value_window = ordered[:, 1].reshape(window_rows, kv_count, head_size)
    doc_padded = jnp.concatenate([jnp.full((span_blocks,), -1, jnp.int32), block_doc])
    window_docs = lax.dynamic_slice_in_dim(doc_padded, own_block, span_blocks + 1, 0)
    key_docs = jnp.repeat(window_docs, tok_rows)
    own_doc = lax.dynamic_slice_in_dim(block_doc, own_block, 1, 0)
    rel_key = jnp.arange(window_rows, dtype=jnp.int32)
    rel_query = jnp.arange(tok_rows, dtype=jnp.int32) + span_blocks * tok_rows
    visible = (rel_key[None, :] <= rel_query[:, None]) & (
        rel_key[None, :] > rel_query[:, None] - WINDOW
    )
    visible = visible & (key_docs[None, :] == own_doc[0])
    query_heads = queries.reshape(tok_rows, kv_count, group_size, head_size)
    scores = (
        jnp.einsum("tkgd,skd->kgts", query_heads, key_window, preferred_element_type=jnp.float32)
        * query_scale
    )
    scores = jnp.where(visible[None, None], scores, -jnp.inf)
    top = jnp.max(scores, axis=-1, keepdims=True)
    expo = jnp.exp(scores - top)
    probs = expo / jnp.sum(expo, axis=-1, keepdims=True)
    probs_low = probs.astype(jnp.bfloat16)
    attn_heads = jnp.einsum(
        "kgts,skd->tkgd", probs_low, value_window, preferred_element_type=jnp.float32
    ).astype(jnp.bfloat16)
    attn = attn_heads.reshape(tok_rows, queries.shape[1])
    output_terms = jnp.dot(attn, out_weight, preferred_element_type=jnp.float32)
    attn_output = lax.psum_scatter(output_terms, "tp", scatter_dimension=1, tiled=True).astype(
        jnp.bfloat16
    )
    weight_terms = jnp.einsum("tr,tc->rc", attn, out_grad, preferred_element_type=jnp.float32)
    out_weight_grad = lax.psum_scatter(weight_terms, "ctx", scatter_dimension=1, tiled=True)
    d_attn = jnp.einsum(
        "te,re->tr", out_grad, out_weight, preferred_element_type=jnp.float32
    ).astype(jnp.bfloat16)
    d_attn_heads = d_attn.reshape(tok_rows, kv_count, group_size, head_size)
    d_probs = jnp.einsum(
        "tkgd,skd->kgts", d_attn_heads, value_window, preferred_element_type=jnp.float32
    )
    delta = jnp.einsum(
        "tkgd,tkgd->kgt", attn_heads, d_attn_heads, preferred_element_type=jnp.float32
    )
    d_scores = (probs * (d_probs - delta[..., None])).astype(jnp.bfloat16)
    query_grad = (
        jnp.einsum("kgts,skd->tkgd", d_scores, key_window, preferred_element_type=jnp.float32)
        * query_scale
    ).astype(jnp.bfloat16)
    query_grad = query_grad.reshape(tok_rows, queries.shape[1])
    key_part = (
        jnp.einsum("kgts,tkgd->skd", d_scores, query_heads, preferred_element_type=jnp.float32)
        * query_scale
    )
    value_part = jnp.einsum(
        "kgts,tkgd->skd", probs_low, d_attn_heads, preferred_element_type=jnp.float32
    )
    by_position = jnp.stack(
        [
            key_part.reshape(span_blocks + 1, tok_rows, key_width),
            value_part.reshape(span_blocks + 1, tok_rows, key_width),
        ],
        axis=1,
    )
    terms_near = by_position[::-1]
    total = terms_near[0] + sum(
        [shifted(terms_near[distance], "ctx", -distance) for distance in range(1, reach_blocks + 1)]
    )
    key_grad = total[0].astype(jnp.bfloat16)
    value_grad = total[1].astype(jnp.bfloat16)
    return (attn_output, query_grad, key_grad, value_grad, out_weight_grad)


def local(queries, keys, values, out_weight, out_grad, block_doc):
    fits = (
        lax.axis_size("ctx") == GROUP * GROUP
        and queries.shape[0] * GROUP == WINDOW
        and keys.shape[1] == 2 * GROUP * HEAD
        and lax.axis_size("tp") == 2
    )
    step = grouped if fits else single
    return step(queries, keys, values, out_weight, out_grad, block_doc)


def solution(mesh):
    placed = (P("ctx", "tp"), P("ctx", "tp"), P("ctx", "tp"), P("tp", None), P("ctx", None), P())
    return jax.shard_map(
        local,
        mesh=mesh,
        in_specs=placed,
        out_specs=(P("ctx", "tp"), P("ctx", "tp"), P("ctx", "tp"), P("ctx", "tp"), P("tp", "ctx")),
        check_vma=False,
    )
```
